256 devices in a mesh: dp: 2 (over core), seq: 16 (over x_hi, z), chan: 8 (over y, x_lo).
Axes of the slice: x: 4 (x_hi: 2, x_lo: 2; x = x_hi * 2 + x_lo), y: 4, z: 8, core: 2. Of those that a mesh axis runs over, the one named last changes fastest.
Arguments:
- recurrence_feed: bfloat16 [8192, 8192], P(('dp', 'seq'), 'chan'), parts along dimension 0, may hold values from -6 to 6
- memory_write_matrix: bfloat16 [8192, 128], P(('dp', 'seq')), parts along dimension 0, may hold values from -0.5 to 0.5
- memory_read_matrix: bfloat16 [8192, 128], P(('dp', 'seq')), parts along dimension 0, may hold values from -0.5 to 0.5
- log_shrink_table: float32 [8192, 128], P(('dp', 'seq'), 'chan'), parts along dimension 0, may hold values from -0.5 to 0
- skip_connection_scale: float32 [128], P('chan'), may hold values from 0.5 to 2
- specialist_choices: int32 [8192, 2], P(('dp', 'seq')), parts along dimension 0, may hold values from 0 to 15, as said below
- specialist_mixing_shares: bfloat16 [8192, 2], P(('dp', 'seq')), parts along dimension 0, may hold values from 0.19921875 to 1
- specialist_rescale_vector: float32 [8192], P('chan'), may hold values from 0.25 to 1.75
- specialist_switch_matrix: bfloat16 [8192, 12288], P('chan', 'seq'), may hold values from -0.0625 to 0.0625
- specialist_widen_matrix: bfloat16 [8192, 12288], P('chan', 'seq'), may hold values from -0.0625 to 0.0625
- specialist_contract_matrix: bfloat16 [12288, 8192], P('seq', 'chan'), may hold values from -0.0546875 to 0.0546875
- closing_rescale_vector: float32 [8192], replicated, may hold values from 0.5 to 1.5
- lexicon_matrix: bfloat16 [8192, 32768], P(None, ('seq', 'chan')), may hold values from -19.887378 to 19.887378
- softness_divisor: float32 [1], replicated, may hold values from 0.5 to 1
- picked_entry_offsets: int32 [512], P(('dp', 'seq')), parts along dimension 0, may hold values from 0 to 255
Outputs:
- layer_out: bfloat16 [8192, 8192], P(('dp', 'seq'), 'chan'), parts along dimension 0
- log_probs: float32 [512, 32768], P('dp', ('seq', 'chan')), parts along dimension 0
The draws below stay inside these ranges and needn't reach their ends.
There are 2 independent parts, one for each index of `dp`. The reference program is written for one: setup_inputs(seed, part) draws one part's arguments, and reference() takes and returns one part's arrays. A program takes and returns all parts, laid end to end along the dimension named above; an argument that names none is the same for every part. Nothing has to cross between parts.
Inputs may be any that keep to these rules, and one draw needn't show every extreme that they name: `specialist_choices`: the two experts of a row differ. In each aligned block of 256 rows, expert 0 is named by at most 64 rows, and by exactly 64 rows in some block.
All inputs are finite; a program needn't handle non-finite values.
Results may differ from the reference program's by a relative error of at most 0.01.
Values may be sent and summed in bfloat16 or wider, within the bound.
A program may use at most 64 MiB of HBM per device.

```python
import math
import jax
import jax.numpy as jnp
from jax import lax

HD = 64
DS = 128
GROUP = 256
EXPERTS = 16
SEQ_DEV = 256
S_SEQ = 16
RECURRENCE_UNITS = 128
D = 8192
HID = 12288
CONTEXT_LENGTH = 4096
CAP = 64
V = 32768
ROWS = 256


def decay_setup(key):
    key_slow = jax.random.fold_in(key, 101)
    key_rate = jax.random.fold_in(key, 102)
    key_fast = jax.random.fold_in(key, 103)
    key_rough = jax.random.fold_in(key, 104)
    key_spots = jax.random.fold_in(key, 105)
    objective_seed_handle = jax.random.fold_in(key, 106)
    slow_share = 0.5
    slow_heads = jax.random.uniform(key_slow, (RECURRENCE_UNITS,), jnp.float32) < slow_share
    slow_rate = jax.random.uniform(key_rate, (RECURRENCE_UNITS,), jnp.float32, 0.1, 0.7) / CONTEXT_LENGTH
    fast_rate = 1.0 / jax.random.uniform(key_fast, (RECURRENCE_UNITS,), jnp.float32, 30.0, 50.0)
    channel_shrink_speed = jnp.where(slow_heads, slow_rate, fast_rate)
    jaggedness_degree = jnp.exp(jax.random.uniform(key_rough, (CONTEXT_LENGTH, RECURRENCE_UNITS), jnp.float32, -0.69, 0.69))
    outlier_locations = jax.random.randint(key_spots, (4,), 0, CONTEXT_LENGTH)
    outlier_count = jnp.any(jnp.arange(CONTEXT_LENGTH)[:, None] == outlier_locations[None, :], axis=1)
    outlier_charge = jax.random.uniform(objective_seed_handle, (RECURRENCE_UNITS,), jnp.float32, 0.2, 0.3)
    shrink_multipliers = -channel_shrink_speed[None, :] * jaggedness_degree + jnp.where(outlier_count[:, None], jnp.log(1.0 - outlier_charge)[None, :], 0.0)
    head_scale = jnp.minimum(1.0, jnp.sqrt(64.0 * channel_shrink_speed))
    return (shrink_multipliers, head_scale)


def draw_log_shrink_table(key, part):
    shrink_multipliers, head_scale = decay_setup(key)
    return shrink_multipliers.astype(jnp.float32)


def draw_recurrence_feed(key, part):
    shrink_multipliers, head_scale = decay_setup(key)
    key_values = jax.random.fold_in(key, 201)
    base = jnp.clip(jax.random.normal(key_values, (CONTEXT_LENGTH, RECURRENCE_UNITS, HD), jnp.float32), -6.0, 6.0)
    return (base * head_scale[None, :, None]).reshape(CONTEXT_LENGTH, RECURRENCE_UNITS * HD).astype(jnp.bfloat16)


def draw_lexicon_matrix(key, part):
    key_base = jax.random.fold_in(key, 301)
    base = jnp.clip(jax.random.normal(key_base, (D, V), jnp.float32), -6.0, 6.0) * (3.0 / math.sqrt(D))
    return base.astype(jnp.bfloat16)


def draw_specialist_choices(key, part):
    block_total = CONTEXT_LENGTH // SEQ_DEV
    first_draw = jax.random.randint(jax.random.fold_in(key, 401), (block_total,), 0, CAP + 1)
    second_draw = jax.random.randint(jax.random.fold_in(key, 402), (block_total,), 0, CAP + 1)
    counts = 1 + first_draw * second_draw // (CAP + 1)
    full_block = jax.random.randint(jax.random.fold_in(key, 403), (), 0, block_total)
    counts = jnp.where(jnp.arange(block_total) == full_block, CAP, counts)
    scores = jax.random.randint(jax.random.fold_in(key, 404), (block_total, SEQ_DEV), 0, 1 << 20)
    scores = scores * SEQ_DEV + jnp.arange(SEQ_DEV, dtype=jnp.int32)[None, :]
    ranking = jnp.argsort(jnp.argsort(scores, axis=1, stable=True), axis=1, stable=True)
    chosen = ranking < counts[:, None]
    side = jax.random.randint(jax.random.fold_in(key, 405), (block_total, SEQ_DEV), 0, 2)
    first_expert = jax.random.randint(jax.random.fold_in(key, 406), (block_total, SEQ_DEV), 1, EXPERTS)
    offset = jax.random.randint(jax.random.fold_in(key, 407), (block_total, SEQ_DEV), 1, EXPERTS - 1)
    second_expert = 1 + (first_expert - 1 + offset) % (EXPERTS - 1)
    column_zero = jnp.where(chosen & (side == 0), 0, first_expert)
    column_one = jnp.where(chosen & (side == 1), 0, second_expert)
    return jnp.stack([column_zero, column_one], axis=-1).reshape(CONTEXT_LENGTH, 2).astype(jnp.int32)


def place_ends(values, stream_key, least, high):
    longest = values.shape.index(max(values.shape))
    spots = []
    for shift in (0, 1):
        where = [jax.random.randint(jax.random.fold_in(stream_key, axis), (), 0, length) for axis, length in enumerate(values.shape)]
        where[longest] = (where[longest] + shift) % values.shape[longest]
        spots.append(tuple(where))
    return values.at[spots[0]].set(least).at[spots[1]].set(high)


def steps_of(rng, shape, split, least, high):
    def one(dim, shards_of):
        draws = jax.random.uniform(jax.random.fold_in(jax.random.fold_in(rng, 6), dim), (shards_of,), jnp.float32, least / len(split), high / len(split))
        return jnp.repeat(jnp.exp(draws), shape[dim] // shards_of).reshape((-1,) + (1,) * (len(shape) - dim - 1))

    loudness = one(*split[0])
    for cut in split[1:]:
        loudness = loudness * one(*cut)
    return loudness


def scatter_about(rng, dims, deviation, reach, cuts=(), held_as=jnp.bfloat16):
    entries = jax.random.normal(rng, dims, jnp.float32) * deviation
    if len(cuts) > 0:
        entries = steps_of(rng, dims, cuts, -0.22, 0.18) * entries
    return jnp.clip(entries, min=-reach, max=reach).astype(held_as)


def setup_inputs(seed: int = 0, part: int = 0) -> dict:
    key_of = jax.random.split(jax.random.key(seed), 16)
    part_splits = jax.random.split(jax.random.fold_in(key_of[15], part), 16)
    recurrence_feed = draw_recurrence_feed(jax.random.fold_in(jax.random.fold_in(key_of[15], part), 71), part)
    memory_write_matrix = scatter_about(part_splits[1], (CONTEXT_LENGTH, DS), DS ** -0.5, 0.5, ((0, 16),))
    memory_read_matrix = scatter_about(part_splits[2], (CONTEXT_LENGTH, DS), DS ** -0.5, 0.5, ((0, 16),))
    log_shrink_table = draw_log_shrink_table(jax.random.fold_in(jax.random.fold_in(key_of[15], part), 71), part)
    skip_connection_scale = jnp.clip(jnp.exp(math.log(2.0) - 1.3862944 * jax.random.uniform(key_of[4], (RECURRENCE_UNITS,), jnp.float32) ** steps_of(key_of[4], (RECURRENCE_UNITS,), ((0, 8),), -0.2, 0.2)), 0.5, 2.0)
    specialist_choices = draw_specialist_choices(jax.random.fold_in(jax.random.fold_in(key_of[15], part), 71), part)
    specialist_mixing_shares = jnp.clip(0.19921875 + 0.80078125 * jax.random.uniform(part_splits[6], (CONTEXT_LENGTH, 2), jnp.float32) ** steps_of(part_splits[6], (CONTEXT_LENGTH, 2), ((0, 16),), -0.2, 0.2), 0.19921875, 1.0).astype(jnp.bfloat16)
    specialist_rescale_vector = jnp.clip(1.0 + 0.15 * jax.random.normal(key_of[7], (D,), jnp.float32), 0.25, 1.75)
    specialist_switch_matrix = scatter_about(key_of[8], (D, HID), D ** -0.5, 0.0625, ((0, 8), (1, 16)))
    specialist_widen_matrix = scatter_about(key_of[9], (D, HID), D ** -0.5, 0.0625, ((0, 8), (1, 16)))
    specialist_contract_matrix = scatter_about(key_of[10], (HID, D), HID ** -0.5, 0.0546875, ((0, 16), (1, 8)))
    closing_rescale_vector = jnp.clip(1.0 + 0.1 * jax.random.normal(key_of[11], (D,), jnp.float32), 0.5, 1.5)
    lexicon_matrix = draw_lexicon_matrix(jax.random.fold_in(key_of[15], 71), part)
    softness_divisor = jnp.clip(jax.random.uniform(key_of[13], (1,), jnp.float32, 0.5, 1.0), 0.5, 1.0)
    picked_entry_offsets = place_ends(jax.random.randint(part_splits[14], (ROWS,), 0, SEQ_DEV), jax.random.fold_in(part_splits[14], 1), 0, SEQ_DEV - 1).astype(jnp.int32)
    return {"recurrence_feed": recurrence_feed, "memory_write_matrix": memory_write_matrix, "memory_read_matrix": memory_read_matrix, "log_shrink_table": log_shrink_table, "skip_connection_scale": skip_connection_scale, "specialist_choices": specialist_choices, "specialist_mixing_shares": specialist_mixing_shares, "specialist_rescale_vector": specialist_rescale_vector, "specialist_switch_matrix": specialist_switch_matrix, "specialist_widen_matrix": specialist_widen_matrix, "specialist_contract_matrix": specialist_contract_matrix, "closing_rescale_vector": closing_rescale_vector, "lexicon_matrix": lexicon_matrix, "softness_divisor": softness_divisor, "picked_entry_offsets": picked_entry_offsets}


def scan_reference(recurrence_feed, memory_write_matrix, memory_read_matrix, log_shrink_table, skip_connection_scale):
    block_total = CONTEXT_LENGTH // GROUP
    x_blocks = recurrence_feed.reshape(block_total, GROUP, RECURRENCE_UNITS, HD)
    b_blocks = memory_write_matrix.reshape(block_total, GROUP, DS)
    c_blocks = memory_read_matrix.reshape(block_total, GROUP, DS)
    decay_blocks = log_shrink_table.reshape(block_total, GROUP, RECURRENCE_UNITS)
    causal = jnp.arange(GROUP)[:, None] >= jnp.arange(GROUP)[None, :]

    def block_step(carry_state, inputs):
        x_block, b_block, c_block, decay_block = inputs
        cumulative = jnp.cumsum(decay_block, axis=0)
        scores = jnp.dot(c_block, b_block.T, preferred_element_type=jnp.float32)
        spread = cumulative[:, None, :] - cumulative[None, :, :]
        decay_mat = jnp.where(causal[:, :, None], jnp.exp(jnp.minimum(spread, 0.0)), 0.0)
        mixing = (scores[:, :, None] * decay_mat).astype(jnp.bfloat16)
        x_float = x_block.astype(jnp.float32)
        y_inner = jnp.einsum('ijh,jhp->ihp', mixing.astype(jnp.float32), x_float)
        y_outer = jnp.exp(cumulative)[:, :, None] * jnp.einsum('in,hpn->ihp', c_block.astype(jnp.float32), carry_state, precision=lax.Precision.HIGHEST)
        tail_decay = jnp.exp(cumulative[-1][None, :] - cumulative)
        weighted = (x_float * tail_decay[:, :, None]).astype(jnp.bfloat16)
        local_state = jnp.einsum('jhp,jn->hpn', weighted.astype(jnp.float32), b_block.astype(jnp.float32))
        next_state = jnp.exp(cumulative[-1])[:, None, None] * carry_state + local_state
        y_block = (y_inner + y_outer + skip_connection_scale[None, :, None] * x_float).astype(jnp.bfloat16)
        return (next_state, y_block)
    start_state = jnp.zeros((RECURRENCE_UNITS, HD, DS), jnp.float32)
    unused, outputs = lax.scan(block_step, start_state, (x_blocks, b_blocks, c_blocks, decay_blocks))
    return outputs.reshape(CONTEXT_LENGTH, D)

def moe_reference(mamba_out, specialist_choices, specialist_mixing_shares, specialist_rescale_vector, specialist_switch_matrix, specialist_widen_matrix, specialist_contract_matrix):
    values = mamba_out.astype(jnp.float32)
    inv_rms = lax.rsqrt(lax.optimization_barrier(jnp.mean(values * values, axis=-1, keepdims=True)) + 1e-05)
    normed = (values * inv_rms * specialist_rescale_vector).astype(jnp.bfloat16)
    chosen = specialist_choices == 0
    token_used = jnp.any(chosen, axis=1)
    gate_sum = lax.optimization_barrier(jnp.sum(jnp.where(chosen, specialist_mixing_shares.astype(jnp.float32), 0.0), axis=1))
    limit = CONTEXT_LENGTH // SEQ_DEV * CAP
    index_list = jnp.nonzero(token_used, size=limit, fill_value=0)[0].astype(jnp.int32)
    valid = jnp.arange(limit) < jnp.sum(token_used.astype(jnp.int32))
    rows_in = normed[index_list]
    gate_part = jnp.dot(rows_in, specialist_switch_matrix, preferred_element_type=jnp.float32)
    up_part = jnp.dot(rows_in, specialist_widen_matrix, preferred_element_type=jnp.float32)
    hidden = (jax.nn.silu(gate_part) * up_part).astype(jnp.bfloat16)
    expert_out = jnp.dot(hidden, specialist_contract_matrix, preferred_element_type=jnp.float32)
    expert_out = jnp.where(valid[:, None], expert_out, 0.0)
    contrib = jnp.zeros((CONTEXT_LENGTH, D), jnp.float32).at[index_list].add(expert_out)
    return (values + gate_sum[:, None] * contrib).astype(jnp.bfloat16)

def reference(recurrence_feed, memory_write_matrix, memory_read_matrix, log_shrink_table, skip_connection_scale, specialist_choices, specialist_mixing_shares, specialist_rescale_vector, specialist_switch_matrix, specialist_widen_matrix, specialist_contract_matrix, closing_rescale_vector, lexicon_matrix, softness_divisor, picked_entry_offsets):
    mamba_out = scan_reference(recurrence_feed, memory_write_matrix, memory_read_matrix, log_shrink_table, skip_connection_scale)
    layer_out = moe_reference(mamba_out, specialist_choices, specialist_mixing_shares, specialist_rescale_vector, specialist_switch_matrix, specialist_widen_matrix, specialist_contract_matrix)
    row_index = jnp.arange(ROWS, dtype=jnp.int32) // S_SEQ * SEQ_DEV + picked_entry_offsets.astype(jnp.int32)
    picked = layer_out[row_index].astype(jnp.float32)
    inv_rms = lax.rsqrt(lax.optimization_barrier(jnp.mean(picked * picked, axis=-1, keepdims=True)) + 1e-05)
    classifier_feed = (picked * inv_rms * closing_rescale_vector).astype(jnp.bfloat16)
    softened_scores = jnp.dot(classifier_feed, lexicon_matrix, preferred_element_type=jnp.float32) / softness_divisor[0]
    row_peak = lax.optimization_barrier(jnp.max(softened_scores, axis=1, keepdims=True))
    row_mass = lax.optimization_barrier(jnp.sum(jnp.exp(softened_scores - row_peak), axis=1, keepdims=True))
    log_probs = softened_scores - row_peak - jnp.log(row_mass)
    return (layer_out, log_probs)
```

```python
import jax
import jax.numpy as jnp
from jax import lax
from jax.experimental import pallas as pl
from jax.experimental.pallas import tpu as pltpu
from jax.sharding import PartitionSpec as P

MESH = pl.DeviceIdType.MESH
F32 = jnp.float32
BF16 = jnp.bfloat16
TOK = 256
CH = 1024
SEQ = 16
CHAN = 8
NZ = 8
CAP = 64
HIDL = 768
RSW = 2 * HIDL + 128
WIDTH = 8192
EPS = 1e-5
VMEM_LIMIT = 56 * 1024 * 1024


def dot(a, b):
    return jnp.dot(a, b, preferred_element_type=F32)


def split2(v):
    hi = v.astype(BF16)
    return hi, (v - hi.astype(F32)).astype(BF16)


def split3(v):
    hi = v.astype(BF16)
    rest = v - hi.astype(F32)
    mid = rest.astype(BF16)
    return hi, mid, (rest - mid.astype(F32)).astype(BF16)


def iota(shape, dim):
    return lax.broadcasted_iota(jnp.int32, shape, dim)


def remote(src, dst, send_sem, recv_sem, where):
    return pltpu.make_async_remote_copy(
        src_ref=src,
        dst_ref=dst,
        send_sem=send_sem,
        recv_sem=recv_sem,
        device_id=where,
        device_id_type=MESH,
    )


def greet(axis, size, me):
    barrier = pltpu.get_barrier_semaphore()

    def one(d, carry):
        pl.semaphore_signal(
            barrier, inc=1, device_id={axis: lax.rem(me + d, size)}, device_id_type=MESH
        )
        return carry

    lax.fori_loop(1, size, one, 0)


def scan_kernel(
    x_ref, b_ref, c_ref, la_ref, skip_ref, choice_ref, share_ref,
    mamba_ref, slots_ref, gmap_ref,
    wide, local, taken, decays, prefixes, entry, y_ref,
    dec_send, dec_recv, a_send, a_recv, p_send, p_recv,
):
    me = lax.axis_index("seq")
    greet("seq", SEQ, me)

    wide[...] = jnp.zeros_like(wide)
    wide[0:TOK, 0:16] = la_ref[...]
    wide[TOK : TOK + 1, 0:16] = skip_ref[...]
    tril = (iota((TOK, TOK), 0) >= iota((TOK, TOK), 1)).astype(F32)
    tril_bf = tril.astype(BF16)
    hi, mid, lo = split3(wide[0:TOK, :])
    cum = dot(tril_bf, hi) + dot(tril_bf, mid) + dot(tril_bf, lo)
    last = cum[TOK - 1 : TOK, :]
    spread_map = (iota((128, CH), 1) // 64 == iota((128, CH), 0)).astype(F32).astype(BF16)

    def expand(v):
        hi, lo = split2(v)
        return dot(hi, spread_map) + dot(lo, spread_map)

    decays[me] = jnp.broadcast_to(jnp.exp(last), (8, 128))
    pl.semaphore_wait(pltpu.get_barrier_semaphore(), SEQ - 1)

    def dec_copy(d, there):
        return remote(
            decays.at[me], decays.at[me], dec_send.at[d], dec_recv.at[d], {"seq": there}
        )

    def send_dec(d, carry):
        dec_copy(d, lax.rem(me + d, SEQ)).start()
        return carry

    lax.fori_loop(1, SEQ, send_dec, 0)

    weighted = (x_ref[...].astype(F32) * expand(jnp.exp(last - cum))).astype(BF16)
    b_t = jnp.transpose(b_ref[...].astype(F32)).astype(BF16)
    local[...] = dot(b_t, weighted).astype(BF16)

    def part(ref, p):
        return ref.at[
            pl.ds(pl.multiple_of((p // 2) * 16, 16), 16),
            pl.ds(pl.multiple_of((p % 2) * 512, 512), 512),
        ]

    def a_copy(d, there):
        return remote(part(local, there), taken.at[me], a_send.at[d], a_recv.at[d], {"seq": there})

    def send_a(d, carry):
        a_copy(d, lax.rem(me + d, SEQ)).start()
        return carry

    lax.fori_loop(1, SEQ, send_a, 0)
    taken[me] = part(local, me)[...]

    scores = lax.dot_general(
        c_ref[...], b_ref[...], (((1,), (1,)), ((), ())), preferred_element_type=F32
    )
    scores = scores * tril
    cum_t = jnp.transpose(cum)
    lane = iota((128, 128), 1)

    def heads(pairs):
        for q in pairs:
            cols = slice(128 * q, 128 * q + 128)
            xq = x_ref[:, cols]
            for r in range(2):
                rows = slice(128 * r, 128 * r + 128)
                width = 128 * (r + 1)
                out = []
                for h in (2 * q, 2 * q + 1):
                    decay = jnp.exp(
                        jnp.minimum(cum[rows, h : h + 1] - cum_t[h : h + 1, 0:width], 0.0)
                    )
                    mixing = (scores[rows, 0:width] * decay).astype(BF16)
                    out.append(dot(mixing, xq[0:width, :]))
                y_ref[rows, cols] = jnp.where(lane < 64, out[0], out[1])

    heads(range(0, 4))

    def wait_dec(d, carry):
        dec_copy(d, me).wait_recv()
        a_copy(d, me).wait_recv()
        return carry

    lax.fori_loop(1, SEQ, wait_dec, 0)
    half = lax.rem(me, 2)
    half_map = (
        ((iota((128, 512), 1) + half * 512) // 64 == iota((128, 512), 0)).astype(F32).astype(BF16)
    )
    hi, mid, lo = split3(decays[...].reshape(SEQ * 8, 128))
    factors = dot(hi, half_map) + dot(mid, half_map) + dot(lo, half_map)
    state = jnp.zeros((16, 512), F32)
    for s in range(SEQ):
        prefixes[s] = state.astype(BF16)
        state = factors[8 * s : 8 * s + 1, :] * state + taken[s].astype(F32)

    def p_copy(d, there):
        return remote(prefixes.at[there], part(entry, me), p_send.at[d], p_recv.at[d], {"seq": there})

    def send_p(d, carry):
        p_copy(d, lax.rem(me + d, SEQ)).start()
        return carry

    lax.fori_loop(1, SEQ, send_p, 0)
    part(entry, me)[...] = prefixes[me]

    heads(range(4, 8))

    first, second = choice_ref[:, 0:1] == 0, choice_ref[:, 1:2] == 0
    used = jnp.where(first, 1.0, 0.0) + jnp.where(second, 1.0, 0.0)
    gate = jnp.where(first, share_ref[:, 0:1].astype(F32), 0.0) + jnp.where(
        second, share_ref[:, 1:2].astype(F32), 0.0
    )
    used = jnp.broadcast_to(used, (TOK, 128))
    place = dot(tril_bf, used.astype(BF16)) - 1.0
    slot_map = jnp.where(place == iota((TOK, 128), 1).astype(F32), used, 0.0)
    gmap_ref[...] = (slot_map * gate).astype(BF16)
    slot_t = jnp.transpose(slot_map)[0:CAP, :].astype(BF16)

    skip_wide = expand(wide[TOK : TOK + 8, :])[0:1, :]
    cum_wide = expand(jnp.exp(cum))

    def wait_p(d, carry):
        there = lax.rem(me - d + SEQ, SEQ)
        remote(
            prefixes.at[me], part(entry, there), p_send.at[d], p_recv.at[d], {"seq": there}
        ).wait_recv()
        return carry

    lax.fori_loop(1, SEQ, wait_p, 0)
    outer = dot(c_ref[...], entry[...])
    mamba = (y_ref[...] + cum_wide * outer + skip_wide * x_ref[...].astype(F32)).astype(BF16)
    mamba_ref[...] = mamba
    slots_ref[...] = dot(slot_t, mamba).astype(BF16)

    def wait_sends(d, carry):
        dec_copy(d, me).wait_send()
        a_copy(d, me).wait_send()
        p_copy(d, me).wait_send()
        return carry

    lax.fori_loop(1, SEQ, wait_sends, 0)


def scan_call(*args):
    vm = pl.BlockSpec(memory_space=pltpu.VMEM)
    dma = pltpu.SemaphoreType.DMA
    return pl.pallas_call(
        scan_kernel,
        out_shape=(
            jax.ShapeDtypeStruct((TOK, CH), BF16),
            jax.ShapeDtypeStruct((CAP, CH), BF16),
            jax.ShapeDtypeStruct((TOK, 128), BF16),
        ),
        in_specs=[vm] * len(args),
        out_specs=(vm, vm, vm),
        scratch_shapes=[
            pltpu.VMEM((TOK + 8, 128), F32),
            pltpu.VMEM((128, CH), BF16),
            pltpu.VMEM((SEQ, 16, 512), BF16),
            pltpu.VMEM((SEQ, 8, 128), F32),
            pltpu.VMEM((SEQ, 16, 512), BF16),
            pltpu.VMEM((128, CH), BF16),
            pltpu.VMEM((TOK, CH), F32),
        ]
        + [dma((SEQ,))] * 6,
        compiler_params=pltpu.CompilerParams(
            collective_id=0, has_side_effects=True, vmem_limit_bytes=VMEM_LIMIT
        ),
        name="scan",
    )(*args)


def near_first(i):
    odd = i % 2
    return odd * ((i + 1) // 2) + (1 - odd) * ((NZ - i // 2) % NZ)


def expert_kernel(
    slots_ref, rescale_ref, switch_ref, widen_ref, contract_ref,
    out_ref,
    rows, parts, sums, hidden, x_out, x_in, kept, z_out, z_in,
    ag_send, ag_recv, fw_send, fw_recv, rs_send, rs_recv, hd_send, hd_recv,
    xs_send, xs_recv, zs_send, zs_recv,
):
    me = lax.axis_index("seq")
    ch = lax.axis_index("chan")
    xh, z = me // NZ, me % NZ
    other = (1 - xh) * NZ + z
    barrier = pltpu.get_barrier_semaphore()

    def greet_z(d, carry):
        pl.semaphore_signal(
            barrier, inc=1, device_id={"seq": xh * NZ + (z + d) % NZ}, device_id_type=MESH
        )
        return carry

    lax.fori_loop(1, NZ, greet_z, 0)
    pl.semaphore_signal(barrier, inc=1, device_id={"seq": other}, device_id_type=MESH)
    greet("chan", CHAN, ch)
    rows[me] = slots_ref[...]
    pl.semaphore_wait(barrier, 7 + 1 + 7)

    def ag_copy(d, src, there):
        return remote(rows.at[src], rows.at[src], ag_send.at[d], ag_recv.at[d], {"seq": there})

    def fw_copy(b, half):
        src = half * NZ + b
        return remote(rows.at[src], rows.at[src], fw_send.at[b], fw_recv.at[b], {"seq": other})

    fw_copy(z, xh).start()

    def send_ag(i, carry):
        d = near_first(i)
        ag_copy(d, me, xh * NZ + (z + d) % NZ).start()
        return carry

    lax.fori_loop(1, NZ, send_ag, 0)

    def forward(i):
        d = near_first(i)
        b = (z - d + NZ) % NZ
        ag_copy(d, xh * NZ + b, other).wait_recv()
        fw_copy(b, xh).start()

    def rs_copy(b, d, there, source):
        take = pl.ds(pl.multiple_of(there * 16, 16), 16)
        return remote(
            parts.at[b, take], sums.at[b, source], rs_send.at[b, d], rs_recv.at[b, d], {"chan": there}
        )

    def project(i, carry):
        @pl.when(i < NZ - 1)
        def _():
            forward(i + 1)

        b = (z - near_first(i) + NZ) % NZ
        fw_copy(b, 1 - xh).wait_recv()
        v = jnp.concatenate([rows[b], rows[NZ + b]], axis=0).astype(F32)
        squares = jnp.sum(v * v, axis=1, keepdims=True)
        scaled = (v * rescale_ref[...]).astype(BF16)
        parts[b, :, 0:HIDL] = dot(scaled, switch_ref[...]).astype(BF16)
        parts[b, :, HIDL : 2 * HIDL] = dot(scaled, widen_ref[...]).astype(BF16)
        hi, mid, lo = split3(squares)
        lane = iota((128, 128), 1)
        parts[b, :, 2 * HIDL :] = jnp.where(
            lane == 0,
            hi.astype(F32),
            jnp.where(lane == 1, mid.astype(F32), jnp.where(lane == 2, lo.astype(F32), 0.0)),
        ).astype(BF16)
        for d in range(1, CHAN):
            rs_copy(b, d, lax.rem(ch + d, CHAN), ch).start()
        return carry

    lax.fori_loop(0, NZ, project, 0)

    mine = pl.ds(pl.multiple_of(ch * 16, 16), 16)

    def hd_copy(b, d, source, there):
        take = pl.ds(pl.multiple_of(source * 16, 16), 16)
        return remote(
            hidden.at[b, take], hidden.at[b, take], hd_send.at[b, d], hd_recv.at[b, d], {"chan": there}
        )

    def activate(i, carry):
        b = (z - near_first(i) + NZ) % NZ
        total = parts[b, mine, :].astype(F32)
        for d in range(1, CHAN):
            source = lax.rem(ch - d + CHAN, CHAN)
            rs_copy(b, d, ch, source).wait_recv()
            total = total + sums[b, source].astype(F32)
        squares = jnp.sum(total[:, 2 * HIDL :], axis=1, keepdims=True)
        inv = lax.rsqrt(squares / WIDTH + EPS)
        gate = total[:, 0:HIDL] * inv
        up = total[:, HIDL : 2 * HIDL] * inv
        hidden[b, mine, :] = (gate / (1.0 + jnp.exp(-gate)) * up).astype(BF16)
        for d in range(1, CHAN):
            hd_copy(b, d, ch, lax.rem(ch + d, CHAN)).start()
        return carry

    lax.fori_loop(0, NZ, activate, 0)

    def xs_copy(b):
        return remote(x_out.at[b], x_in.at[b], xs_send.at[b], xs_recv.at[b], {"seq": other})

    ours = pl.ds(pl.multiple_of(xh * CAP, CAP), CAP)
    theirs = pl.ds(pl.multiple_of((1 - xh) * CAP, CAP), CAP)

    def contract(i, carry):
        b = (z - near_first(i) + NZ) % NZ
        for d in range(1, CHAN):
            hd_copy(b, d, lax.rem(ch - d + CHAN, CHAN), ch).wait_recv()
        x_out[b] = dot(hidden[b, theirs, :], contract_ref[...]).astype(BF16)
        xs_copy(b).start()
        kept[b] = dot(hidden[b, ours, :], contract_ref[...])
        return carry

    lax.fori_loop(0, NZ, contract, 0)

    def zs_copy(d, b, source):
        return remote(
            z_out.at[b], z_in.at[source], zs_send.at[d], zs_recv.at[d], {"seq": xh * NZ + b}
        )

    def pass_on(i, carry):
        d = near_first(i)
        b = (z + d) % NZ
        xs_copy(b).wait_recv()
        z_out[b] = (kept[b] + x_in[b].astype(F32)).astype(BF16)
        zs_copy(d, b, z).start()
        return carry

    lax.fori_loop(1, NZ, pass_on, 0)
    xs_copy(z).wait_recv()
    out_ref[...] = kept[z] + x_in[z].astype(F32)

    def collect(i, carry):
        d = near_first(i)
        source = (z - d + NZ) % NZ
        zs_copy(d, z, source).wait_recv()
        out_ref[...] += z_in[source].astype(F32)
        return carry

    lax.fori_loop(1, NZ, collect, 0)

    def wait_sends(i, carry):
        fw_copy(i, xh).wait_send()
        xs_copy(i).wait_send()
        for d in range(1, CHAN):
            rs_copy(i, d, ch, ch).wait_send()
            hd_copy(i, d, ch, ch).wait_send()
        return carry

    lax.fori_loop(0, NZ, wait_sends, 0)

    def wait_z_sends(d, carry):
        ag_copy(d, me, other).wait_send()
        zs_copy(d, z, z).wait_send()
        return carry

    lax.fori_loop(1, NZ, wait_z_sends, 0)


def expert_call(*args):
    vm = pl.BlockSpec(memory_space=pltpu.VMEM)
    dma = pltpu.SemaphoreType.DMA
    return pl.pallas_call(
        expert_kernel,
        out_shape=jax.ShapeDtypeStruct((CAP, CH), F32),
        in_specs=[vm] * len(args),
        out_specs=vm,
        scratch_shapes=[
            pltpu.VMEM((SEQ, CAP, CH), BF16),
            pltpu.VMEM((NZ, 128, RSW), BF16),
            pltpu.VMEM((NZ, CHAN, 16, RSW), BF16),
            pltpu.VMEM((NZ, 128, HIDL), BF16),
            pltpu.VMEM((NZ, CAP, CH), BF16),
            pltpu.VMEM((NZ, CAP, CH), BF16),
            pltpu.VMEM((NZ, CAP, CH), F32),
            pltpu.VMEM((NZ, CAP, CH), BF16),
            pltpu.VMEM((NZ, CAP, CH), BF16),
        ]
        + [dma((NZ,))] * 4
        + [dma((NZ, CHAN))] * 4
        + [dma((NZ,))] * 4,
        compiler_params=pltpu.CompilerParams(
            collective_id=1, has_side_effects=True, vmem_limit_bytes=VMEM_LIMIT
        ),
        name="expert",
    )(*args)


def head_kernel(
    mamba_ref, gmap_ref, expert_ref, pick_ref, closing_ref, lexicon_ref, div_ref,
    layer_ref, prob_ref,
    held, acc, squares, chan_stats, seq_stats,
    z_send, z_recv, a_send, a_recv, b_send, b_recv, c_send, c_recv, s_send, s_recv,
):
    me = lax.axis_index("seq")
    ch = lax.axis_index("chan")
    xh, z = me // NZ, me % NZ
    y, xl = ch // 2, ch % 2
    x = xh * 2 + xl
    barrier = pltpu.get_barrier_semaphore()
    greet("seq", SEQ, me)
    greet("chan", CHAN, ch)
    diagonal = {"seq": (1 - xh) * NZ + z, "chan": y * 2 + 1 - xl}
    pl.semaphore_signal(barrier, inc=1, device_id=diagonal, device_id_type=MESH)

    hi, lo = split2(expert_ref[...])
    gmap = gmap_ref[:, 0:CAP]
    layer = (mamba_ref[...].astype(F32) + dot(gmap, hi) + dot(gmap, lo)).astype(BF16)
    layer_ref[...] = layer
    pick = (iota((16, TOK), 1) == pick_ref[...]).astype(F32).astype(BF16)
    picked = dot(pick, layer).astype(BF16)
    own = pl.ds(pl.multiple_of(z * 16, 16), 16)
    held[0, y, x, own, :] = picked[:, 0:512]
    held[1, y, x, own, :] = picked[:, 512:1024]
    pl.semaphore_wait(barrier, 15 + 7 + 1)

    def at_x(there):
        return {"seq": (there // 2) * NZ + z, "chan": y * 2 + there % 2}

    def at_y(there):
        return {"chan": there * 2 + xl}

    def z_copy(d, source, there):
        ref = held.at[:, y, x, pl.ds(pl.multiple_of(source * 16, 16), 16), :]
        return remote(ref, ref, z_send.at[d], z_recv.at[d], {"seq": xh * NZ + there})

    def send_z(i, carry):
        d = near_first(i)
        z_copy(d, z, (z + d) % NZ).start()
        return carry

    lax.fori_loop(1, NZ, send_z, 0)

    def piece(h, yy, xx):
        return held.at[h, yy, xx]

    def first_copy(h, d, yy, xx, there):
        ref = piece(h, yy, xx)
        return remote(ref, ref, a_send.at[h, d], a_recv.at[h, d], there)

    def second_copy(h, k, d, yy, xx, there):
        ref = piece(h, yy, xx)
        return remote(ref, ref, b_send.at[h, k, d], b_recv.at[h, k, d], there)

    def wait_z(d, carry):
        z_copy(d, (z - d + NZ) % NZ, z).wait_recv()
        return carry

    lax.fori_loop(1, NZ, wait_z, 0)
    for d in (1, 3, 2):
        first_copy(0, d, y, x, at_y((y + d) % 4)).start()
        first_copy(1, d, y, x, at_x((x + d) % 4)).start()
    for d in (1, 3, 2):
        second_copy(0, 0, d, y, x, at_x((x + d) % 4)).start()
        second_copy(1, 0, d, y, x, at_y((y + d) % 4)).start()

    acc[...] = jnp.zeros_like(acc)
    squares[...] = jnp.zeros_like(squares)

    def use(h, yy, xx):
        upper, right = xx // 2, xx % 2
        first = pl.multiple_of((yy * 2 + right) * CH + h * 512, 512)
        v = held[h, yy, xx].astype(F32)
        squares[upper] += jnp.sum(v * v, axis=1, keepdims=True)
        scaled = (v * closing_ref[:, pl.ds(first, 512)]).astype(BF16)
        acc[upper] += dot(scaled, lexicon_ref[pl.ds(first, 512), :])

    def own_pieces(h, carry):
        use(h, y, x)
        return carry

    lax.fori_loop(0, 2, own_pieces, 0)
    for d in (1, 3, 2):
        yy, xx = (y - d + 4) % 4, (x - d + 4) % 4
        first_copy(0, d, yy, x, at_y(y)).wait_recv()
        first_copy(1, d, y, xx, at_x(x)).wait_recv()
        for e in (1, 3, 2):
            second_copy(0, d, e, yy, x, at_x((x + e) % 4)).start()
            second_copy(1, d, e, y, xx, at_y((y + e) % 4)).start()
    for d in (1, 3, 2):
        use(0, (y - d + 4) % 4, x)
        use(1, y, (x - d + 4) % 4)
    def last_pieces(k, carry):
        for e in (1, 3, 2):
            yy, xx = (y - k + 4) % 4, (x - e + 4) % 4
            second_copy(0, k, e, yy, xx, at_x(x)).wait_recv()
            use(0, yy, xx)
            yy, xx = (y - e + 4) % 4, (x - k + 4) % 4
            second_copy(1, k, e, yy, xx, at_y(y)).wait_recv()
            use(1, yy, xx)
        return carry

    lax.fori_loop(0, 4, last_pieces, 0)

    inv = lax.rsqrt(squares[...] / WIDTH + EPS).reshape(TOK, 1)
    scores = acc[...].reshape(TOK, TOK) * inv / div_ref[0, 0]
    top = jnp.max(scores, axis=1, keepdims=True)
    mass = jnp.sum(jnp.exp(scores - top), axis=1, keepdims=True)
    chan_stats[ch, 0] = jnp.transpose(jnp.broadcast_to(top, (TOK, 128)))[0:8, :]
    chan_stats[ch, 1] = jnp.transpose(jnp.broadcast_to(mass, (TOK, 128)))[0:8, :]

    def chan_copy(d, source, there):
        ref = chan_stats.at[source]
        return remote(ref, ref, c_send.at[d], c_recv.at[d], {"chan": there})

    def send_c(d, carry):
        chan_copy(d, ch, lax.rem(ch + d, CHAN)).start()
        return carry

    lax.fori_loop(1, CHAN, send_c, 0)

    def wait_c(d, carry):
        chan_copy(d, lax.rem(ch - d + CHAN, CHAN), ch).wait_recv()
        return carry

    lax.fori_loop(1, CHAN, wait_c, 0)

    def join(ref):
        tops = ref[:, 0]
        top = jnp.max(tops, axis=0)
        return top, jnp.sum(ref[:, 1] * jnp.exp(tops - top[None]), axis=0)

    seq_stats[me, 0], seq_stats[me, 1] = join(chan_stats)

    def seq_copy(d, source, there):
        ref = seq_stats.at[source]
        return remote(ref, ref, s_send.at[d], s_recv.at[d], {"seq": there})

    def send_s(d, carry):
        seq_copy(d, me, lax.rem(me + d, SEQ)).start()
        return carry

    lax.fori_loop(1, SEQ, send_s, 0)

    def wait_s(d, carry):
        seq_copy(d, lax.rem(me - d + SEQ, SEQ), me).wait_recv()
        return carry

    lax.fori_loop(1, SEQ, wait_s, 0)
    top, mass = join(seq_stats)
    norm = top + jnp.log(mass)
    column = jnp.transpose(jnp.broadcast_to(norm[0:1, :], (128, TOK)))[:, 0:1]
    prob_ref[...] = scores - column

    def wait_sends(d, carry):
        z_copy(d, z, z).wait_send()
        chan_copy(d, ch, ch).wait_send()
        return carry

    lax.fori_loop(1, NZ, wait_sends, 0)

    def wait_s_sends(d, carry):
        seq_copy(d, me, me).wait_send()
        return carry

    lax.fori_loop(1, SEQ, wait_s_sends, 0)

    def wait_a_sends(d, carry):
        for h in range(2):
            first_copy(h, d, y, x, at_y(y)).wait_send()
            for k in range(4):
                second_copy(h, k, d, y, x, at_y(y)).wait_send()
        return carry

    lax.fori_loop(1, 4, wait_a_sends, 0)


def head_call(*args):
    vm = pl.BlockSpec(memory_space=pltpu.VMEM)
    dma = pltpu.SemaphoreType.DMA
    return pl.pallas_call(
        head_kernel,
        out_shape=(
            jax.ShapeDtypeStruct((TOK, CH), BF16),
            jax.ShapeDtypeStruct((TOK, TOK), F32),
        ),
        in_specs=[vm] * (len(args) - 1) + [pl.BlockSpec(memory_space=pltpu.SMEM)],
        out_specs=(vm, vm),
        scratch_shapes=[
            pltpu.VMEM((2, 4, 4, 128, 512), BF16),
            pltpu.VMEM((2, 128, TOK), F32),
            pltpu.VMEM((2, 128, 1), F32),
            pltpu.VMEM((CHAN, 2, 8, TOK), F32),
            pltpu.VMEM((SEQ, 2, 8, TOK), F32),
            dma((NZ,)), dma((NZ,)),
            dma((2, 4)), dma((2, 4)),
            dma((2, 4, 4)), dma((2, 4, 4)),
            dma((CHAN,)), dma((CHAN,)),
            dma((SEQ,)), dma((SEQ,)),
        ],
        compiler_params=pltpu.CompilerParams(
            collective_id=2, has_side_effects=True, vmem_limit_bytes=VMEM_LIMIT
        ),
        name="head",
    )(*args)


def shards(
    recurrence_feed,
    memory_write_matrix,
    memory_read_matrix,
    log_shrink_table,
    skip_connection_scale,
    specialist_choices,
    specialist_mixing_shares,
    specialist_rescale_vector,
    specialist_switch_matrix,
    specialist_widen_matrix,
    specialist_contract_matrix,
    closing_rescale_vector,
    lexicon_matrix,
    softness_divisor,
    picked_entry_offsets,
):
    mamba, slots, gmap = scan_call(
        recurrence_feed,
        memory_write_matrix,
        memory_read_matrix,
        log_shrink_table,
        skip_connection_scale.reshape(1, -1),
        specialist_choices,
        specialist_mixing_shares,
    )
    expert = expert_call(
        slots,
        specialist_rescale_vector.reshape(1, -1),
        specialist_switch_matrix,
        specialist_widen_matrix,
        specialist_contract_matrix,
    )
    return head_call(
        mamba,
        gmap,
        expert,
        picked_entry_offsets.reshape(-1, 1),
        closing_rescale_vector.reshape(1, -1),
        lexicon_matrix,
        softness_divisor.reshape(1, 1),
    )


def solution(mesh):
    in_specs = (
        P(("dp", "seq"), "chan"),
        P(("dp", "seq"), None),
        P(("dp", "seq"), None),
        P(("dp", "seq"), "chan"),
        P("chan"),
        P(("dp", "seq"), None),
        P(("dp", "seq"), None),
        P("chan"),
        P("chan", "seq"),
        P("chan", "seq"),
        P("seq", "chan"),
        P(),
        P(None, ("seq", "chan")),
        P(),
        P(("dp", "seq")),
    )
    out_specs = (P(("dp", "seq"), "chan"), P("dp", ("seq", "chan")))
    return jax.shard_map(shards, mesh=mesh, in_specs=in_specs, out_specs=out_specs, check_vma=False)
```

```python
import jax
import jax.numpy as jnp
from jax import lax
from jax.experimental import pallas as pl
from jax.experimental.pallas import tpu as pltpu
from jax.sharding import PartitionSpec as P

MESH = pl.DeviceIdType.MESH
F32 = jnp.float32
BF16 = jnp.bfloat16
TOK = 256
CH = 1024
SEQ = 16
CHAN = 8
NZ = 8
CAP = 64
HIDL = 768
WIDTH = 8192
EPS = 1e-5
VMEM_LIMIT = 56 * 1024 * 1024


def dot(a, b):
    return jnp.dot(a, b, preferred_element_type=F32)


def split2(v):
    hi = v.astype(BF16)
    return hi, (v - hi.astype(F32)).astype(BF16)


def split3(v):
    hi = v.astype(BF16)
    rest = v - hi.astype(F32)
    mid = rest.astype(BF16)
    return hi, mid, (rest - mid.astype(F32)).astype(BF16)


def iota(shape, dim):
    return lax.broadcasted_iota(jnp.int32, shape, dim)


def remote(src, dst, send_sem, recv_sem, where):
    return pltpu.make_async_remote_copy(
        src_ref=src,
        dst_ref=dst,
        send_sem=send_sem,
        recv_sem=recv_sem,
        device_id=where,
        device_id_type=MESH,
    )


def greet(axis, size, me):
    barrier = pltpu.get_barrier_semaphore()

    def one(d, carry):
        pl.semaphore_signal(
            barrier, inc=1, device_id={axis: lax.rem(me + d, size)}, device_id_type=MESH
        )
        return carry

    lax.fori_loop(1, size, one, 0)


def scan_kernel(
    x_ref, b_ref, c_ref, la_ref, skip_ref, choice_ref, share_ref,
    mamba_ref, slots_ref, gmap_ref,
    wide, local, taken, decays, prefixes, entry, y_ref,
    dec_send, dec_recv, a_send, a_recv, p_send, p_recv,
):
    me = lax.axis_index("seq")
    greet("seq", SEQ, me)

    wide[...] = jnp.zeros_like(wide)
    wide[0:16, :] = la_ref[...]
    tril = (iota((TOK, TOK), 0) >= iota((TOK, TOK), 1)).astype(F32)
    triu_bf = (iota((TOK, TOK), 0) <= iota((TOK, TOK), 1)).astype(F32).astype(BF16)
    hi, mid, lo = split3(wide[...])
    cum_t = dot(hi, triu_bf) + dot(mid, triu_bf) + dot(lo, triu_bf)
    cum = jnp.transpose(cum_t)
    last = cum[TOK - 1 : TOK, :]
    spread_map = (iota((128, CH), 1) // 64 == iota((128, CH), 0)).astype(F32).astype(BF16)

    def expand(v):
        hi, lo = split2(v)
        return dot(hi, spread_map) + dot(lo, spread_map)

    decays[me] = jnp.broadcast_to(jnp.exp(last), (8, 128))
    pl.semaphore_wait(pltpu.get_barrier_semaphore(), SEQ - 1)

    def dec_copy(d, there):
        return remote(
            decays.at[me], decays.at[me], dec_send.at[d], dec_recv.at[d], {"seq": there}
        )

    def send_dec(d, carry):
        dec_copy(d, lax.rem(me + d, SEQ)).start()
        return carry

    lax.fori_loop(1, SEQ, send_dec, 0)

    weighted = (x_ref[...].astype(F32) * expand(jnp.exp(last - cum))).astype(BF16)
    b_t = jnp.transpose(b_ref[...].astype(F32)).astype(BF16)
    local[...] = dot(b_t, weighted).astype(BF16)

    def part(ref, p):
        return ref.at[
            pl.ds(pl.multiple_of((p // 2) * 16, 16), 16),
            pl.ds(pl.multiple_of((p % 2) * 512, 512), 512),
        ]

    def a_copy(d, there):
        return remote(part(local, there), taken.at[me], a_send.at[d], a_recv.at[d], {"seq": there})

    def send_a(d, carry):
        a_copy(d, lax.rem(me + d, SEQ)).start()
        return carry

    lax.fori_loop(1, SEQ, send_a, 0)
    taken[me] = part(local, me)[...]

    scores = lax.dot_general(
        c_ref[...], b_ref[...], (((1,), (1,)), ((), ())), preferred_element_type=F32
    )
    scores = scores * tril
    lane = iota((128, 128), 1)

    def heads(pairs):
        for q in pairs:
            cols = slice(128 * q, 128 * q + 128)
            xq = x_ref[:, cols]
            for r in range(2):
                rows = slice(128 * r, 128 * r + 128)
                width = 128 * (r + 1)
                out = []
                for h in (2 * q, 2 * q + 1):
                    decay = jnp.exp(
                        jnp.minimum(cum[rows, h : h + 1] - cum_t[h : h + 1, 0:width], 0.0)
                    )
                    mixing = (scores[rows, 0:width] * decay).astype(BF16)
                    out.append(dot(mixing, xq[0:width, :]))
                y_ref[rows, cols] = jnp.where(lane < 64, out[0], out[1])

    heads(range(0, 4))

    def wait_dec(d, carry):
        dec_copy(d, me).wait_recv()
        a_copy(d, me).wait_recv()
        return carry

    lax.fori_loop(1, SEQ, wait_dec, 0)
    half = lax.rem(me, 2)
    half_map = (
        ((iota((128, 512), 1) + half * 512) // 64 == iota((128, 512), 0)).astype(F32).astype(BF16)
    )
    hi, mid, lo = split3(decays[...].reshape(SEQ * 8, 128))
    factors = dot(hi, half_map) + dot(mid, half_map) + dot(lo, half_map)
    state = jnp.zeros((16, 512), F32)
    for s in range(SEQ):
        prefixes[s] = state.astype(BF16)
        state = factors[8 * s : 8 * s + 1, :] * state + taken[s].astype(F32)

    def p_copy(d, there):
        return remote(prefixes.at[there], part(entry, me), p_send.at[d], p_recv.at[d], {"seq": there})

    def send_p(d, carry):
        p_copy(d, lax.rem(me + d, SEQ)).start()
        return carry

    lax.fori_loop(1, SEQ, send_p, 0)
    part(entry, me)[...] = prefixes[me]

    heads(range(4, 8))

    first, second = choice_ref[0:1, :] == 0, choice_ref[1:2, :] == 0
    used = jnp.where(first, 1.0, 0.0) + jnp.where(second, 1.0, 0.0)
    gate = jnp.where(first, share_ref[0:1, :].astype(F32), 0.0) + jnp.where(
        second, share_ref[1:2, :].astype(F32), 0.0
    )
    used = jnp.broadcast_to(used, (128, TOK))
    place = dot(used.astype(BF16), triu_bf) - 1.0
    slot_map = jnp.where(place == iota((128, TOK), 0).astype(F32), used, 0.0)
    gmap_ref[...] = jnp.transpose(slot_map * gate).astype(BF16)
    slot_t = slot_map[0:CAP, :].astype(BF16)

    skip = jnp.concatenate([skip_ref[...], jnp.zeros((1, 112), F32)], axis=1)
    skip_wide = expand(jnp.broadcast_to(skip, (8, 128)))[0:1, :]
    cum_wide = expand(jnp.exp(cum))

    def wait_p(d, carry):
        there = lax.rem(me - d + SEQ, SEQ)
        remote(
            prefixes.at[me], part(entry, there), p_send.at[d], p_recv.at[d], {"seq": there}
        ).wait_recv()
        return carry

    lax.fori_loop(1, SEQ, wait_p, 0)
    outer = dot(c_ref[...], entry[...])
    mamba = (y_ref[...] + cum_wide * outer + skip_wide * x_ref[...].astype(F32)).astype(BF16)
    mamba_ref[...] = mamba
    slots_ref[...] = dot(slot_t, mamba).astype(BF16)

    def wait_sends(d, carry):
        dec_copy(d, me).wait_send()
        a_copy(d, me).wait_send()
        p_copy(d, me).wait_send()
        return carry

    lax.fori_loop(1, SEQ, wait_sends, 0)


def scan_call(*args):
    vm = pl.BlockSpec(memory_space=pltpu.VMEM)
    dma = pltpu.SemaphoreType.DMA
    return pl.pallas_call(
        scan_kernel,
        out_shape=(
            jax.ShapeDtypeStruct((TOK, CH), BF16),
            jax.ShapeDtypeStruct((CAP, CH), BF16),
            jax.ShapeDtypeStruct((TOK, 128), BF16),
        ),
        in_specs=[vm] * len(args),
        out_specs=(vm, vm, vm),
        scratch_shapes=[
            pltpu.VMEM((128, TOK), F32),
            pltpu.VMEM((128, CH), BF16),
            pltpu.VMEM((SEQ, 16, 512), BF16),
            pltpu.VMEM((SEQ, 8, 128), F32),
            pltpu.VMEM((SEQ, 16, 512), BF16),
            pltpu.VMEM((128, CH), BF16),
            pltpu.VMEM((TOK, CH), F32),
        ]
        + [dma((SEQ,))] * 6,
        compiler_params=pltpu.CompilerParams(
            collective_id=0, has_side_effects=True, vmem_limit_bytes=VMEM_LIMIT
        ),
        name="scan",
    )(*args)


def near_first(i):
    odd = i % 2
    return odd * ((i + 1) // 2) + (1 - odd) * ((NZ - i // 2) % NZ)


def expert_kernel(
    slots_ref, rescale_ref, switch_ref, widen_ref, contract_ref,
    out_ref,
    rows, pg, pu, g1, u1, us, g2, u2, hidden, x_out, x_in, kept, z_out, z_in,
    ag_send, ag_recv, fw_send, fw_recv,
    g1_send, g1_recv, u1_send, u1_recv, g2_send, g2_recv, u2_send, u2_recv,
    hx_send, hx_recv, hy_send, hy_recv,
    xs_send, xs_recv, zs_send, zs_recv,
):
    me = lax.axis_index("seq")
    ch = lax.axis_index("chan")
    xh, z = me // NZ, me % NZ
    y, xl = ch // 2, ch % 2
    other = {"seq": (1 - xh) * NZ + z}
    beside = {"chan": y * 2 + 1 - xl}
    barrier = pltpu.get_barrier_semaphore()

    def at_z(there):
        return {"seq": xh * NZ + there % NZ}

    def at_y(there):
        return {"chan": (there % 4) * 2 + xl}

    for d in range(1, NZ):
        pl.semaphore_signal(barrier, inc=1, device_id=at_z(z + d), device_id_type=MESH)
    for d in range(1, 4):
        pl.semaphore_signal(barrier, inc=1, device_id=at_y(y + d), device_id_type=MESH)
    pl.semaphore_signal(barrier, inc=1, device_id=other, device_id_type=MESH)
    pl.semaphore_signal(barrier, inc=1, device_id=beside, device_id_type=MESH)
    rows[me] = slots_ref[...]
    pl.semaphore_wait(barrier, 7 + 3 + 1 + 1)

    def order(i):
        return (z - near_first(i) + NZ) % NZ

    def sixteen(start):
        return pl.ds(pl.multiple_of(start, 16), 16)

    fw = remote(rows.at[me], rows.at[me], fw_send, fw_recv, other)

    def ag_copy(way, k, half, block):
        row = half * NZ + block % NZ
        ref = rows.at[row]
        there = at_z(z + 1 if way == 0 else z + NZ - 1)
        return remote(ref, ref, ag_send.at[way, k, half], ag_recv.at[way, k, half], there)

    def ag_last(way, half, block):
        ref = rows.at[half * NZ + block % NZ, pl.ds(32 * way, 32)]
        there = at_z(z + 1 if way == 0 else z + NZ - 1)
        return remote(ref, ref, ag_send.at[way, 4, half], ag_recv.at[way, 4, half], there)

    def behind(way, k):
        return z - k + NZ if way == 0 else z + k

    fw.start()
    for way in range(2):
        ag_copy(way, 1, xh, z).start()

    def gather(i):
        @pl.when(i == 0)
        def _():
            remote(rows.at[(1 - xh) * NZ + z], rows.at[(1 - xh) * NZ + z], fw_send, fw_recv, other).wait_recv()
            for way in range(2):
                ag_copy(way, 1, 1 - xh, z).start()

        @pl.when((i % 2 == 1) & (i < NZ - 1))
        def _():
            k = (i + 1) // 2
            for j in range(2):
                half = xh + j - 2 * j * xh
                for way in range(2):
                    ag_copy(way, k, half, behind(way, k)).wait_recv()

                    @pl.when(k < 3)
                    def _():
                        ag_copy(way, k + 1, half, behind(way, k)).start()

                    @pl.when(k == 3)
                    def _():
                        ag_last(way, half, behind(way, k)).start()

        @pl.when(i == NZ - 1)
        def _():
            for way in range(2):
                for half in range(2):
                    ag_last(way, half, z + 4).wait_recv()

    def g1_copy(b):
        return remote(pg.at[b, 1 - xl], g1.at[b], g1_send.at[b], g1_recv.at[b], beside)

    def u1_copy(b, d, there, source):
        return remote(
            pu.at[b, :, sixteen(there * 16)], u1.at[b, source], u1_send.at[b, d], u1_recv.at[b, d], at_y(there)
        )

    def g2_copy(b, d, there, source):
        return remote(
            pg.at[b, xl, sixteen(there * 16)], g2.at[b, source], g2_send.at[b, d], g2_recv.at[b, d], at_y(there)
        )

    def u2_copy(b):
        return remote(us.at[b, 1 - xl], u2.at[b], u2_send.at[b], u2_recv.at[b], beside)

    lane = iota((128, 128), 1)

    def project(i):
        gather(i)
        b = order(i)
        v = jnp.concatenate([rows[b], rows[NZ + b]], axis=0).astype(F32)
        squares = jnp.sum(v * v, axis=1, keepdims=True)
        scaled = (v * rescale_ref[...]).astype(BF16)
        hi, mid, lo = split3(squares)
        extra = jnp.where(
            lane == 0,
            hi.astype(F32),
            jnp.where(lane == 1, mid.astype(F32), jnp.where(lane == 2, lo.astype(F32), 0.0)),
        ).astype(BF16)
        pg[b, :, :, HIDL:] = extra.reshape(2, 64, 128)
        pg[b, :, :, 0:HIDL] = dot(scaled, switch_ref[...]).astype(BF16).reshape(2, 64, HIDL)
        g1_copy(b).start()
        pu[b] = dot(scaled, widen_ref[...]).astype(BF16).reshape(2, 64, HIDL)
        for d in (1, 3, 2):
            u1_copy(b, d, (y + d) % 4, y).start()

    def fold(i):
        b = order(i)
        g1_copy(b).wait_recv()
        pg[b, xl] = (pg[b, xl].astype(F32) + g1[b].astype(F32)).astype(BF16)
        for d in (1, 3, 2):
            g2_copy(b, d, (y + d) % 4, y).start()
        total = pu[b, :, sixteen(y * 16), :].astype(F32)
        for d in (1, 3, 2):
            source = (y - d + 4) % 4
            u1_copy(b, d, y, source).wait_recv()
            total = total + u1[b, source].astype(F32)
        us[b] = total.astype(BF16)
        u2_copy(b).start()

    def hx_copy(b, owner):
        ref = hidden.at[b, owner, sixteen(y * 16)]
        return remote(ref, ref, hx_send.at[b], hx_recv.at[b], beside)

    def hy_copy(b, owner, d, source, there):
        ref = hidden.at[b, owner, sixteen(source * 16)]
        return remote(ref, ref, hy_send.at[b, owner, d], hy_recv.at[b, owner, d], at_y(there))

    def activate(i):
        b = order(i)
        gate = pg[b, xl, sixteen(y * 16), :].astype(F32)
        for d in (1, 3, 2):
            source = (y - d + 4) % 4
            g2_copy(b, d, y, source).wait_recv()
            gate = gate + g2[b, source].astype(F32)
        u2_copy(b).wait_recv()
        up = us[b, xl].astype(F32) + u2[b].astype(F32)
        squares = jnp.sum(gate[:, HIDL:], axis=1, keepdims=True)
        inv = lax.rsqrt(squares / WIDTH + EPS)
        gate = gate[:, 0:HIDL] * inv
        hidden[b, xl, sixteen(y * 16), :] = (gate / (1.0 + jnp.exp(-gate)) * (up * inv)).astype(BF16)
        hx_copy(b, xl).start()
        for d in (1, 3, 2):
            hy_copy(b, xl, d, y, y + d).start()

    def relay(i):
        b = order(i)
        hx_copy(b, 1 - xl).wait_recv()
        for d in (1, 3, 2):
            hy_copy(b, 1 - xl, d, y, y + d).start()

    def xs_copy(b):
        return remote(x_out.at[b], x_in.at[b], xs_send.at[b], xs_recv.at[b], other)

    def contract(i):
        b = order(i)
        for half in range(2):
            for d in (1, 3, 2):
                hy_copy(b, half, d, (y - d + 4) % 4, y).wait_recv()
        x_out[b] = dot(hidden[b, 1 - xh], contract_ref[...]).astype(BF16)
        xs_copy(b).start()
        kept[b] = dot(hidden[b, xh], contract_ref[...])

    def zs_copy(i, b, source):
        return remote(z_out.at[b], z_in.at[source], zs_send.at[i], zs_recv.at[i], at_z(b))

    def pass_on(i):
        b = order(i)
        xs_copy(b).wait_recv()
        z_out[b] = (kept[b] + x_in[b].astype(F32)).astype(BF16)

        @pl.when(i > 0)
        def _():
            zs_copy(i, b, z).start()

    stages = ((project, 0), (fold, 1), (activate, 2), (relay, 3), (contract, 4), (pass_on, 5))

    def step(i, carry):
        for stage, off in stages:

            @pl.when((i >= off) & (i < off + NZ))
            def _():
                stage(i - off)

        return carry

    lax.fori_loop(0, NZ + stages[-1][1], step, 0)
    out_ref[...] = kept[z] + x_in[z].astype(F32)

    def collect(i, carry):
        source = (z + near_first(i)) % NZ
        zs_copy(i, z, source).wait_recv()
        out_ref[...] += z_in[source].astype(F32)
        return carry

    lax.fori_loop(1, NZ, collect, 0)

    def wait_sends(b, carry):
        g1_copy(b).wait_send()
        u2_copy(b).wait_send()
        hx_copy(b, xl).wait_send()
        xs_copy(b).wait_send()
        for d in range(1, 4):
            u1_copy(b, d, y, y).wait_send()
            g2_copy(b, d, y, y).wait_send()
            for half in range(2):
                hy_copy(b, half, d, y, y).wait_send()
        return carry

    lax.fori_loop(0, NZ, wait_sends, 0)

    def wait_z_sends(i, carry):
        zs_copy(i, z, z).wait_send()
        return carry

    lax.fori_loop(1, NZ, wait_z_sends, 0)
    fw.wait_send()
    for way in range(2):
        for half in range(2):
            ag_last(way, half, z).wait_send()
            for k in range(1, 4):
                ag_copy(way, k, half, z).wait_send()


def expert_call(*args):
    vm = pl.BlockSpec(memory_space=pltpu.VMEM)
    dma = pltpu.SemaphoreType.DMA
    return pl.pallas_call(
        expert_kernel,
        out_shape=jax.ShapeDtypeStruct((CAP, CH), F32),
        in_specs=[vm] * len(args),
        out_specs=vm,
        scratch_shapes=[
            pltpu.VMEM((SEQ, CAP, CH), BF16),
            pltpu.VMEM((NZ, 2, 64, HIDL + 128), BF16),
            pltpu.VMEM((NZ, 2, 64, HIDL), BF16),
            pltpu.VMEM((NZ, 64, HIDL + 128), BF16),
            pltpu.VMEM((NZ, 4, 2, 16, HIDL), BF16),
            pltpu.VMEM((NZ, 2, 16, HIDL), BF16),
            pltpu.VMEM((NZ, 4, 16, HIDL + 128), BF16),
            pltpu.VMEM((NZ, 16, HIDL), BF16),
            pltpu.VMEM((NZ, 2, 64, HIDL), BF16),
            pltpu.VMEM((NZ, CAP, CH), BF16),
            pltpu.VMEM((NZ, CAP, CH), BF16),
            pltpu.VMEM((NZ, CAP, CH), F32),
            pltpu.VMEM((NZ, CAP, CH), BF16),
            pltpu.VMEM((NZ, CAP, CH), BF16),
            dma((2, 5, 2)), dma((2, 5, 2)), dma, dma,
            dma((NZ,)), dma((NZ,)), dma((NZ, 4)), dma((NZ, 4)),
            dma((NZ, 4)), dma((NZ, 4)), dma((NZ,)), dma((NZ,)),
            dma((NZ,)), dma((NZ,)), dma((NZ, 2, 4)), dma((NZ, 2, 4)),
            dma((NZ,)), dma((NZ,)), dma((NZ,)), dma((NZ,)),
        ],
        compiler_params=pltpu.CompilerParams(
            collective_id=1, has_side_effects=True, vmem_limit_bytes=VMEM_LIMIT
        ),
        name="expert",
    )(*args)


def head_kernel(
    mamba_ref, gmap_ref, expert_ref, pick_ref, closing_ref, lexicon_ref, div_ref,
    layer_ref, prob_ref,
    held, acc, squares, chan_stats, seq_stats,
    z_send, z_recv, a_send, a_recv, b_send, b_recv, c_send, c_recv, s_send, s_recv,
):
    me = lax.axis_index("seq")
    ch = lax.axis_index("chan")
    xh, z = me // NZ, me % NZ
    y, xl = ch // 2, ch % 2
    x = xh * 2 + xl
    barrier = pltpu.get_barrier_semaphore()
    greet("seq", SEQ, me)
    greet("chan", CHAN, ch)
    diagonal = {"seq": (1 - xh) * NZ + z, "chan": y * 2 + 1 - xl}
    pl.semaphore_signal(barrier, inc=1, device_id=diagonal, device_id_type=MESH)

    hi, lo = split2(expert_ref[...])
    gmap = gmap_ref[:, 0:CAP]
    layer = (mamba_ref[...].astype(F32) + dot(gmap, hi) + dot(gmap, lo)).astype(BF16)
    layer_ref[...] = layer
    offsets = jnp.concatenate(
        [pick_ref[...].astype(F32), jnp.full((1, 112), -1.0, F32)], axis=1
    )
    offsets = jnp.transpose(jnp.broadcast_to(offsets, (128, 128)))[0:16, 0:1]
    pick = (iota((16, TOK), 1).astype(F32) == offsets).astype(F32).astype(BF16)
    picked = dot(pick, layer).astype(BF16)
    own = pl.ds(pl.multiple_of(z * 16, 16), 16)
    held[0, y, x, own, :] = picked[:, 0:512]
    held[1, y, x, own, :] = picked[:, 512:1024]
    pl.semaphore_wait(barrier, 15 + 7 + 1)

    def at_x(there):
        return {"seq": (there // 2) * NZ + z, "chan": y * 2 + there % 2}

    def at_y(there):
        return {"chan": there * 2 + xl}

    def z_copy(d, source, there):
        ref = held.at[:, y, x, pl.ds(pl.multiple_of(source * 16, 16), 16), :]
        return remote(ref, ref, z_send.at[d], z_recv.at[d], {"seq": xh * NZ + there})

    def send_z(i, carry):
        d = near_first(i)
        z_copy(d, z, (z + d) % NZ).start()
        return carry

    lax.fori_loop(1, NZ, send_z, 0)

    def piece(h, yy, xx):
        return held.at[h, yy, xx]

    def first_copy(h, d, yy, xx, there):
        ref = piece(h, yy, xx)
        return remote(ref, ref, a_send.at[h, d], a_recv.at[h, d], there)

    def second_copy(h, k, d, yy, xx, there):
        ref = piece(h, yy, xx)
        return remote(ref, ref, b_send.at[h, k, d], b_recv.at[h, k, d], there)

    def wait_z(d, carry):
        z_copy(d, (z - d + NZ) % NZ, z).wait_recv()
        return carry

    lax.fori_loop(1, NZ, wait_z, 0)
    for d in (1, 3, 2):
        first_copy(0, d, y, x, at_y((y + d) % 4)).start()
        first_copy(1, d, y, x, at_x((x + d) % 4)).start()
    for d in (1, 3, 2):
        second_copy(0, 0, d, y, x, at_x((x + d) % 4)).start()
        second_copy(1, 0, d, y, x, at_y((y + d) % 4)).start()

    acc[...] = jnp.zeros_like(acc)
    squares[...] = jnp.zeros_like(squares)

    def use(h, yy, xx):
        upper, right = xx // 2, xx % 2
        first = pl.multiple_of((yy * 2 + right) * CH + h * 512, 512)
        v = held[h, yy, xx].astype(F32)
        squares[upper] += jnp.sum(v * v, axis=1, keepdims=True)
        scaled = (v * closing_ref[:, pl.ds(first, 512)]).astype(BF16)
        acc[upper] += dot(scaled, lexicon_ref[pl.ds(first, 512), :])

    def own_pieces(h, carry):
        use(h, y, x)
        return carry

    lax.fori_loop(0, 2, own_pieces, 0)
    for d in (1, 3, 2):
        yy, xx = (y - d + 4) % 4, (x - d + 4) % 4
        first_copy(0, d, yy, x, at_y(y)).wait_recv()
        first_copy(1, d, y, xx, at_x(x)).wait_recv()
        for e in (1, 3, 2):
            second_copy(0, d, e, yy, x, at_x((x + e) % 4)).start()
            second_copy(1, d, e, y, xx, at_y((y + e) % 4)).start()
    for d in (1, 3, 2):
        use(0, (y - d + 4) % 4, x)
        use(1, y, (x - d + 4) % 4)
    def last_pieces(k, carry):
        for e in (1, 3, 2):
            yy, xx = (y - k + 4) % 4, (x - e + 4) % 4
            second_copy(0, k, e, yy, xx, at_x(x)).wait_recv()
            use(0, yy, xx)
            yy, xx = (y - e + 4) % 4, (x - k + 4) % 4
            second_copy(1, k, e, yy, xx, at_y(y)).wait_recv()
            use(1, yy, xx)
        return carry

    lax.fori_loop(0, 4, last_pieces, 0)

    inv = lax.rsqrt(squares[...] / WIDTH + EPS).reshape(TOK, 1)
    scores = acc[...].reshape(TOK, TOK) * inv / div_ref[0, 0]
    top = jnp.max(scores, axis=1, keepdims=True)
    mass = jnp.sum(jnp.exp(scores - top), axis=1, keepdims=True)
    chan_stats[ch, 0] = jnp.transpose(jnp.broadcast_to(top, (TOK, 128)))[0:8, :]
    chan_stats[ch, 1] = jnp.transpose(jnp.broadcast_to(mass, (TOK, 128)))[0:8, :]

    def chan_copy(d, source, there):
        ref = chan_stats.at[source]
        return remote(ref, ref, c_send.at[d], c_recv.at[d], {"chan": there})

    def send_c(d, carry):
        chan_copy(d, ch, lax.rem(ch + d, CHAN)).start()
        return carry

    lax.fori_loop(1, CHAN, send_c, 0)

    def wait_c(d, carry):
        chan_copy(d, lax.rem(ch - d + CHAN, CHAN), ch).wait_recv()
        return carry

    lax.fori_loop(1, CHAN, wait_c, 0)

    def join(ref):
        tops = ref[:, 0]
        top = jnp.max(tops, axis=0)
        return top, jnp.sum(ref[:, 1] * jnp.exp(tops - top[None]), axis=0)

    seq_stats[me, 0], seq_stats[me, 1] = join(chan_stats)

    def seq_copy(d, source, there):
        ref = seq_stats.at[source]
        return remote(ref, ref, s_send.at[d], s_recv.at[d], {"seq": there})

    def send_s(d, carry):
        seq_copy(d, me, lax.rem(me + d, SEQ)).start()
        return carry

    lax.fori_loop(1, SEQ, send_s, 0)

    def wait_s(d, carry):
        seq_copy(d, lax.rem(me - d + SEQ, SEQ), me).wait_recv()
        return carry

    lax.fori_loop(1, SEQ, wait_s, 0)
    top, mass = join(seq_stats)
    norm = top + jnp.log(mass)
    column = jnp.transpose(jnp.broadcast_to(norm[0:1, :], (128, TOK)))[:, 0:1]
    prob_ref[...] = scores - column

    def wait_sends(d, carry):
        z_copy(d, z, z).wait_send()
        chan_copy(d, ch, ch).wait_send()
        return carry

    lax.fori_loop(1, NZ, wait_sends, 0)

    def wait_s_sends(d, carry):
        seq_copy(d, me, me).wait_send()
        return carry

    lax.fori_loop(1, SEQ, wait_s_sends, 0)

    def wait_a_sends(d, carry):
        for h in range(2):
            first_copy(h, d, y, x, at_y(y)).wait_send()
            for k in range(4):
                second_copy(h, k, d, y, x, at_y(y)).wait_send()
        return carry

    lax.fori_loop(1, 4, wait_a_sends, 0)


def head_call(*args):
    vm = pl.BlockSpec(memory_space=pltpu.VMEM)
    dma = pltpu.SemaphoreType.DMA
    return pl.pallas_call(
        head_kernel,
        out_shape=(
            jax.ShapeDtypeStruct((TOK, CH), BF16),
            jax.ShapeDtypeStruct((TOK, TOK), F32),
        ),
        in_specs=[vm] * (len(args) - 1) + [pl.BlockSpec(memory_space=pltpu.SMEM)],
        out_specs=(vm, vm),
        scratch_shapes=[
            pltpu.VMEM((2, 4, 4, 128, 512), BF16),
            pltpu.VMEM((2, 128, TOK), F32),
            pltpu.VMEM((2, 128, 1), F32),
            pltpu.VMEM((CHAN, 2, 8, TOK), F32),
            pltpu.VMEM((SEQ, 2, 8, TOK), F32),
            dma((NZ,)), dma((NZ,)),
            dma((2, 4)), dma((2, 4)),
            dma((2, 4, 4)), dma((2, 4, 4)),
            dma((CHAN,)), dma((CHAN,)),
            dma((SEQ,)), dma((SEQ,)),
        ],
        compiler_params=pltpu.CompilerParams(
            collective_id=2, has_side_effects=True, vmem_limit_bytes=VMEM_LIMIT
        ),
        name="head",
    )(*args)


def shards(
    recurrence_feed,
    memory_write_matrix,
    memory_read_matrix,
    log_shrink_table,
    skip_connection_scale,
    specialist_choices,
    specialist_mixing_shares,
    specialist_rescale_vector,
    specialist_switch_matrix,
    specialist_widen_matrix,
    specialist_contract_matrix,
    closing_rescale_vector,
    lexicon_matrix,
    softness_divisor,
    picked_entry_offsets,
):
    mamba, slots, gmap = scan_call(
        recurrence_feed,
        memory_write_matrix,
        memory_read_matrix,
        log_shrink_table.T,
        skip_connection_scale.reshape(1, -1),
        specialist_choices.T,
        specialist_mixing_shares.T,
    )
    expert = expert_call(
        slots,
        specialist_rescale_vector.reshape(1, -1),
        specialist_switch_matrix,
        specialist_widen_matrix,
        specialist_contract_matrix,
    )
    return head_call(
        mamba,
        gmap,
        expert,
        picked_entry_offsets.reshape(1, -1),
        closing_rescale_vector.reshape(1, -1),
        lexicon_matrix,
        softness_divisor.reshape(1, 1),
    )


def solution(mesh):
    in_specs = (
        P(("dp", "seq"), "chan"),
        P(("dp", "seq"), None),
        P(("dp", "seq"), None),
        P(("dp", "seq"), "chan"),
        P("chan"),
        P(("dp", "seq"), None),
        P(("dp", "seq"), None),
        P("chan"),
        P("chan", "seq"),
        P("chan", "seq"),
        P("seq", "chan"),
        P(),
        P(None, ("seq", "chan")),
        P(),
        P(("dp", "seq")),
    )
    out_specs = (P(("dp", "seq"), "chan"), P("dp", ("seq", "chan")))
    return jax.shard_map(shards, mesh=mesh, in_specs=in_specs, out_specs=out_specs, check_vma=False)
```

```python
import jax
import jax.numpy as jnp
from jax import lax
from jax.experimental import pallas as pl
from jax.experimental.pallas import tpu as pltpu
from jax.sharding import PartitionSpec as P

MESH = pl.DeviceIdType.MESH
F32 = jnp.float32
BF16 = jnp.bfloat16
TOK = 256
CH = 1024
SEQ = 16
CHAN = 8
NZ = 8
CAP = 64
HIDL = 768
WIDTH = 8192
EPS = 1e-5
VMEM_LIMIT = 56 * 1024 * 1024


def dot(a, b):
    return jnp.dot(a, b, preferred_element_type=F32)


def split2(v):
    hi = v.astype(BF16)
    return hi, (v - hi.astype(F32)).astype(BF16)


def split3(v):
    hi = v.astype(BF16)
    rest = v - hi.astype(F32)
    mid = rest.astype(BF16)
    return hi, mid, (rest - mid.astype(F32)).astype(BF16)


def iota(shape, dim):
    return lax.broadcasted_iota(jnp.int32, shape, dim)


def remote(src, dst, send_sem, recv_sem, where):
    return pltpu.make_async_remote_copy(
        src_ref=src,
        dst_ref=dst,
        send_sem=send_sem,
        recv_sem=recv_sem,
        device_id=where,
        device_id_type=MESH,
    )


def greet(axis, size, me):
    barrier = pltpu.get_barrier_semaphore()

    def one(d, carry):
        pl.semaphore_signal(
            barrier, inc=1, device_id={axis: lax.rem(me + d, size)}, device_id_type=MESH
        )
        return carry

    lax.fori_loop(1, size, one, 0)


def scan_part(
    x_ref, b_ref, c_ref, la_ref, skip_ref, choice_ref, share_ref,
    mamba_ref, rows, gmap_ref,
    wide, local, taken, decays, prefixes, entry, y_ref,
    dec_send, dec_recv, a_send, a_recv, p_send, p_recv,
):
    me = lax.axis_index("seq")

    wide[...] = jnp.zeros_like(wide)
    wide[0:16, :] = la_ref[...]
    tril = (iota((TOK, TOK), 0) >= iota((TOK, TOK), 1)).astype(F32)
    triu_bf = (iota((TOK, TOK), 0) <= iota((TOK, TOK), 1)).astype(F32).astype(BF16)
    hi, mid, lo = split3(wide[...])
    cum_t = dot(hi, triu_bf) + dot(mid, triu_bf) + dot(lo, triu_bf)
    cum = jnp.transpose(cum_t)
    last = cum[TOK - 1 : TOK, :]
    spread_map = (iota((128, CH), 1) // 64 == iota((128, CH), 0)).astype(F32).astype(BF16)

    def expand(v):
        hi, lo = split2(v)
        return dot(hi, spread_map) + dot(lo, spread_map)

    decays[me] = jnp.broadcast_to(jnp.exp(last), (8, 128))
    pl.semaphore_wait(pltpu.get_barrier_semaphore(), 15 + 7 + 1)

    def dec_copy(d, there):
        return remote(
            decays.at[me], decays.at[me], dec_send.at[d], dec_recv.at[d], {"seq": there}
        )

    def send_dec(d, carry):
        dec_copy(d, lax.rem(me + d, SEQ)).start()
        return carry

    lax.fori_loop(1, SEQ, send_dec, 0)

    weighted = (x_ref[...].astype(F32) * expand(jnp.exp(last - cum))).astype(BF16)
    b_t = jnp.transpose(b_ref[...].astype(F32)).astype(BF16)
    local[...] = dot(b_t, weighted).astype(BF16)

    def part(ref, p):
        return ref.at[
            pl.ds(pl.multiple_of((p // 2) * 16, 16), 16),
            pl.ds(pl.multiple_of((p % 2) * 512, 512), 512),
        ]

    def a_copy(d, there):
        return remote(part(local, there), taken.at[me], a_send.at[d], a_recv.at[d], {"seq": there})

    def send_a(d, carry):
        a_copy(d, lax.rem(me + d, SEQ)).start()
        return carry

    lax.fori_loop(1, SEQ, send_a, 0)
    taken[me] = part(local, me)[...]

    scores = lax.dot_general(
        c_ref[...], b_ref[...], (((1,), (1,)), ((), ())), preferred_element_type=F32
    )
    scores = scores * tril
    lane = iota((128, 128), 1)

    def heads(pairs):
        for q in pairs:
            cols = slice(128 * q, 128 * q + 128)
            xq = x_ref[:, cols]
            for r in range(2):
                rows = slice(128 * r, 128 * r + 128)
                width = 128 * (r + 1)
                out = []
                for h in (2 * q, 2 * q + 1):
                    decay = jnp.exp(
                        jnp.minimum(cum[rows, h : h + 1] - cum_t[h : h + 1, 0:width], 0.0)
                    )
                    mixing = (scores[rows, 0:width] * decay).astype(BF16)
                    out.append(dot(mixing, xq[0:width, :]))
                y_ref[rows, cols] = jnp.where(lane < 64, out[0], out[1])

    heads(range(0, 4))

    def wait_dec(d, carry):
        dec_copy(d, me).wait_recv()
        a_copy(d, me).wait_recv()
        return carry

    lax.fori_loop(1, SEQ, wait_dec, 0)
    half = lax.rem(me, 2)
    half_map = (
        ((iota((128, 512), 1) + half * 512) // 64 == iota((128, 512), 0)).astype(F32).astype(BF16)
    )
    hi, mid, lo = split3(decays[...].reshape(SEQ * 8, 128))
    factors = dot(hi, half_map) + dot(mid, half_map) + dot(lo, half_map)
    state = jnp.zeros((16, 512), F32)
    for s in range(SEQ):
        prefixes[s] = state.astype(BF16)
        state = factors[8 * s : 8 * s + 1, :] * state + taken[s].astype(F32)

    def p_copy(d, there):
        return remote(prefixes.at[there], part(entry, me), p_send.at[d], p_recv.at[d], {"seq": there})

    def send_p(d, carry):
        p_copy(d, lax.rem(me + d, SEQ)).start()
        return carry

    lax.fori_loop(1, SEQ, send_p, 0)
    part(entry, me)[...] = prefixes[me]

    heads(range(4, 8))

    first, second = choice_ref[0:1, :] == 0, choice_ref[1:2, :] == 0
    used = jnp.where(first, 1.0, 0.0) + jnp.where(second, 1.0, 0.0)
    gate = jnp.where(first, share_ref[0:1, :].astype(F32), 0.0) + jnp.where(
        second, share_ref[1:2, :].astype(F32), 0.0
    )
    used = jnp.broadcast_to(used, (128, TOK))
    place = dot(used.astype(BF16), triu_bf) - 1.0
    slot_map = jnp.where(place == iota((128, TOK), 0).astype(F32), used, 0.0)
    gmap_ref[...] = jnp.transpose(slot_map * gate).astype(BF16)
    slot_t = slot_map[0:CAP, :].astype(BF16)

    skip = jnp.concatenate([skip_ref[...], jnp.zeros((1, 112), F32)], axis=1)
    skip_wide = expand(jnp.broadcast_to(skip, (8, 128)))[0:1, :]
    cum_wide = expand(jnp.exp(cum))

    def wait_p(d, carry):
        there = lax.rem(me - d + SEQ, SEQ)
        remote(
            prefixes.at[me], part(entry, there), p_send.at[d], p_recv.at[d], {"seq": there}
        ).wait_recv()
        return carry

    lax.fori_loop(1, SEQ, wait_p, 0)
    outer = dot(c_ref[...], entry[...])
    mamba = (y_ref[...] + cum_wide * outer + skip_wide * x_ref[...].astype(F32)).astype(BF16)
    mamba_ref[...] = mamba
    rows[me] = dot(slot_t, mamba).astype(BF16)

    def drain():
        def wait_sends(d, carry):
            dec_copy(d, me).wait_send()
            a_copy(d, me).wait_send()
            p_copy(d, me).wait_send()
            return carry

        lax.fori_loop(1, SEQ, wait_sends, 0)

    return drain


def near_first(i):
    odd = i % 2
    return odd * ((i + 1) // 2) + (1 - odd) * ((NZ - i // 2) % NZ)


def expert_part(
    idle, rescale_ref, switch_ref, widen_ref, contract_ref,
    out_ref,
    rows, pg, pu, g1, u1, us, g2, u2, hidden, x_out, x_in, kept, z_out, z_in,
    ag_send, ag_recv, fw_send, fw_recv,
    g1_send, g1_recv, u1_send, u1_recv, g2_send, g2_recv, u2_send, u2_recv,
    hx_send, hx_recv, hy_send, hy_recv,
    xs_send, xs_recv, zs_send, zs_recv,
):
    me = lax.axis_index("seq")
    ch = lax.axis_index("chan")
    xh, z = me // NZ, me % NZ
    y, xl = ch // 2, ch % 2
    other = {"seq": (1 - xh) * NZ + z}
    beside = {"chan": y * 2 + 1 - xl}

    def at_z(there):
        return {"seq": xh * NZ + there % NZ}

    def at_y(there):
        return {"chan": (there % 4) * 2 + xl}

    def order(i):
        return (z - near_first(i) + NZ) % NZ

    def sixteen(start):
        return pl.ds(pl.multiple_of(start, 16), 16)

    fw = remote(rows.at[me], rows.at[me], fw_send, fw_recv, other)

    def ag_copy(way, k, half, block):
        row = half * NZ + block % NZ
        ref = rows.at[row]
        there = at_z(z + 1 if way == 0 else z + NZ - 1)
        return remote(ref, ref, ag_send.at[way, k, half], ag_recv.at[way, k, half], there)

    def ag_last(way, half, block):
        ref = rows.at[half * NZ + block % NZ, pl.ds(32 * way, 32)]
        there = at_z(z + 1 if way == 0 else z + NZ - 1)
        return remote(ref, ref, ag_send.at[way, 4, half], ag_recv.at[way, 4, half], there)

    def behind(way, k):
        return z - k + NZ if way == 0 else z + k

    fw.start()
    for way in range(2):
        ag_copy(way, 1, xh, z).start()

    def gather(i):
        @pl.when(i == 0)
        def _():
            remote(rows.at[(1 - xh) * NZ + z], rows.at[(1 - xh) * NZ + z], fw_send, fw_recv, other).wait_recv()
            for way in range(2):
                ag_copy(way, 1, 1 - xh, z).start()
            idle()

        @pl.when((i % 2 == 1) & (i < NZ - 1))
        def _():
            k = (i + 1) // 2
            for j in range(2):
                half = xh + j - 2 * j * xh
                for way in range(2):
                    ag_copy(way, k, half, behind(way, k)).wait_recv()

                    @pl.when(k < 3)
                    def _():
                        ag_copy(way, k + 1, half, behind(way, k)).start()

                    @pl.when(k == 3)
                    def _():
                        ag_last(way, half, behind(way, k)).start()

        @pl.when(i == NZ - 1)
        def _():
            for way in range(2):
                for half in range(2):
                    ag_last(way, half, z + 4).wait_recv()

    def g1_copy(b):
        return remote(pg.at[b, 1 - xl], g1.at[b], g1_send.at[b], g1_recv.at[b], beside)

    def u1_copy(b, d, there, source):
        return remote(
            pu.at[b, :, sixteen(there * 16)], u1.at[b, source], u1_send.at[b, d], u1_recv.at[b, d], at_y(there)
        )

    def g2_copy(b, d, there, source):
        return remote(
            pg.at[b, xl, sixteen(there * 16)], g2.at[b, source], g2_send.at[b, d], g2_recv.at[b, d], at_y(there)
        )

    def u2_copy(b):
        return remote(us.at[b, 1 - xl], u2.at[b], u2_send.at[b], u2_recv.at[b], beside)

    lane = iota((128, 128), 1)

    def project(i):
        gather(i)
        b = order(i)
        v = jnp.concatenate([rows[b], rows[NZ + b]], axis=0).astype(F32)
        squares = jnp.sum(v * v, axis=1, keepdims=True)
        scaled = (v * rescale_ref[...]).astype(BF16)
        hi, mid, lo = split3(squares)
        extra = jnp.where(
            lane == 0,
            hi.astype(F32),
            jnp.where(lane == 1, mid.astype(F32), jnp.where(lane == 2, lo.astype(F32), 0.0)),
        ).astype(BF16)
        pg[b, :, :, HIDL:] = extra.reshape(2, 64, 128)
        pg[b, :, :, 0:HIDL] = dot(scaled, switch_ref[...]).astype(BF16).reshape(2, 64, HIDL)
        g1_copy(b).start()
        pu[b] = dot(scaled, widen_ref[...]).astype(BF16).reshape(2, 64, HIDL)
        for d in (1, 3, 2):
            u1_copy(b, d, (y + d) % 4, y).start()

    def fold(i):
        b = order(i)
        g1_copy(b).wait_recv()
        pg[b, xl] = (pg[b, xl].astype(F32) + g1[b].astype(F32)).astype(BF16)
        for d in (1, 3, 2):
            g2_copy(b, d, (y + d) % 4, y).start()
        total = pu[b, :, sixteen(y * 16), :].astype(F32)
        for d in (1, 3, 2):
            source = (y - d + 4) % 4
            u1_copy(b, d, y, source).wait_recv()
            total = total + u1[b, source].astype(F32)
        us[b] = total.astype(BF16)
        u2_copy(b).start()

    def hx_copy(b, owner):
        ref = hidden.at[b, owner, sixteen(y * 16)]
        return remote(ref, ref, hx_send.at[b], hx_recv.at[b], beside)

    def hy_copy(b, owner, d, source, there):
        ref = hidden.at[b, owner, sixteen(source * 16)]
        return remote(ref, ref, hy_send.at[b, owner, d], hy_recv.at[b, owner, d], at_y(there))

    def activate(i):
        b = order(i)
        gate = pg[b, xl, sixteen(y * 16), :].astype(F32)
        for d in (1, 3, 2):
            source = (y - d + 4) % 4
            g2_copy(b, d, y, source).wait_recv()
            gate = gate + g2[b, source].astype(F32)
        u2_copy(b).wait_recv()
        up = us[b, xl].astype(F32) + u2[b].astype(F32)
        squares = jnp.sum(gate[:, HIDL:], axis=1, keepdims=True)
        inv = lax.rsqrt(squares / WIDTH + EPS)
        gate = gate[:, 0:HIDL] * inv
        hidden[b, xl, sixteen(y * 16), :] = (gate / (1.0 + jnp.exp(-gate)) * (up * inv)).astype(BF16)
        hx_copy(b, xl).start()
        for d in (1, 3, 2):
            hy_copy(b, xl, d, y, y + d).start()

    def relay(i):
        b = order(i)
        hx_copy(b, 1 - xl).wait_recv()
        for d in (1, 3, 2):
            hy_copy(b, 1 - xl, d, y, y + d).start()

    def xs_copy(b):
        return remote(x_out.at[b], x_in.at[b], xs_send.at[b], xs_recv.at[b], other)

    def contract(i):
        b = order(i)
        for half in range(2):
            for d in (1, 3, 2):
                hy_copy(b, half, d, (y - d + 4) % 4, y).wait_recv()
        x_out[b] = dot(hidden[b, 1 - xh], contract_ref[...]).astype(BF16)
        xs_copy(b).start()
        kept[b] = dot(hidden[b, xh], contract_ref[...])

    def zs_copy(i, b, source):
        return remote(z_out.at[b], z_in.at[source], zs_send.at[i], zs_recv.at[i], at_z(b))

    def pass_on(i):
        b = order(i)
        xs_copy(b).wait_recv()
        z_out[b] = (kept[b] + x_in[b].astype(F32)).astype(BF16)

        @pl.when(i > 0)
        def _():
            zs_copy(i, b, z).start()

    stages = ((project, 0), (fold, 1), (activate, 2), (relay, 3), (contract, 4), (pass_on, 5))

    def step(i, carry):
        for stage, off in stages:

            @pl.when((i >= off) & (i < off + NZ))
            def _():
                stage(i - off)

        return carry

    lax.fori_loop(0, NZ + stages[-1][1], step, 0)
    out_ref[...] = kept[z] + x_in[z].astype(F32)

    def collect(i, carry):
        source = (z + near_first(i)) % NZ
        zs_copy(i, z, source).wait_recv()
        out_ref[...] += z_in[source].astype(F32)
        return carry

    lax.fori_loop(1, NZ, collect, 0)

    def drain():
        def wait_sends(b, carry):
            g1_copy(b).wait_send()
            u2_copy(b).wait_send()
            hx_copy(b, xl).wait_send()
            xs_copy(b).wait_send()
            for d in range(1, 4):
                u1_copy(b, d, y, y).wait_send()
                g2_copy(b, d, y, y).wait_send()
                for half in range(2):
                    hy_copy(b, half, d, y, y).wait_send()
            return carry

        lax.fori_loop(0, NZ, wait_sends, 0)

        def wait_z_sends(i, carry):
            zs_copy(i, z, z).wait_send()
            return carry

        lax.fori_loop(1, NZ, wait_z_sends, 0)
        fw.wait_send()
        for way in range(2):
            for half in range(2):
                ag_last(way, half, z).wait_send()
                for k in range(1, 4):
                    ag_copy(way, k, half, z).wait_send()

    return drain


def head_part(
    idle, mamba_ref, gmap_ref, expert_ref, pick_ref, closing_ref, lexicon_ref, div_ref,
    layer_ref, prob_ref,
    held, acc, squares, chan_stats, seq_stats,
    z_send, z_recv, a_send, a_recv, b_send, b_recv, c_send, c_recv, s_send, s_recv,
):
    me = lax.axis_index("seq")
    ch = lax.axis_index("chan")
    xh, z = me // NZ, me % NZ
    y, xl = ch // 2, ch % 2
    x = xh * 2 + xl
    hi, lo = split2(expert_ref[...])
    gmap = gmap_ref[:, 0:CAP]
    layer = (mamba_ref[...].astype(F32) + dot(gmap, hi) + dot(gmap, lo)).astype(BF16)
    layer_ref[...] = layer
    offsets = jnp.concatenate(
        [pick_ref[...].astype(F32), jnp.full((1, 112), -1.0, F32)], axis=1
    )
    offsets = jnp.transpose(jnp.broadcast_to(offsets, (128, 128)))[0:16, 0:1]
    pick = (iota((16, TOK), 1).astype(F32) == offsets).astype(F32).astype(BF16)
    picked = dot(pick, layer).astype(BF16)
    own = pl.ds(pl.multiple_of(z * 16, 16), 16)
    held[0, y, x, own, :] = picked[:, 0:512]
    held[1, y, x, own, :] = picked[:, 512:1024]
    def at_x(there):
        return {"seq": (there // 2) * NZ + z, "chan": y * 2 + there % 2}

    def at_y(there):
        return {"chan": there * 2 + xl}

    def z_copy(d, source, there):
        ref = held.at[:, y, x, pl.ds(pl.multiple_of(source * 16, 16), 16), :]
        return remote(ref, ref, z_send.at[d], z_recv.at[d], {"seq": xh * NZ + there})

    def send_z(i, carry):
        d = near_first(i)
        z_copy(d, z, (z + d) % NZ).start()
        return carry

    lax.fori_loop(1, NZ, send_z, 0)

    def piece(h, yy, xx):
        return held.at[h, yy, xx]

    def first_copy(h, d, yy, xx, there):
        ref = piece(h, yy, xx)
        return remote(ref, ref, a_send.at[h, d], a_recv.at[h, d], there)

    def second_copy(h, k, d, yy, xx, there):
        ref = piece(h, yy, xx)
        return remote(ref, ref, b_send.at[h, k, d], b_recv.at[h, k, d], there)

    def wait_z(d, carry):
        z_copy(d, (z - d + NZ) % NZ, z).wait_recv()
        return carry

    lax.fori_loop(1, NZ, wait_z, 0)
    for d in (1, 3, 2):
        first_copy(0, d, y, x, at_y((y + d) % 4)).start()
        first_copy(1, d, y, x, at_x((x + d) % 4)).start()
    for d in (1, 3, 2):
        second_copy(0, 0, d, y, x, at_x((x + d) % 4)).start()
        second_copy(1, 0, d, y, x, at_y((y + d) % 4)).start()

    idle()
    acc[...] = jnp.zeros_like(acc)
    squares[...] = jnp.zeros_like(squares)

    def use(h, yy, xx):
        upper, right = xx // 2, xx % 2
        first = pl.multiple_of((yy * 2 + right) * CH + h * 512, 512)
        v = held[h, yy, xx].astype(F32)
        squares[upper] += jnp.sum(v * v, axis=1, keepdims=True)
        scaled = (v * closing_ref[:, pl.ds(first, 512)]).astype(BF16)
        acc[upper] += dot(scaled, lexicon_ref[pl.ds(first, 512), :])

    def own_pieces(h, carry):
        use(h, y, x)
        return carry

    lax.fori_loop(0, 2, own_pieces, 0)
    for d in (1, 3, 2):
        yy, xx = (y - d + 4) % 4, (x - d + 4) % 4
        first_copy(0, d, yy, x, at_y(y)).wait_recv()
        first_copy(1, d, y, xx, at_x(x)).wait_recv()
        for e in (1, 3, 2):
            second_copy(0, d, e, yy, x, at_x((x + e) % 4)).start()
            second_copy(1, d, e, y, xx, at_y((y + e) % 4)).start()
    for d in (1, 3, 2):
        use(0, (y - d + 4) % 4, x)
        use(1, y, (x - d + 4) % 4)
    def last_pieces(k, carry):
        for e in (1, 3, 2):
            yy, xx = (y - k + 4) % 4, (x - e + 4) % 4
            second_copy(0, k, e, yy, xx, at_x(x)).wait_recv()
            use(0, yy, xx)
            yy, xx = (y - e + 4) % 4, (x - k + 4) % 4
            second_copy(1, k, e, yy, xx, at_y(y)).wait_recv()
            use(1, yy, xx)
        return carry

    lax.fori_loop(0, 4, last_pieces, 0)

    inv = lax.rsqrt(squares[...] / WIDTH + EPS).reshape(TOK, 1)
    scores = acc[...].reshape(TOK, TOK) * inv / div_ref[0, 0]
    top = jnp.max(scores, axis=1, keepdims=True)
    mass = jnp.sum(jnp.exp(scores - top), axis=1, keepdims=True)
    chan_stats[ch, 0] = jnp.transpose(jnp.broadcast_to(top, (TOK, 128)))[0:8, :]
    chan_stats[ch, 1] = jnp.transpose(jnp.broadcast_to(mass, (TOK, 128)))[0:8, :]

    def chan_copy(d, source, there):
        ref = chan_stats.at[source]
        return remote(ref, ref, c_send.at[d], c_recv.at[d], {"chan": there})

    def send_c(d, carry):
        chan_copy(d, ch, lax.rem(ch + d, CHAN)).start()
        return carry

    lax.fori_loop(1, CHAN, send_c, 0)

    def wait_c(d, carry):
        chan_copy(d, lax.rem(ch - d + CHAN, CHAN), ch).wait_recv()
        return carry

    lax.fori_loop(1, CHAN, wait_c, 0)

    def join(ref):
        tops = ref[:, 0]
        top = jnp.max(tops, axis=0)
        return top, jnp.sum(ref[:, 1] * jnp.exp(tops - top[None]), axis=0)

    seq_stats[me, 0], seq_stats[me, 1] = join(chan_stats)

    def seq_copy(d, source, there):
        ref = seq_stats.at[source]
        return remote(ref, ref, s_send.at[d], s_recv.at[d], {"seq": there})

    def send_s(d, carry):
        seq_copy(d, me, lax.rem(me + d, SEQ)).start()
        return carry

    lax.fori_loop(1, SEQ, send_s, 0)

    def wait_sends(d, carry):
        z_copy(d, z, z).wait_send()
        chan_copy(d, ch, ch).wait_send()
        return carry

    lax.fori_loop(1, NZ, wait_sends, 0)

    def wait_a_sends(d, carry):
        for h in range(2):
            first_copy(h, d, y, x, at_y(y)).wait_send()
            for k in range(4):
                second_copy(h, k, d, y, x, at_y(y)).wait_send()
        return carry

    lax.fori_loop(1, 4, wait_a_sends, 0)

    def wait_s(d, carry):
        seq_copy(d, lax.rem(me - d + SEQ, SEQ), me).wait_recv()
        return carry

    lax.fori_loop(1, SEQ, wait_s, 0)
    top, mass = join(seq_stats)
    norm = top + jnp.log(mass)
    column = jnp.transpose(jnp.broadcast_to(norm[0:1, :], (128, TOK)))[:, 0:1]
    prob_ref[...] = scores - column

    def wait_s_sends(d, carry):
        seq_copy(d, me, me).wait_send()
        return carry

    lax.fori_loop(1, SEQ, wait_s_sends, 0)


def whole_kernel(
    x_ref, b_ref, c_ref, la_ref, skip_ref, choice_ref, share_ref,
    rescale_ref, switch_hbm, widen_hbm, contract_hbm,
    pick_ref, closing_ref, lexicon_hbm, div_ref,
    layer_ref, prob_ref,
    mamba, gmap, expert, switch, widen, contract, lexicon, rows, load_sem,
    *scratch,
):
    barrier = pltpu.get_barrier_semaphore()
    me = lax.axis_index("seq")
    ch = lax.axis_index("chan")
    greet("seq", SEQ, me)
    greet("chan", CHAN, ch)
    xh, z = me // NZ, me % NZ
    y, xl = ch // 2, ch % 2
    diagonal = {"seq": (1 - xh) * NZ + z, "chan": y * 2 + 1 - xl}
    pl.semaphore_signal(barrier, inc=1, device_id=diagonal, device_id_type=MESH)
    loads = [
        pltpu.make_async_copy(src, dst, load_sem.at[k])
        for k, (src, dst) in enumerate(
            ((switch_hbm, switch), (widen_hbm, widen), (contract_hbm, contract), (lexicon_hbm, lexicon))
        )
    ]
    for load in loads:
        load.start()
    drain = scan_part(
        x_ref, b_ref, c_ref, la_ref, skip_ref, choice_ref, share_ref,
        mamba, rows, gmap, *scratch[:13],
    )
    first = drain

    def idle():
        first()
        for load in loads:
            load.wait()

    drain = expert_part(idle, rescale_ref, switch, widen, contract, expert, rows, *scratch[13 : 13 + 33])
    head_part(
        drain, mamba, gmap, expert, pick_ref, closing_ref, lexicon, div_ref, layer_ref, prob_ref, *scratch[46:]
    )


def whole_call(*args):
    vm = pl.BlockSpec(memory_space=pltpu.VMEM)
    hbm = pl.BlockSpec(memory_space=pl.ANY)
    dma = pltpu.SemaphoreType.DMA
    in_specs = [vm] * 8 + [hbm] * 3 + [vm] * 2 + [hbm, pl.BlockSpec(memory_space=pltpu.SMEM)]
    return pl.pallas_call(
        whole_kernel,
        out_shape=(
            jax.ShapeDtypeStruct((TOK, CH), BF16),
            jax.ShapeDtypeStruct((TOK, TOK), F32),
        ),
        in_specs=in_specs,
        out_specs=(vm, vm),
        scratch_shapes=[
            pltpu.VMEM((TOK, CH), BF16),
            pltpu.VMEM((TOK, 128), BF16),
            pltpu.VMEM((CAP, CH), F32),
            pltpu.VMEM((CH, HIDL), BF16),
            pltpu.VMEM((CH, HIDL), BF16),
            pltpu.VMEM((HIDL, CH), BF16),
            pltpu.VMEM((WIDTH, TOK), BF16),
            pltpu.VMEM((SEQ, CAP, CH), BF16),
            dma((4,)),
            pltpu.VMEM((128, TOK), F32),
            pltpu.VMEM((128, CH), BF16),
            pltpu.VMEM((SEQ, 16, 512), BF16),
            pltpu.VMEM((SEQ, 8, 128), F32),
            pltpu.VMEM((SEQ, 16, 512), BF16),
            pltpu.VMEM((128, CH), BF16),
            pltpu.VMEM((TOK, CH), F32),
            *[dma((SEQ,))] * 6,
            pltpu.VMEM((NZ, 2, 64, HIDL + 128), BF16),
            pltpu.VMEM((NZ, 2, 64, HIDL), BF16),
            pltpu.VMEM((NZ, 64, HIDL + 128), BF16),
            pltpu.VMEM((NZ, 4, 2, 16, HIDL), BF16),
            pltpu.VMEM((NZ, 2, 16, HIDL), BF16),
            pltpu.VMEM((NZ, 4, 16, HIDL + 128), BF16),
            pltpu.VMEM((NZ, 16, HIDL), BF16),
            pltpu.VMEM((NZ, 2, 64, HIDL), BF16),
            pltpu.VMEM((NZ, CAP, CH), BF16),
            pltpu.VMEM((NZ, CAP, CH), BF16),
            pltpu.VMEM((NZ, CAP, CH), F32),
            pltpu.VMEM((NZ, CAP, CH), BF16),
            pltpu.VMEM((NZ, CAP, CH), BF16),
            dma((2, 5, 2)), dma((2, 5, 2)), dma, dma,
            dma((NZ,)), dma((NZ,)), dma((NZ, 4)), dma((NZ, 4)),
            dma((NZ, 4)), dma((NZ, 4)), dma((NZ,)), dma((NZ,)),
            dma((NZ,)), dma((NZ,)), dma((NZ, 2, 4)), dma((NZ, 2, 4)),
            dma((NZ,)), dma((NZ,)), dma((NZ,)), dma((NZ,)),
            pltpu.VMEM((2, 4, 4, 128, 512), BF16),
            pltpu.VMEM((2, 128, TOK), F32),
            pltpu.VMEM((2, 128, 1), F32),
            pltpu.VMEM((CHAN, 2, 8, TOK), F32),
            pltpu.VMEM((SEQ, 2, 8, TOK), F32),
            dma((NZ,)), dma((NZ,)),
            dma((2, 4)), dma((2, 4)),
            dma((2, 4, 4)), dma((2, 4, 4)),
            dma((CHAN,)), dma((CHAN,)),
            dma((SEQ,)), dma((SEQ,)),
        ],
        compiler_params=pltpu.CompilerParams(
            collective_id=0, has_side_effects=True, vmem_limit_bytes=VMEM_LIMIT
        ),
        name="whole",
    )(*args)


def shards(
    recurrence_feed,
    memory_write_matrix,
    memory_read_matrix,
    log_shrink_table,
    skip_connection_scale,
    specialist_choices,
    specialist_mixing_shares,
    specialist_rescale_vector,
    specialist_switch_matrix,
    specialist_widen_matrix,
    specialist_contract_matrix,
    closing_rescale_vector,
    lexicon_matrix,
    softness_divisor,
    picked_entry_offsets,
):
    return whole_call(
        recurrence_feed,
        memory_write_matrix,
        memory_read_matrix,
        log_shrink_table.T,
        skip_connection_scale.reshape(1, -1),
        specialist_choices.T,
        specialist_mixing_shares.T,
        specialist_rescale_vector.reshape(1, -1),
        specialist_switch_matrix,
        specialist_widen_matrix,
        specialist_contract_matrix,
        picked_entry_offsets.reshape(1, -1),
        closing_rescale_vector.reshape(1, -1),
        lexicon_matrix,
        softness_divisor.reshape(1, 1),
    )


def solution(mesh):
    in_specs = (
        P(("dp", "seq"), "chan"),
        P(("dp", "seq"), None),
        P(("dp", "seq"), None),
        P(("dp", "seq"), "chan"),
        P("chan"),
        P(("dp", "seq"), None),
        P(("dp", "seq"), None),
        P("chan"),
        P("chan", "seq"),
        P("chan", "seq"),
        P("seq", "chan"),
        P(),
        P(None, ("seq", "chan")),
        P(),
        P(("dp", "seq")),
    )
    out_specs = (P(("dp", "seq"), "chan"), P("dp", ("seq", "chan")))
    return jax.shard_map(shards, mesh=mesh, in_specs=in_specs, out_specs=out_specs, check_vma=False)
```

```python
import jax
import jax.numpy as jnp
from jax import lax
from jax.experimental import pallas as pl
from jax.experimental.pallas import tpu as pltpu
from jax.sharding import PartitionSpec as P

MESH = pl.DeviceIdType.MESH
F32 = jnp.float32
BF16 = jnp.bfloat16
TOK = 256
CH = 1024
SEQ = 16
CHAN = 8
NZ = 8
CAP = 64
HIDL = 768
WIDTH = 8192
EPS = 1e-5
VMEM_LIMIT = 56 * 1024 * 1024


def dot(a, b):
    return jnp.dot(a, b, preferred_element_type=F32)


def split2(v):
    hi = v.astype(BF16)
    return hi, (v - hi.astype(F32)).astype(BF16)


def split3(v):
    hi = v.astype(BF16)
    rest = v - hi.astype(F32)
    mid = rest.astype(BF16)
    return hi, mid, (rest - mid.astype(F32)).astype(BF16)


def iota(shape, dim):
    return lax.broadcasted_iota(jnp.int32, shape, dim)


def remote(src, dst, send_sem, recv_sem, where):
    return pltpu.make_async_remote_copy(
        src_ref=src,
        dst_ref=dst,
        send_sem=send_sem,
        recv_sem=recv_sem,
        device_id=where,
        device_id_type=MESH,
    )


def greet(axis, size, me):
    barrier = pltpu.get_barrier_semaphore()

    def one(d, carry):
        pl.semaphore_signal(
            barrier, inc=1, device_id={axis: lax.rem(me + d, size)}, device_id_type=MESH
        )
        return carry

    lax.fori_loop(1, size, one, 0)


def scan_part(
    x_ref, b_ref, c_ref, la_ref, skip_ref, choice_ref, share_ref,
    mamba_ref, rows, gmap_ref,
    wide, local, taken, decays, prefixes, entry, y_ref,
    dec_send, dec_recv, a_send, a_recv, p_send, p_recv,
):
    me = lax.axis_index("seq")

    wide[...] = jnp.zeros_like(wide)
    wide[0:16, :] = la_ref[...]
    tril = (iota((TOK, TOK), 0) >= iota((TOK, TOK), 1)).astype(F32)
    triu_bf = (iota((TOK, TOK), 0) <= iota((TOK, TOK), 1)).astype(F32).astype(BF16)
    hi, mid, lo = split3(wide[...])
    cum_t = dot(hi, triu_bf) + dot(mid, triu_bf) + dot(lo, triu_bf)
    cum = jnp.transpose(cum_t)
    last = cum[TOK - 1 : TOK, :]
    spread_map = (iota((128, CH), 1) // 64 == iota((128, CH), 0)).astype(F32).astype(BF16)

    def expand(v):
        hi, lo = split2(v)
        return dot(hi, spread_map) + dot(lo, spread_map)

    decays[me] = jnp.broadcast_to(jnp.exp(last), (8, 128))
    pl.semaphore_wait(pltpu.get_barrier_semaphore(), 15 + 7 + 1)

    def dec_copy(d, there):
        return remote(
            decays.at[me], decays.at[me], dec_send.at[d], dec_recv.at[d], {"seq": there}
        )

    def send_dec(d, carry):
        dec_copy(d, lax.rem(me + d, SEQ)).start()
        return carry

    lax.fori_loop(1, SEQ, send_dec, 0)

    weighted = (x_ref[...].astype(F32) * expand(jnp.exp(last - cum))).astype(BF16)
    b_t = jnp.transpose(b_ref[...].astype(F32)).astype(BF16)
    local[...] = dot(b_t, weighted).astype(BF16)

    def part(ref, p):
        return ref.at[
            pl.ds(pl.multiple_of((p // 2) * 16, 16), 16),
            pl.ds(pl.multiple_of((p % 2) * 512, 512), 512),
        ]

    def a_copy(d, there):
        return remote(part(local, there), taken.at[me], a_send.at[d], a_recv.at[d], {"seq": there})

    def send_a(d, carry):
        a_copy(d, lax.rem(me + d, SEQ)).start()
        return carry

    lax.fori_loop(1, SEQ, send_a, 0)
    taken[me] = part(local, me)[...]

    scores = lax.dot_general(
        c_ref[...], b_ref[...], (((1,), (1,)), ((), ())), preferred_element_type=F32
    )
    scores = scores * tril
    lane = iota((128, 128), 1)

    def heads(pairs):
        for q in pairs:
            cols = slice(128 * q, 128 * q + 128)
            xq = x_ref[:, cols]
            for r in range(2):
                rows = slice(128 * r, 128 * r + 128)
                width = 128 * (r + 1)
                out = []
                for h in (2 * q, 2 * q + 1):
                    decay = jnp.exp(
                        jnp.minimum(cum[rows, h : h + 1] - cum_t[h : h + 1, 0:width], 0.0)
                    )
                    mixing = (scores[rows, 0:width] * decay).astype(BF16)
                    out.append(dot(mixing, xq[0:width, :]))
                y_ref[rows, cols] = jnp.where(lane < 64, out[0], out[1])

    heads(range(0, 4))

    def wait_dec(d, carry):
        dec_copy(d, me).wait_recv()
        a_copy(d, me).wait_recv()
        return carry

    lax.fori_loop(1, SEQ, wait_dec, 0)
    half = lax.rem(me, 2)
    half_map = (
        ((iota((128, 512), 1) + half * 512) // 64 == iota((128, 512), 0)).astype(F32).astype(BF16)
    )
    hi, mid, lo = split3(decays[...].reshape(SEQ * 8, 128))
    factors = dot(hi, half_map) + dot(mid, half_map) + dot(lo, half_map)
    state = jnp.zeros((16, 512), F32)
    for s in range(SEQ):
        prefixes[s] = state.astype(BF16)
        state = factors[8 * s : 8 * s + 1, :] * state + taken[s].astype(F32)

    def p_copy(d, there):
        return remote(prefixes.at[there], part(entry, me), p_send.at[d], p_recv.at[d], {"seq": there})

    def send_p(d, carry):
        p_copy(d, lax.rem(me + d, SEQ)).start()
        return carry

    lax.fori_loop(1, SEQ, send_p, 0)
    part(entry, me)[...] = prefixes[me]

    heads(range(4, 8))

    first, second = choice_ref[0:1, :] == 0, choice_ref[1:2, :] == 0
    used = jnp.where(first, 1.0, 0.0) + jnp.where(second, 1.0, 0.0)
    gate = jnp.where(first, share_ref[0:1, :].astype(F32), 0.0) + jnp.where(
        second, share_ref[1:2, :].astype(F32), 0.0
    )
    used = jnp.broadcast_to(used, (128, TOK))
    place = dot(used.astype(BF16), triu_bf) - 1.0
    slot_map = jnp.where(place == iota((128, TOK), 0).astype(F32), used, 0.0)
    gmap_ref[...] = jnp.transpose(slot_map * gate).astype(BF16)
    slot_t = slot_map[0:CAP, :].astype(BF16)

    skip = jnp.concatenate([skip_ref[...], jnp.zeros((1, 112), F32)], axis=1)
    skip_wide = expand(jnp.broadcast_to(skip, (8, 128)))[0:1, :]
    decay_in = jnp.exp(cum)
    cum_wide = expand(decay_in)
    y_ref[...] += skip_wide * x_ref[...].astype(F32)

    def routed(v):
        hi, mid, lo = split3(v)
        return dot(slot_t, hi) + dot(slot_t, mid) + dot(slot_t, lo)

    slot_before = routed(y_ref[...])
    slot_cum = expand(routed(decay_in))
    slot_c = dot(slot_t, c_ref[...]).astype(BF16)

    def wait_p(d, carry):
        there = lax.rem(me - d + SEQ, SEQ)
        remote(
            prefixes.at[me], part(entry, there), p_send.at[d], p_recv.at[d], {"seq": there}
        ).wait_recv()
        return carry

    lax.fori_loop(1, SEQ, wait_p, 0)
    rows[me] = (slot_before + slot_cum * dot(slot_c, entry[...])).astype(BF16)

    def finish():
        outer = dot(c_ref[...], entry[...])
        mamba_ref[...] = (y_ref[...] + cum_wide * outer).astype(BF16)

    def drain():
        def wait_sends(d, carry):
            dec_copy(d, me).wait_send()
            a_copy(d, me).wait_send()
            p_copy(d, me).wait_send()
            return carry

        lax.fori_loop(1, SEQ, wait_sends, 0)

    return drain, finish


def near_first(i):
    odd = i % 2
    return odd * ((i + 1) // 2) + (1 - odd) * ((NZ - i // 2) % NZ)


def expert_part(
    finish, idle, rescale_ref, switch_ref, widen_ref, contract_ref,
    out_ref,
    rows, pg, pu, g1, u1, us, g2, u2, hidden, x_out, x_in, kept, z_out, z_in,
    ag_send, ag_recv, fw_send, fw_recv,
    g1_send, g1_recv, u1_send, u1_recv, g2_send, g2_recv, u2_send, u2_recv,
    hx_send, hx_recv, hy_send, hy_recv,
    xs_send, xs_recv, zs_send, zs_recv,
):
    me = lax.axis_index("seq")
    ch = lax.axis_index("chan")
    xh, z = me // NZ, me % NZ
    y, xl = ch // 2, ch % 2
    other = {"seq": (1 - xh) * NZ + z}
    beside = {"chan": y * 2 + 1 - xl}

    def at_z(there):
        return {"seq": xh * NZ + there % NZ}

    def at_y(there):
        return {"chan": (there % 4) * 2 + xl}

    def order(i):
        return (z - near_first(i) + NZ) % NZ

    def sixteen(start):
        return pl.ds(pl.multiple_of(start, 16), 16)

    fw = remote(rows.at[me], rows.at[me], fw_send, fw_recv, other)

    def ag_copy(way, k, half, block):
        row = half * NZ + block % NZ
        ref = rows.at[row]
        there = at_z(z + 1 if way == 0 else z + NZ - 1)
        return remote(ref, ref, ag_send.at[way, k, half], ag_recv.at[way, k, half], there)

    def ag_last(way, half, block):
        ref = rows.at[half * NZ + block % NZ, pl.ds(32 * way, 32)]
        there = at_z(z + 1 if way == 0 else z + NZ - 1)
        return remote(ref, ref, ag_send.at[way, 4, half], ag_recv.at[way, 4, half], there)

    def behind(way, k):
        return z - k + NZ if way == 0 else z + k

    fw.start()
    for way in range(2):
        ag_copy(way, 1, xh, z).start()
    finish()

    def gather(i):
        @pl.when(i == 0)
        def _():
            remote(rows.at[(1 - xh) * NZ + z], rows.at[(1 - xh) * NZ + z], fw_send, fw_recv, other).wait_recv()
            for way in range(2):
                ag_copy(way, 1, 1 - xh, z).start()
            idle()

        @pl.when((i % 2 == 1) & (i < NZ - 1))
        def _():
            k = (i + 1) // 2
            for j in range(2):
                half = xh + j - 2 * j * xh
                for way in range(2):
                    ag_copy(way, k, half, behind(way, k)).wait_recv()

                    @pl.when(k < 3)
                    def _():
                        ag_copy(way, k + 1, half, behind(way, k)).start()

                    @pl.when(k == 3)
                    def _():
                        ag_last(way, half, behind(way, k)).start()

        @pl.when(i == NZ - 1)
        def _():
            for way in range(2):
                for half in range(2):
                    ag_last(way, half, z + 4).wait_recv()

    def g1_copy(b):
        return remote(pg.at[b, 1 - xl], g1.at[b], g1_send.at[b], g1_recv.at[b], beside)

    def u1_copy(b, d, there, source):
        return remote(
            pu.at[b, :, sixteen(there * 16)], u1.at[b, source], u1_send.at[b, d], u1_recv.at[b, d], at_y(there)
        )

    def g2_copy(b, d, there, source):
        return remote(
            pg.at[b, xl, sixteen(there * 16)], g2.at[b, source], g2_send.at[b, d], g2_recv.at[b, d], at_y(there)
        )

    def u2_copy(b):
        return remote(us.at[b, 1 - xl], u2.at[b], u2_send.at[b], u2_recv.at[b], beside)

    lane = iota((128, 128), 1)

    def project(i):
        gather(i)
        b = order(i)
        v = jnp.concatenate([rows[b], rows[NZ + b]], axis=0).astype(F32)
        squares = jnp.sum(v * v, axis=1, keepdims=True)
        scaled = (v * rescale_ref[...]).astype(BF16)
        hi, mid, lo = split3(squares)
        extra = jnp.where(
            lane == 0,
            hi.astype(F32),
            jnp.where(lane == 1, mid.astype(F32), jnp.where(lane == 2, lo.astype(F32), 0.0)),
        ).astype(BF16)
        pg[b, :, :, HIDL:] = extra.reshape(2, 64, 128)
        pg[b, :, :, 0:HIDL] = dot(scaled, switch_ref[...]).astype(BF16).reshape(2, 64, HIDL)
        g1_copy(b).start()
        pu[b] = dot(scaled, widen_ref[...]).astype(BF16).reshape(2, 64, HIDL)
        for d in (1, 3, 2):
            u1_copy(b, d, (y + d) % 4, y).start()

    def fold(i):
        b = order(i)
        g1_copy(b).wait_recv()
        pg[b, xl] = (pg[b, xl].astype(F32) + g1[b].astype(F32)).astype(BF16)
        for d in (1, 3, 2):
            g2_copy(b, d, (y + d) % 4, y).start()
        total = pu[b, :, sixteen(y * 16), :].astype(F32)
        for d in (1, 3, 2):
            source = (y - d + 4) % 4
            u1_copy(b, d, y, source).wait_recv()
            total = total + u1[b, source].astype(F32)
        us[b] = total.astype(BF16)
        u2_copy(b).start()

    def hx_copy(b, owner):
        ref = hidden.at[b, owner, sixteen(y * 16)]
        return remote(ref, ref, hx_send.at[b], hx_recv.at[b], beside)

    def hy_copy(b, owner, d, source, there):
        ref = hidden.at[b, owner, sixteen(source * 16)]
        return remote(ref, ref, hy_send.at[b, owner, d], hy_recv.at[b, owner, d], at_y(there))

    def activate(i):
        b = order(i)
        gate = pg[b, xl, sixteen(y * 16), :].astype(F32)
        for d in (1, 3, 2):
            source = (y - d + 4) % 4
            g2_copy(b, d, y, source).wait_recv()
            gate = gate + g2[b, source].astype(F32)
        u2_copy(b).wait_recv()
        up = us[b, xl].astype(F32) + u2[b].astype(F32)
        squares = jnp.sum(gate[:, HIDL:], axis=1, keepdims=True)
        inv = lax.rsqrt(squares / WIDTH + EPS)
        gate = gate[:, 0:HIDL] * inv
        hidden[b, xl, sixteen(y * 16), :] = (gate / (1.0 + jnp.exp(-gate)) * (up * inv)).astype(BF16)
        hx_copy(b, xl).start()
        for d in (1, 3, 2):
            hy_copy(b, xl, d, y, y + d).start()

    def relay(i):
        b = order(i)
        hx_copy(b, 1 - xl).wait_recv()
        for d in (1, 3, 2):
            hy_copy(b, 1 - xl, d, y, y + d).start()

    def xs_copy(b):
        return remote(x_out.at[b], x_in.at[b], xs_send.at[b], xs_recv.at[b], other)

    def contract(i):
        b = order(i)
        for half in range(2):
            for d in (1, 3, 2):
                hy_copy(b, half, d, (y - d + 4) % 4, y).wait_recv()
        x_out[b] = dot(hidden[b, 1 - xh], contract_ref[...]).astype(BF16)
        xs_copy(b).start()
        kept[b] = dot(hidden[b, xh], contract_ref[...])

    def zs_copy(i, b, source):
        return remote(z_out.at[b], z_in.at[source], zs_send.at[i], zs_recv.at[i], at_z(b))

    def pass_on(i):
        b = order(i)
        xs_copy(b).wait_recv()
        z_out[b] = (kept[b] + x_in[b].astype(F32)).astype(BF16)

        @pl.when(i > 0)
        def _():
            zs_copy(i, b, z).start()

    stages = ((project, 0), (fold, 1), (activate, 2), (relay, 3), (contract, 4), (pass_on, 5))

    def step(i, carry):
        for stage, off in stages:

            @pl.when((i >= off) & (i < off + NZ))
            def _():
                stage(i - off)

        return carry

    lax.fori_loop(0, NZ + stages[-1][1], step, 0)
    out_ref[...] = kept[z] + x_in[z].astype(F32)

    def collect(i, carry):
        source = (z + near_first(i)) % NZ
        zs_copy(i, z, source).wait_recv()
        out_ref[...] += z_in[source].astype(F32)
        return carry

    lax.fori_loop(1, NZ, collect, 0)

    def drain():
        def wait_sends(b, carry):
            g1_copy(b).wait_send()
            u2_copy(b).wait_send()
            hx_copy(b, xl).wait_send()
            xs_copy(b).wait_send()
            for d in range(1, 4):
                u1_copy(b, d, y, y).wait_send()
                g2_copy(b, d, y, y).wait_send()
                for half in range(2):
                    hy_copy(b, half, d, y, y).wait_send()
            return carry

        lax.fori_loop(0, NZ, wait_sends, 0)

        def wait_z_sends(i, carry):
            zs_copy(i, z, z).wait_send()
            return carry

        lax.fori_loop(1, NZ, wait_z_sends, 0)
        fw.wait_send()
        for way in range(2):
            for half in range(2):
                ag_last(way, half, z).wait_send()
                for k in range(1, 4):
                    ag_copy(way, k, half, z).wait_send()

    return drain


def head_part(
    idle, mamba_ref, gmap_ref, expert_ref, pick_ref, closing_ref, lexicon_ref, div_ref,
    layer_ref, prob_ref,
    held, acc, ordered, squares, chan_stats, seq_stats,
    z_send, z_recv, r_send, r_recv, c_send, c_recv, s_send, s_recv,
):
    me = lax.axis_index("seq")
    ch = lax.axis_index("chan")
    xh, z = me // NZ, me % NZ
    y, xl = ch // 2, ch % 2
    x = xh * 2 + xl
    hi, lo = split2(expert_ref[...])
    gmap = gmap_ref[:, 0:CAP]
    layer = (mamba_ref[...].astype(F32) + dot(gmap, hi) + dot(gmap, lo)).astype(BF16)
    layer_ref[...] = layer
    offsets = jnp.concatenate(
        [pick_ref[...].astype(F32), jnp.full((1, 112), -1.0, F32)], axis=1
    )
    offsets = jnp.transpose(jnp.broadcast_to(offsets, (128, 128)))[0:16, 0:1]
    pick = (iota((16, TOK), 1).astype(F32) == offsets).astype(F32).astype(BF16)
    picked = dot(pick, layer).astype(BF16)
    held[0, y, x, 0:16, :] = picked[:, 0:512]
    held[1, y, x, 0:16, :] = picked[:, 512:1024]

    def at_x(there):
        there = there % 4
        return {"seq": (there // 2) * NZ + z, "chan": y * 2 + there % 2}

    def at_y(there):
        return {"chan": (there % 4) * 2 + xl}

    def z_copy(r):
        return remote(
            held.at[:, y, x, pl.ds(0, 16), :],
            held.at[:, y, x, pl.ds(16 * r, 16), :],
            z_send.at[r],
            z_recv.at[r],
            {"seq": xh * NZ + (z + near_first(r)) % NZ},
        )

    for r in range(1, NZ):
        z_copy(r).start()

    def piece(h, stage, e, g, kind):
        k, e = (e, 0) if stage == 0 else (stage - 1, e)
        yy, xx = (k, e) if h == 0 else (e, k)
        rows = (pl.ds(64 * g, 64), pl.ds(64 * g, 64), pl.ds(64 * g, 32), pl.ds(64 * g + 32, 32))[kind]
        return held.at[h, (y - yy + 4) % 4, (x - xx + 4) % 4, rows]

    def ring(h, stage, g, kind, source):
        ref = piece(h, stage, source, g, kind)
        move = 1 if kind % 2 == 0 else 3
        there = at_y(y + move) if (h == 0) == (stage == 0) else at_x(x + move)
        return remote(ref, ref, r_send.at[h, stage, g, kind], r_recv.at[h, stage, g, kind], there)

    def start(stage, g):
        for h in range(2):
            for kind in range(2):
                ring(h, stage, g, kind, 0).start()

    def arrive(stage, g):
        for kind in range(2):
            for h in range(2):
                ring(h, stage, g, kind, (1, 3)[kind]).wait_recv()
                ring(h, stage, g, kind + 2, (1, 3)[kind]).start()

    def arrive_far(stage, g):
        for h in range(2):
            for kind in (2, 3):
                ring(h, stage, g, kind, 2).wait_recv()

    acc[...] = jnp.zeros_like(acc)
    squares[...] = jnp.zeros_like(squares)

    def use(stage, e):
        for h in range(2):
            k, ee = (e, 0) if stage == 0 else (stage - 1, e)
            yy, xx = (k, ee) if h == 0 else (ee, k)
            yy, xx = (y - yy + 4) % 4, (x - xx + 4) % 4
            upper, right = xx // 2, xx % 2
            first = pl.multiple_of((yy * 2 + right) * CH + h * 512, 512)
            v = held[h, yy, xx].astype(F32)
            squares[upper] += jnp.sum(v * v, axis=1, keepdims=True)
            scaled = (v * closing_ref[:, pl.ds(first, 512)]).astype(BF16)
            acc[upper] += dot(scaled, lexicon_ref[pl.ds(first, 512), :])

    for r in range(1, 4):
        z_copy(r).wait_recv()
    start(0, 0)
    start(1, 0)
    for r in range(4, NZ):
        z_copy(r).wait_recv()
    start(0, 1)
    start(1, 1)
    use(0, 0)
    idle()
    for g in range(2):
        arrive(0, g)
        for k in (1, 3):
            start(1 + k, g)
        arrive(1, g)
    for g in range(2):
        arrive_far(0, g)
        start(3, g)
    for e in (1, 3, 2):
        use(0, e)
    for e in (1, 3):
        use(1, e)
    for g in range(2):
        for k in (1, 3):
            arrive(1 + k, g)
    for g in range(2):
        arrive_far(1, g)
    use(1, 2)
    for k in (1, 3):
        for e in (1, 3):
            use(1 + k, e)
    for g in range(2):
        arrive(3, g)
    for k in (1, 3):
        for g in range(2):
            arrive_far(1 + k, g)
        use(1 + k, 2)
    for e in (1, 3):
        use(3, e)
    for g in range(2):
        arrive_far(3, g)
    use(3, 2)

    inv = lax.rsqrt(squares[...] / WIDTH + EPS)
    for r in range(NZ):
        rows = pl.ds(pl.multiple_of(((z - near_first(r) + NZ) % NZ) * 16, 16), 16)
        part = slice(16 * r, 16 * r + 16)
        ordered[:, rows, :] = acc[:, part, :] * inv[:, part, :]
    scores = ordered[...].reshape(TOK, TOK) / div_ref[0, 0]
    top = jnp.max(scores, axis=1, keepdims=True)
    mass = jnp.sum(jnp.exp(scores - top), axis=1, keepdims=True)
    chan_stats[ch, 0] = jnp.transpose(jnp.broadcast_to(top, (TOK, 128)))[0:8, :]
    chan_stats[ch, 1] = jnp.transpose(jnp.broadcast_to(mass, (TOK, 128)))[0:8, :]

    def chan_copy(d, source, there):
        ref = chan_stats.at[source]
        return remote(ref, ref, c_send.at[d], c_recv.at[d], {"chan": there})

    def send_c(d, carry):
        chan_copy(d, ch, lax.rem(ch + d, CHAN)).start()
        return carry

    lax.fori_loop(1, CHAN, send_c, 0)

    def wait_c(d, carry):
        chan_copy(d, lax.rem(ch - d + CHAN, CHAN), ch).wait_recv()
        return carry

    lax.fori_loop(1, CHAN, wait_c, 0)

    def join(ref):
        tops = ref[:, 0]
        top = jnp.max(tops, axis=0)
        return top, jnp.sum(ref[:, 1] * jnp.exp(tops - top[None]), axis=0)

    seq_stats[me, 0], seq_stats[me, 1] = join(chan_stats)

    def seq_copy(d, source, there):
        ref = seq_stats.at[source]
        return remote(ref, ref, s_send.at[d], s_recv.at[d], {"seq": there})

    def send_s(d, carry):
        seq_copy(d, me, lax.rem(me + d, SEQ)).start()
        return carry

    lax.fori_loop(1, SEQ, send_s, 0)

    def wait_sends(d, carry):
        z_copy(d).wait_send()
        chan_copy(d, ch, ch).wait_send()
        return carry

    lax.fori_loop(1, NZ, wait_sends, 0)
    for stage in range(5):
        for g in range(2):
            for h in range(2):
                for kind in range(4):
                    ring(h, stage, g, kind, 0).wait_send()

    def wait_s(d, carry):
        seq_copy(d, lax.rem(me - d + SEQ, SEQ), me).wait_recv()
        return carry

    lax.fori_loop(1, SEQ, wait_s, 0)
    top, mass = join(seq_stats)
    norm = top + jnp.log(mass)
    column = jnp.transpose(jnp.broadcast_to(norm[0:1, :], (128, TOK)))[:, 0:1]
    prob_ref[...] = scores - column

    def wait_s_sends(d, carry):
        seq_copy(d, me, me).wait_send()
        return carry

    lax.fori_loop(1, SEQ, wait_s_sends, 0)


def whole_kernel(
    x_ref, b_ref, c_ref, la_ref, skip_ref, choice_ref, share_ref,
    rescale_ref, switch_hbm, widen_hbm, contract_hbm,
    pick_ref, closing_ref, lexicon_hbm, div_ref,
    layer_ref, prob_ref,
    mamba, gmap, expert, switch, widen, contract, lexicon, rows, load_sem,
    *scratch,
):
    barrier = pltpu.get_barrier_semaphore()
    me = lax.axis_index("seq")
    ch = lax.axis_index("chan")
    greet("seq", SEQ, me)
    greet("chan", CHAN, ch)
    xh, z = me // NZ, me % NZ
    y, xl = ch // 2, ch % 2
    diagonal = {"seq": (1 - xh) * NZ + z, "chan": y * 2 + 1 - xl}
    pl.semaphore_signal(barrier, inc=1, device_id=diagonal, device_id_type=MESH)
    loads = [
        pltpu.make_async_copy(src, dst, load_sem.at[k])
        for k, (src, dst) in enumerate(
            ((switch_hbm, switch), (widen_hbm, widen), (contract_hbm, contract), (lexicon_hbm, lexicon))
        )
    ]
    for load in loads:
        load.start()
    first, finish = scan_part(
        x_ref, b_ref, c_ref, la_ref, skip_ref, choice_ref, share_ref,
        mamba, rows, gmap, *scratch[:13],
    )
    def idle():
        first()
        for load in loads:
            load.wait()

    drain = expert_part(finish, idle, rescale_ref, switch, widen, contract, expert, rows, *scratch[13 : 13 + 33])
    head_part(
        drain, mamba, gmap, expert, pick_ref, closing_ref, lexicon, div_ref, layer_ref, prob_ref, *scratch[46:]
    )


def whole_call(*args):
    vm = pl.BlockSpec(memory_space=pltpu.VMEM)
    hbm = pl.BlockSpec(memory_space=pl.ANY)
    dma = pltpu.SemaphoreType.DMA
    in_specs = [vm] * 8 + [hbm] * 3 + [vm] * 2 + [hbm, pl.BlockSpec(memory_space=pltpu.SMEM)]
    return pl.pallas_call(
        whole_kernel,
        out_shape=(
            jax.ShapeDtypeStruct((TOK, CH), BF16),
            jax.ShapeDtypeStruct((TOK, TOK), F32),
        ),
        in_specs=in_specs,
        out_specs=(vm, vm),
        scratch_shapes=[
            pltpu.VMEM((TOK, CH), BF16),
            pltpu.VMEM((TOK, 128), BF16),
            pltpu.VMEM((CAP, CH), F32),
            pltpu.VMEM((CH, HIDL), BF16),
            pltpu.VMEM((CH, HIDL), BF16),
            pltpu.VMEM((HIDL, CH), BF16),
            pltpu.VMEM((WIDTH, TOK), BF16),
            pltpu.VMEM((SEQ, CAP, CH), BF16),
            dma((4,)),
            pltpu.VMEM((128, TOK), F32),
            pltpu.VMEM((128, CH), BF16),
            pltpu.VMEM((SEQ, 16, 512), BF16),
            pltpu.VMEM((SEQ, 8, 128), F32),
            pltpu.VMEM((SEQ, 16, 512), BF16),
            pltpu.VMEM((128, CH), BF16),
            pltpu.VMEM((TOK, CH), F32),
            *[dma((SEQ,))] * 6,
            pltpu.VMEM((NZ, 2, 64, HIDL + 128), BF16),
            pltpu.VMEM((NZ, 2, 64, HIDL), BF16),
            pltpu.VMEM((NZ, 64, HIDL + 128), BF16),
            pltpu.VMEM((NZ, 4, 2, 16, HIDL), BF16),
            pltpu.VMEM((NZ, 2, 16, HIDL), BF16),
            pltpu.VMEM((NZ, 4, 16, HIDL + 128), BF16),
            pltpu.VMEM((NZ, 16, HIDL), BF16),
            pltpu.VMEM((NZ, 2, 64, HIDL), BF16),
            pltpu.VMEM((NZ, CAP, CH), BF16),
            pltpu.VMEM((NZ, CAP, CH), BF16),
            pltpu.VMEM((NZ, CAP, CH), F32),
            pltpu.VMEM((NZ, CAP, CH), BF16),
            pltpu.VMEM((NZ, CAP, CH), BF16),
            dma((2, 5, 2)), dma((2, 5, 2)), dma, dma,
            dma((NZ,)), dma((NZ,)), dma((NZ, 4)), dma((NZ, 4)),
            dma((NZ, 4)), dma((NZ, 4)), dma((NZ,)), dma((NZ,)),
            dma((NZ,)), dma((NZ,)), dma((NZ, 2, 4)), dma((NZ, 2, 4)),
            dma((NZ,)), dma((NZ,)), dma((NZ,)), dma((NZ,)),
            pltpu.VMEM((2, 4, 4, 128, 512), BF16),
            pltpu.VMEM((2, 128, TOK), F32),
            pltpu.VMEM((2, 128, TOK), F32),
            pltpu.VMEM((2, 128, 1), F32),
            pltpu.VMEM((CHAN, 2, 8, TOK), F32),
            pltpu.VMEM((SEQ, 2, 8, TOK), F32),
            dma((NZ,)), dma((NZ,)),
            dma((2, 5, 2, 4)), dma((2, 5, 2, 4)),
            dma((CHAN,)), dma((CHAN,)),
            dma((SEQ,)), dma((SEQ,)),
        ],
        compiler_params=pltpu.CompilerParams(
            collective_id=0, has_side_effects=True, vmem_limit_bytes=VMEM_LIMIT
        ),
        name="whole",
    )(*args)


def shards(
    recurrence_feed,
    memory_write_matrix,
    memory_read_matrix,
    log_shrink_table,
    skip_connection_scale,
    specialist_choices,
    specialist_mixing_shares,
    specialist_rescale_vector,
    specialist_switch_matrix,
    specialist_widen_matrix,
    specialist_contract_matrix,
    closing_rescale_vector,
    lexicon_matrix,
    softness_divisor,
    picked_entry_offsets,
):
    return whole_call(
        recurrence_feed,
        memory_write_matrix,
        memory_read_matrix,
        log_shrink_table.T,
        skip_connection_scale.reshape(1, -1),
        specialist_choices.T,
        specialist_mixing_shares.T,
        specialist_rescale_vector.reshape(1, -1),
        specialist_switch_matrix,
        specialist_widen_matrix,
        specialist_contract_matrix,
        picked_entry_offsets.reshape(1, -1),
        closing_rescale_vector.reshape(1, -1),
        lexicon_matrix,
        softness_divisor.reshape(1, 1),
    )


def solution(mesh):
    in_specs = (
        P(("dp", "seq"), "chan"),
        P(("dp", "seq"), None),
        P(("dp", "seq"), None),
        P(("dp", "seq"), "chan"),
        P("chan"),
        P(("dp", "seq"), None),
        P(("dp", "seq"), None),
        P("chan"),
        P("chan", "seq"),
        P("chan", "seq"),
        P("seq", "chan"),
        P(),
        P(None, ("seq", "chan")),
        P(),
        P(("dp", "seq")),
    )
    out_specs = (P(("dp", "seq"), "chan"), P("dp", ("seq", "chan")))
    return jax.shard_map(shards, mesh=mesh, in_specs=in_specs, out_specs=out_specs, check_vma=False)
```

```python
import jax
import jax.numpy as jnp
from jax import lax
from jax.experimental import pallas as pl
from jax.experimental.pallas import tpu as pltpu
from jax.sharding import PartitionSpec as P

MESH = pl.DeviceIdType.MESH
F32 = jnp.float32
BF16 = jnp.bfloat16
TOK = 256
CH = 1024
SEQ = 16
CHAN = 8
NZ = 8
CAP = 64
HIDL = 768
WIDTH = 8192
EPS = 1e-5
VMEM_LIMIT = 56 * 1024 * 1024


def dot(a, b):
    return jnp.dot(a, b, preferred_element_type=F32)


def split2(v):
    hi = v.astype(BF16)
    return hi, (v - hi.astype(F32)).astype(BF16)


def split3(v):
    hi = v.astype(BF16)
    rest = v - hi.astype(F32)
    mid = rest.astype(BF16)
    return hi, mid, (rest - mid.astype(F32)).astype(BF16)


def iota(shape, dim):
    return lax.broadcasted_iota(jnp.int32, shape, dim)


def remote(src, dst, send_sem, recv_sem, where):
    return pltpu.make_async_remote_copy(
        src_ref=src,
        dst_ref=dst,
        send_sem=send_sem,
        recv_sem=recv_sem,
        device_id=where,
        device_id_type=MESH,
    )


def greet(axis, size, me):
    barrier = pltpu.get_barrier_semaphore()

    def one(d, carry):
        pl.semaphore_signal(
            barrier, inc=1, device_id={axis: lax.rem(me + d, size)}, device_id_type=MESH
        )
        return carry

    lax.fori_loop(1, size, one, 0)


def scan_part(
    x_ref, b_ref, c_ref, la_ref, skip_ref, choice_ref, share_ref,
    mamba_ref, rows, gmap_ref,
    wide, local, taken, decays, prefixes, entry, y_ref,
    dec_send, dec_recv, a_send, a_recv, p_send, p_recv,
):
    me = lax.axis_index("seq")

    wide[...] = jnp.zeros_like(wide)
    wide[0:16, :] = la_ref[...]
    tril = (iota((TOK, TOK), 0) >= iota((TOK, TOK), 1)).astype(F32)
    triu_bf = (iota((TOK, TOK), 0) <= iota((TOK, TOK), 1)).astype(F32).astype(BF16)
    hi, mid, lo = split3(wide[...])
    cum_t = dot(hi, triu_bf) + dot(mid, triu_bf) + dot(lo, triu_bf)
    cum = jnp.transpose(cum_t)
    last = cum[TOK - 1 : TOK, :]
    spread_map = (iota((128, CH), 1) // 64 == iota((128, CH), 0)).astype(F32).astype(BF16)

    def expand(v):
        hi, lo = split2(v)
        return dot(hi, spread_map) + dot(lo, spread_map)

    decays[me] = jnp.broadcast_to(jnp.exp(last), (8, 128))
    pl.semaphore_wait(pltpu.get_barrier_semaphore(), 15 + 7 + 1)

    def dec_copy(d, there):
        return remote(
            decays.at[me], decays.at[me], dec_send.at[d], dec_recv.at[d], {"seq": there}
        )

    def send_dec(d, carry):
        dec_copy(d, lax.rem(me + d, SEQ)).start()
        return carry

    lax.fori_loop(1, SEQ, send_dec, 0)

    weighted = (x_ref[...].astype(F32) * expand(jnp.exp(last - cum))).astype(BF16)
    b_t = jnp.transpose(b_ref[...].astype(F32)).astype(BF16)
    local[...] = dot(b_t, weighted).astype(BF16)

    def part(ref, p):
        return ref.at[
            pl.ds(pl.multiple_of((p // 2) * 16, 16), 16),
            pl.ds(pl.multiple_of((p % 2) * 512, 512), 512),
        ]

    def a_copy(d, there):
        return remote(part(local, there), taken.at[me], a_send.at[d], a_recv.at[d], {"seq": there})

    def send_a(d, carry):
        a_copy(d, lax.rem(me + d, SEQ)).start()
        return carry

    lax.fori_loop(1, SEQ, send_a, 0)
    taken[me] = part(local, me)[...]

    scores = lax.dot_general(
        c_ref[...], b_ref[...], (((1,), (1,)), ((), ())), preferred_element_type=F32
    )
    scores = scores * tril
    lane = iota((128, 128), 1)

    def heads(pairs):
        for q in pairs:
            cols = slice(128 * q, 128 * q + 128)
            xq = x_ref[:, cols]
            for r in range(2):
                rows = slice(128 * r, 128 * r + 128)
                width = 128 * (r + 1)
                out = []
                for h in (2 * q, 2 * q + 1):
                    decay = jnp.exp(
                        jnp.minimum(cum[rows, h : h + 1] - cum_t[h : h + 1, 0:width], 0.0)
                    )
                    mixing = (scores[rows, 0:width] * decay).astype(BF16)
                    out.append(dot(mixing, xq[0:width, :]))
                y_ref[rows, cols] = jnp.where(lane < 64, out[0], out[1])

    heads(range(0, 4))

    def wait_dec(d, carry):
        dec_copy(d, me).wait_recv()
        a_copy(d, me).wait_recv()
        return carry

    lax.fori_loop(1, SEQ, wait_dec, 0)
    half = lax.rem(me, 2)
    half_map = (
        ((iota((128, 512), 1) + half * 512) // 64 == iota((128, 512), 0)).astype(F32).astype(BF16)
    )
    hi, mid, lo = split3(decays[...].reshape(SEQ * 8, 128))
    factors = dot(hi, half_map) + dot(mid, half_map) + dot(lo, half_map)
    state = jnp.zeros((16, 512), F32)
    for s in range(SEQ):
        prefixes[s] = state.astype(BF16)
        state = factors[8 * s : 8 * s + 1, :] * state + taken[s].astype(F32)

    def p_copy(d, there):
        return remote(prefixes.at[there], part(entry, me), p_send.at[d], p_recv.at[d], {"seq": there})

    def send_p(d, carry):
        p_copy(d, lax.rem(me + d, SEQ)).start()
        return carry

    lax.fori_loop(1, SEQ, send_p, 0)
    part(entry, me)[...] = prefixes[me]

    heads(range(4, 8))

    first, second = choice_ref[0:1, :] == 0, choice_ref[1:2, :] == 0
    used = jnp.where(first, 1.0, 0.0) + jnp.where(second, 1.0, 0.0)
    gate = jnp.where(first, share_ref[0:1, :].astype(F32), 0.0) + jnp.where(
        second, share_ref[1:2, :].astype(F32), 0.0
    )
    used = jnp.broadcast_to(used, (128, TOK))
    place = dot(used.astype(BF16), triu_bf) - 1.0
    slot_map = jnp.where(place == iota((128, TOK), 0).astype(F32), used, 0.0)
    gmap_ref[...] = jnp.transpose(slot_map * gate).astype(BF16)
    slot_t = slot_map[0:CAP, :].astype(BF16)

    skip = jnp.concatenate([skip_ref[...], jnp.zeros((1, 112), F32)], axis=1)
    skip_wide = expand(jnp.broadcast_to(skip, (8, 128)))[0:1, :]
    decay_in = jnp.exp(cum)
    cum_wide = expand(decay_in)
    y_ref[...] += skip_wide * x_ref[...].astype(F32)

    def routed(v):
        hi, mid, lo = split3(v)
        return dot(slot_t, hi) + dot(slot_t, mid) + dot(slot_t, lo)

    slot_before = routed(y_ref[...])
    slot_cum = expand(routed(decay_in))
    slot_c = dot(slot_t, c_ref[...]).astype(BF16)

    def wait_p(d, carry):
        there = lax.rem(me - d + SEQ, SEQ)
        remote(
            prefixes.at[me], part(entry, there), p_send.at[d], p_recv.at[d], {"seq": there}
        ).wait_recv()
        return carry

    lax.fori_loop(1, SEQ, wait_p, 0)
    rows[me] = (slot_before + slot_cum * dot(slot_c, entry[...])).astype(BF16)

    def finish():
        outer = dot(c_ref[...], entry[...])
        mamba_ref[...] = (y_ref[...] + cum_wide * outer).astype(BF16)

    def drain():
        def wait_sends(d, carry):
            dec_copy(d, me).wait_send()
            a_copy(d, me).wait_send()
            p_copy(d, me).wait_send()
            return carry

        lax.fori_loop(1, SEQ, wait_sends, 0)

    return drain, finish


def near_first(i):
    odd = i % 2
    return odd * ((i + 1) // 2) + (1 - odd) * ((NZ - i // 2) % NZ)


def expert_part(
    finish, idle, rescale_ref, switch_ref, widen_ref, contract_ref,
    out_ref,
    rows, pg, pu, g1, u1, us, g2, u2, hidden, x_out, x_in, kept, z_out, z_in,
    ag_send, ag_recv, fw_send, fw_recv,
    g1_send, g1_recv, u1_send, u1_recv, g2_send, g2_recv, u2_send, u2_recv,
    hx_send, hx_recv, hy_send, hy_recv,
    xs_send, xs_recv, zs_send, zs_recv,
):
    me = lax.axis_index("seq")
    ch = lax.axis_index("chan")
    xh, z = me // NZ, me % NZ
    y, xl = ch // 2, ch % 2
    other = {"seq": (1 - xh) * NZ + z}
    beside = {"chan": y * 2 + 1 - xl}

    def at_z(there):
        return {"seq": xh * NZ + there % NZ}

    def at_y(there):
        return {"chan": (there % 4) * 2 + xl}

    def order(i):
        return (z - near_first(i) + NZ) % NZ

    def sixteen(start):
        return pl.ds(pl.multiple_of(start, 16), 16)

    fw = remote(rows.at[me], rows.at[me], fw_send, fw_recv, other)

    def ag_copy(way, k, half, block):
        row = half * NZ + block % NZ
        ref = rows.at[row]
        there = at_z(z + 1 if way == 0 else z + NZ - 1)
        return remote(ref, ref, ag_send.at[way, k, half], ag_recv.at[way, k, half], there)

    def ag_last(way, half, block):
        ref = rows.at[half * NZ + block % NZ, pl.ds(32 * way, 32)]
        there = at_z(z + 1 if way == 0 else z + NZ - 1)
        return remote(ref, ref, ag_send.at[way, 4, half], ag_recv.at[way, 4, half], there)

    def behind(way, k):
        return z - k + NZ if way == 0 else z + k

    fw.start()
    for way in range(2):
        ag_copy(way, 1, xh, z).start()
    finish()

    def gather(i):
        @pl.when(i == 0)
        def _():
            remote(rows.at[(1 - xh) * NZ + z], rows.at[(1 - xh) * NZ + z], fw_send, fw_recv, other).wait_recv()
            for way in range(2):
                ag_copy(way, 1, 1 - xh, z).start()
            idle()

        @pl.when((i % 2 == 1) & (i < NZ - 1))
        def _():
            k = (i + 1) // 2
            for j in range(2):
                half = xh + j - 2 * j * xh
                for way in range(2):
                    ag_copy(way, k, half, behind(way, k)).wait_recv()

                    @pl.when(k < 3)
                    def _():
                        ag_copy(way, k + 1, half, behind(way, k)).start()

                    @pl.when(k == 3)
                    def _():
                        ag_last(way, half, behind(way, k)).start()

        @pl.when(i == NZ - 1)
        def _():
            for way in range(2):
                for half in range(2):
                    ag_last(way, half, z + 4).wait_recv()

    def g1_copy(b):
        return remote(pg.at[b, 1 - xl], g1.at[b], g1_send.at[b], g1_recv.at[b], beside)

    def u1_copy(b, d, there, source):
        return remote(
            pu.at[b, :, sixteen(there * 16)], u1.at[b, source], u1_send.at[b, d], u1_recv.at[b, d], at_y(there)
        )

    def g2_copy(b, d, there, source):
        return remote(
            pg.at[b, xl, sixteen(there * 16)], g2.at[b, source], g2_send.at[b, d], g2_recv.at[b, d], at_y(there)
        )

    def u2_copy(b):
        return remote(us.at[b, 1 - xl], u2.at[b], u2_send.at[b], u2_recv.at[b], beside)

    lane = iota((128, 128), 1)

    def project(i):
        gather(i)
        b = order(i)
        v = jnp.concatenate([rows[b], rows[NZ + b]], axis=0).astype(F32)
        squares = jnp.sum(v * v, axis=1, keepdims=True)
        scaled = (v * rescale_ref[...]).astype(BF16)
        hi, mid, lo = split3(squares)
        extra = jnp.where(
            lane == 0,
            hi.astype(F32),
            jnp.where(lane == 1, mid.astype(F32), jnp.where(lane == 2, lo.astype(F32), 0.0)),
        ).astype(BF16)
        pg[b, :, :, HIDL:] = extra.reshape(2, 64, 128)
        pg[b, :, :, 0:HIDL] = dot(scaled, switch_ref[...]).astype(BF16).reshape(2, 64, HIDL)
        g1_copy(b).start()
        pu[b] = dot(scaled, widen_ref[...]).astype(BF16).reshape(2, 64, HIDL)
        for d in (1, 3, 2):
            u1_copy(b, d, (y + d) % 4, y).start()

    def fold(i):
        b = order(i)
        g1_copy(b).wait_recv()
        pg[b, xl] = (pg[b, xl].astype(F32) + g1[b].astype(F32)).astype(BF16)
        for d in (1, 3, 2):
            g2_copy(b, d, (y + d) % 4, y).start()
        total = pu[b, :, sixteen(y * 16), :].astype(F32)
        for d in (1, 3, 2):
            source = (y - d + 4) % 4
            u1_copy(b, d, y, source).wait_recv()
            total = total + u1[b, source].astype(F32)
        us[b] = total.astype(BF16)
        u2_copy(b).start()

    def hx_copy(b, owner):
        ref = hidden.at[b, owner, sixteen(y * 16)]
        return remote(ref, ref, hx_send.at[b], hx_recv.at[b], beside)

    def hy_copy(b, owner, d, source, there):
        ref = hidden.at[b, owner, sixteen(source * 16)]
        return remote(ref, ref, hy_send.at[b, owner, d], hy_recv.at[b, owner, d], at_y(there))

    def activate(i):
        b = order(i)
        gate = pg[b, xl, sixteen(y * 16), :].astype(F32)
        for d in (1, 3, 2):
            source = (y - d + 4) % 4
            g2_copy(b, d, y, source).wait_recv()
            gate = gate + g2[b, source].astype(F32)
        u2_copy(b).wait_recv()
        up = us[b, xl].astype(F32) + u2[b].astype(F32)
        squares = jnp.sum(gate[:, HIDL:], axis=1, keepdims=True)
        inv = lax.rsqrt(squares / WIDTH + EPS)
        gate = gate[:, 0:HIDL] * inv
        hidden[b, xl, sixteen(y * 16), :] = (gate / (1.0 + jnp.exp(-gate)) * (up * inv)).astype(BF16)
        hx_copy(b, xl).start()
        for d in (1, 3, 2):
            hy_copy(b, xl, d, y, y + d).start()

    def relay(i):
        b = order(i)
        hx_copy(b, 1 - xl).wait_recv()
        for d in (1, 3, 2):
            hy_copy(b, 1 - xl, d, y, y + d).start()

    def xs_copy(b):
        return remote(x_out.at[b], x_in.at[b], xs_send.at[b], xs_recv.at[b], other)

    def contract(i):
        b = order(i)
        for half in range(2):
            for d in (1, 3, 2):
                hy_copy(b, half, d, (y - d + 4) % 4, y).wait_recv()
        x_out[b] = dot(hidden[b, 1 - xh], contract_ref[...]).astype(BF16)
        xs_copy(b).start()
        kept[b] = dot(hidden[b, xh], contract_ref[...])

    def zs_copy(i, b, source):
        return remote(z_out.at[b], z_in.at[source], zs_send.at[i], zs_recv.at[i], at_z(b))

    def pass_on(i):
        b = order(i)
        xs_copy(b).wait_recv()
        z_out[b] = (kept[b] + x_in[b].astype(F32)).astype(BF16)

        @pl.when(i > 0)
        def _():
            zs_copy(i, b, z).start()

    stages = ((project, 0), (fold, 1), (activate, 2), (relay, 3), (contract, 4), (pass_on, 5))

    def step(i, carry):
        for stage, off in stages:

            @pl.when((i >= off) & (i < off + NZ))
            def _():
                stage(i - off)

        return carry

    lax.fori_loop(0, NZ + stages[-1][1], step, 0)
    out_ref[...] = kept[z] + x_in[z].astype(F32)

    def collect(i, carry):
        source = (z + near_first(i)) % NZ
        zs_copy(i, z, source).wait_recv()
        out_ref[...] += z_in[source].astype(F32)
        return carry

    lax.fori_loop(1, NZ, collect, 0)

    def drain():
        def wait_sends(b, carry):
            g1_copy(b).wait_send()
            u2_copy(b).wait_send()
            hx_copy(b, xl).wait_send()
            xs_copy(b).wait_send()
            for d in range(1, 4):
                u1_copy(b, d, y, y).wait_send()
                g2_copy(b, d, y, y).wait_send()
                for half in range(2):
                    hy_copy(b, half, d, y, y).wait_send()
            return carry

        lax.fori_loop(0, NZ, wait_sends, 0)

        def wait_z_sends(i, carry):
            zs_copy(i, z, z).wait_send()
            return carry

        lax.fori_loop(1, NZ, wait_z_sends, 0)
        fw.wait_send()
        for way in range(2):
            for half in range(2):
                ag_last(way, half, z).wait_send()
                for k in range(1, 4):
                    ag_copy(way, k, half, z).wait_send()

    return drain


def head_part(
    idle, mamba_ref, gmap_ref, expert_ref, pick_ref, closing_ref, lexicon_ref, div_ref,
    layer_ref, prob_ref,
    held, acc, ordered, squares, chan_stats, seq_stats,
    z_send, z_recv, r_send, r_recv, c_send, c_recv, s_send, s_recv,
):
    me = lax.axis_index("seq")
    ch = lax.axis_index("chan")
    xh, z = me // NZ, me % NZ
    y, xl = ch // 2, ch % 2
    x = xh * 2 + xl
    hi, lo = split2(expert_ref[...])
    gmap = gmap_ref[:, 0:CAP]
    layer = (mamba_ref[...].astype(F32) + dot(gmap, hi) + dot(gmap, lo)).astype(BF16)
    layer_ref[...] = layer
    offsets = jnp.concatenate(
        [pick_ref[...].astype(F32), jnp.full((1, 112), -1.0, F32)], axis=1
    )
    offsets = jnp.transpose(jnp.broadcast_to(offsets, (128, 128)))[0:16, 0:1]
    pick = (iota((16, TOK), 1).astype(F32) == offsets).astype(F32).astype(BF16)
    picked = dot(pick, layer).astype(BF16)
    held[0, y, x, 0:16, :] = picked[:, 0:512]
    held[1, y, x, 0:16, :] = picked[:, 512:1024]

    def at_x(there):
        there = there % 4
        return {"seq": (there // 2) * NZ + z, "chan": y * 2 + there % 2}

    def at_y(there):
        return {"chan": (there % 4) * 2 + xl}

    def z_copy(r):
        return remote(
            held.at[:, y, x, pl.ds(0, 16), :],
            held.at[:, y, x, pl.ds(16 * r, 16), :],
            z_send.at[r],
            z_recv.at[r],
            {"seq": xh * NZ + (z + near_first(r)) % NZ},
        )

    for r in range(1, NZ):
        z_copy(r).start()

    def piece(h, stage, e, g, kind):
        k, e = (e, 0) if stage == 0 else (stage - 1, e)
        yy, xx = (k, e) if h == 0 else (e, k)
        rows = (pl.ds(64 * g, 64), pl.ds(64 * g, 64), pl.ds(64 * g, 32), pl.ds(64 * g + 32, 32))[kind]
        return held.at[h, (y - yy + 4) % 4, (x - xx + 4) % 4, rows]

    def ring(h, stage, g, kind, source):
        ref = piece(h, stage, source, g, kind)
        move = 1 if kind % 2 == 0 else 3
        there = at_y(y + move) if (h == 0) == (stage == 0) else at_x(x + move)
        return remote(ref, ref, r_send.at[h, stage, g, kind], r_recv.at[h, stage, g, kind], there)

    def start(stage, g):
        for h in range(2):
            for kind in range(2):
                ring(h, stage, g, kind, 0).start()

    def arrive(stage, g):
        for kind in range(2):
            for h in range(2):
                ring(h, stage, g, kind, (1, 3)[kind]).wait_recv()
                ring(h, stage, g, kind + 2, (1, 3)[kind]).start()

    def arrive_far(stage, g):
        for h in range(2):
            for kind in (2, 3):
                ring(h, stage, g, kind, 2).wait_recv()

    acc[...] = jnp.zeros_like(acc)
    squares[...] = jnp.zeros_like(squares)

    def use(stage, e):
        for h in range(2):
            k, ee = (e, 0) if stage == 0 else (stage - 1, e)
            yy, xx = (k, ee) if h == 0 else (ee, k)
            yy, xx = (y - yy + 4) % 4, (x - xx + 4) % 4
            upper, right = xx // 2, xx % 2
            first = pl.multiple_of((yy * 2 + right) * CH + h * 512, 512)
            v = held[h, yy, xx].astype(F32)
            squares[upper] += jnp.sum(v * v, axis=1, keepdims=True)
            scaled = (v * closing_ref[:, pl.ds(first, 512)]).astype(BF16)
            acc[upper] += dot(scaled, lexicon_ref[pl.ds(first, 512), :])

    for r in range(1, 4):
        z_copy(r).wait_recv()
    start(0, 0)
    start(1, 0)
    for r in range(4, NZ):
        z_copy(r).wait_recv()
    start(0, 1)
    start(1, 1)
    use(0, 0)
    idle()
    for g in range(2):
        arrive(0, g)
        for k in (1, 3):
            start(1 + k, g)
        arrive(1, g)
    for g in range(2):
        arrive_far(0, g)
        start(3, g)
    for e in (1, 3, 2):
        use(0, e)
    for e in (1, 3):
        use(1, e)
    for g in range(2):
        for k in (1, 3):
            arrive(1 + k, g)
    for g in range(2):
        arrive_far(1, g)
    use(1, 2)
    for k in (1, 3):
        for e in (1, 3):
            use(1 + k, e)
    for g in range(2):
        arrive(3, g)
    for k in (1, 3):
        for g in range(2):
            arrive_far(1 + k, g)
        use(1 + k, 2)
    for e in (1, 3):
        use(3, e)
    for g in range(2):
        arrive_far(3, g)
    use(3, 2)

    inv = lax.rsqrt(squares[...] / WIDTH + EPS)
    for r in range(NZ):
        rows = pl.ds(pl.multiple_of(((z - near_first(r) + NZ) % NZ) * 16, 16), 16)
        part = slice(16 * r, 16 * r + 16)
        ordered[:, rows, :] = acc[:, part, :] * inv[:, part, :]
    scores = ordered[...].reshape(TOK, TOK) / div_ref[0, 0]
    top = jnp.max(scores, axis=1, keepdims=True)
    mass = jnp.sum(jnp.exp(scores - top), axis=1, keepdims=True)
    tops = jnp.transpose(jnp.broadcast_to(top, (TOK, 128)))[0:8, :]
    masses = jnp.transpose(jnp.broadcast_to(mass, (TOK, 128)))[0:8, :]
    row = iota((8, 128), 0)
    chan_stats[ch] = jnp.where(
        row == 0,
        tops[:, 0:128],
        jnp.where(row == 1, tops[:, 128:256], jnp.where(row == 2, masses[:, 0:128], masses[:, 128:256])),
    )
    seq_stats[me] = jnp.zeros((8, 128), F32)

    def chan_copy(d, source, there):
        ref = chan_stats.at[source]
        return remote(ref, ref, c_send.at[d], c_recv.at[d], {"chan": there})

    def send_c(d, carry):
        chan_copy(d, ch, lax.rem(ch + d, CHAN)).start()
        return carry

    lax.fori_loop(1, CHAN, send_c, 0)

    def wait_c(d, carry):
        chan_copy(d, lax.rem(ch - d + CHAN, CHAN), ch).wait_recv()
        return carry

    lax.fori_loop(1, CHAN, wait_c, 0)

    def join(ref):
        tops = ref[:, 0:2, :]
        top = jnp.max(tops, axis=0)
        return top, jnp.sum(ref[:, 2:4, :] * jnp.exp(tops - top[None]), axis=0)

    seq_stats[me, 0:2, :], seq_stats[me, 2:4, :] = join(chan_stats)

    def seq_copy(d, source, there):
        ref = seq_stats.at[source]
        return remote(ref, ref, s_send.at[d], s_recv.at[d], {"seq": there})

    def send_s(d, carry):
        seq_copy(d, me, lax.rem(me + d, SEQ)).start()
        return carry

    lax.fori_loop(1, SEQ, send_s, 0)

    def wait_sends(d, carry):
        z_copy(d).wait_send()
        chan_copy(d, ch, ch).wait_send()
        return carry

    lax.fori_loop(1, NZ, wait_sends, 0)
    for stage in range(5):
        for g in range(2):
            for h in range(2):
                for kind in range(4):
                    ring(h, stage, g, kind, 0).wait_send()

    def wait_s(d, carry):
        seq_copy(d, lax.rem(me - d + SEQ, SEQ), me).wait_recv()
        return carry

    lax.fori_loop(1, SEQ, wait_s, 0)
    top, mass = join(seq_stats)
    norm = top + jnp.log(mass)
    for half in range(2):
        rows = slice(128 * half, 128 * half + 128)
        column = jnp.transpose(jnp.broadcast_to(norm[half : half + 1, :], (128, 128)))[:, 0:1]
        prob_ref[rows, :] = scores[rows, :] - column

    def wait_s_sends(d, carry):
        seq_copy(d, me, me).wait_send()
        return carry

    lax.fori_loop(1, SEQ, wait_s_sends, 0)


def whole_kernel(
    x_ref, b_ref, c_ref, la_ref, skip_ref, choice_ref, share_ref,
    rescale_ref, switch_hbm, widen_hbm, contract_hbm,
    pick_ref, closing_ref, lexicon_hbm, div_ref,
    layer_ref, prob_ref,
    mamba, gmap, expert, switch, widen, contract, lexicon, rows, load_sem,
    *scratch,
):
    barrier = pltpu.get_barrier_semaphore()
    me = lax.axis_index("seq")
    ch = lax.axis_index("chan")
    greet("seq", SEQ, me)
    greet("chan", CHAN, ch)
    xh, z = me // NZ, me % NZ
    y, xl = ch // 2, ch % 2
    diagonal = {"seq": (1 - xh) * NZ + z, "chan": y * 2 + 1 - xl}
    pl.semaphore_signal(barrier, inc=1, device_id=diagonal, device_id_type=MESH)
    loads = [
        pltpu.make_async_copy(src, dst, load_sem.at[k])
        for k, (src, dst) in enumerate(
            ((switch_hbm, switch), (widen_hbm, widen), (contract_hbm, contract), (lexicon_hbm, lexicon))
        )
    ]
    for load in loads:
        load.start()
    first, finish = scan_part(
        x_ref, b_ref, c_ref, la_ref, skip_ref, choice_ref, share_ref,
        mamba, rows, gmap, *scratch[:13],
    )
    def idle():
        first()
        for load in loads:
            load.wait()

    drain = expert_part(finish, idle, rescale_ref, switch, widen, contract, expert, rows, *scratch[13 : 13 + 33])
    head_part(
        drain, mamba, gmap, expert, pick_ref, closing_ref, lexicon, div_ref, layer_ref, prob_ref, *scratch[46:]
    )


def whole_call(*args):
    vm = pl.BlockSpec(memory_space=pltpu.VMEM)
    hbm = pl.BlockSpec(memory_space=pl.ANY)
    dma = pltpu.SemaphoreType.DMA
    in_specs = [vm] * 8 + [hbm] * 3 + [vm] * 2 + [hbm, pl.BlockSpec(memory_space=pltpu.SMEM)]
    return pl.pallas_call(
        whole_kernel,
        out_shape=(
            jax.ShapeDtypeStruct((TOK, CH), BF16),
            jax.ShapeDtypeStruct((TOK, TOK), F32),
        ),
        in_specs=in_specs,
        out_specs=(vm, vm),
        scratch_shapes=[
            pltpu.VMEM((TOK, CH), BF16),
            pltpu.VMEM((TOK, 128), BF16),
            pltpu.VMEM((CAP, CH), F32),
            pltpu.VMEM((CH, HIDL), BF16),
            pltpu.VMEM((CH, HIDL), BF16),
            pltpu.VMEM((HIDL, CH), BF16),
            pltpu.VMEM((WIDTH, TOK), BF16),
            pltpu.VMEM((SEQ, CAP, CH), BF16),
            dma((4,)),
            pltpu.VMEM((128, TOK), F32),
            pltpu.VMEM((128, CH), BF16),
            pltpu.VMEM((SEQ, 16, 512), BF16),
            pltpu.VMEM((SEQ, 8, 128), F32),
            pltpu.VMEM((SEQ, 16, 512), BF16),
            pltpu.VMEM((128, CH), BF16),
            pltpu.VMEM((TOK, CH), F32),
            *[dma((SEQ,))] * 6,
            pltpu.VMEM((NZ, 2, 64, HIDL + 128), BF16),
            pltpu.VMEM((NZ, 2, 64, HIDL), BF16),
            pltpu.VMEM((NZ, 64, HIDL + 128), BF16),
            pltpu.VMEM((NZ, 4, 2, 16, HIDL), BF16),
            pltpu.VMEM((NZ, 2, 16, HIDL), BF16),
            pltpu.VMEM((NZ, 4, 16, HIDL + 128), BF16),
            pltpu.VMEM((NZ, 16, HIDL), BF16),
            pltpu.VMEM((NZ, 2, 64, HIDL), BF16),
            pltpu.VMEM((NZ, CAP, CH), BF16),
            pltpu.VMEM((NZ, CAP, CH), BF16),
            pltpu.VMEM((NZ, CAP, CH), F32),
            pltpu.VMEM((NZ, CAP, CH), BF16),
            pltpu.VMEM((NZ, CAP, CH), BF16),
            dma((2, 5, 2)), dma((2, 5, 2)), dma, dma,
            dma((NZ,)), dma((NZ,)), dma((NZ, 4)), dma((NZ, 4)),
            dma((NZ, 4)), dma((NZ, 4)), dma((NZ,)), dma((NZ,)),
            dma((NZ,)), dma((NZ,)), dma((NZ, 2, 4)), dma((NZ, 2, 4)),
            dma((NZ,)), dma((NZ,)), dma((NZ,)), dma((NZ,)),
            pltpu.VMEM((2, 4, 4, 128, 512), BF16),
            pltpu.VMEM((2, 128, TOK), F32),
            pltpu.VMEM((2, 128, TOK), F32),
            pltpu.VMEM((2, 128, 1), F32),
            pltpu.VMEM((CHAN, 8, 128), F32),
            pltpu.VMEM((SEQ, 8, 128), F32),
            dma((NZ,)), dma((NZ,)),
            dma((2, 5, 2, 4)), dma((2, 5, 2, 4)),
            dma((CHAN,)), dma((CHAN,)),
            dma((SEQ,)), dma((SEQ,)),
        ],
        compiler_params=pltpu.CompilerParams(
            collective_id=0, has_side_effects=True, vmem_limit_bytes=VMEM_LIMIT
        ),
        name="whole",
    )(*args)


def shards(
    recurrence_feed,
    memory_write_matrix,
    memory_read_matrix,
    log_shrink_table,
    skip_connection_scale,
    specialist_choices,
    specialist_mixing_shares,
    specialist_rescale_vector,
    specialist_switch_matrix,
    specialist_widen_matrix,
    specialist_contract_matrix,
    closing_rescale_vector,
    lexicon_matrix,
    softness_divisor,
    picked_entry_offsets,
):
    return whole_call(
        recurrence_feed,
        memory_write_matrix,
        memory_read_matrix,
        log_shrink_table.T,
        skip_connection_scale.reshape(1, -1),
        specialist_choices.T,
        specialist_mixing_shares.T,
        specialist_rescale_vector.reshape(1, -1),
        specialist_switch_matrix,
        specialist_widen_matrix,
        specialist_contract_matrix,
        picked_entry_offsets.reshape(1, -1),
        closing_rescale_vector.reshape(1, -1),
        lexicon_matrix,
        softness_divisor.reshape(1, 1),
    )


def solution(mesh):
    in_specs = (
        P(("dp", "seq"), "chan"),
        P(("dp", "seq"), None),
        P(("dp", "seq"), None),
        P(("dp", "seq"), "chan"),
        P("chan"),
        P(("dp", "seq"), None),
        P(("dp", "seq"), None),
        P("chan"),
        P("chan", "seq"),
        P("chan", "seq"),
        P("seq", "chan"),
        P(),
        P(None, ("seq", "chan")),
        P(),
        P(("dp", "seq")),
    )
    out_specs = (P(("dp", "seq"), "chan"), P("dp", ("seq", "chan")))
    return jax.shard_map(shards, mesh=mesh, in_specs=in_specs, out_specs=out_specs, check_vma=False)
```

```python
import jax
import jax.numpy as jnp
from jax import lax
from jax.experimental import pallas as pl
from jax.experimental.pallas import tpu as pltpu
from jax.sharding import PartitionSpec as P

MESH = pl.DeviceIdType.MESH
F32 = jnp.float32
BF16 = jnp.bfloat16
TOK = 256
CH = 1024
SEQ = 16
CHAN = 8
NZ = 8
CAP = 64
HIDL = 768
WIDTH = 8192
EPS = 1e-5
VMEM_LIMIT = 56 * 1024 * 1024


def dot(a, b):
    return jnp.dot(a, b, preferred_element_type=F32)


def split2(v):
    hi = v.astype(BF16)
    return hi, (v - hi.astype(F32)).astype(BF16)


def split3(v):
    hi = v.astype(BF16)
    rest = v - hi.astype(F32)
    mid = rest.astype(BF16)
    return hi, mid, (rest - mid.astype(F32)).astype(BF16)


def iota(shape, dim):
    return lax.broadcasted_iota(jnp.int32, shape, dim)


def remote(src, dst, send_sem, recv_sem, where):
    return pltpu.make_async_remote_copy(
        src_ref=src,
        dst_ref=dst,
        send_sem=send_sem,
        recv_sem=recv_sem,
        device_id=where,
        device_id_type=MESH,
    )


def greet(axis, size, me):
    barrier = pltpu.get_barrier_semaphore()

    def one(d, carry):
        pl.semaphore_signal(
            barrier, inc=1, device_id={axis: lax.rem(me + d, size)}, device_id_type=MESH
        )
        return carry

    lax.fori_loop(1, size, one, 0)


def scan_part(
    x_ref, b_ref, c_ref, la_ref, skip_ref, choice_ref, share_ref,
    mamba_ref, rows, gmap_ref,
    wide, local, taken, decays, prefixes, entry, y_ref,
    dec_send, dec_recv, a_send, a_recv, p_send, p_recv,
):
    me = lax.axis_index("seq")

    wide[...] = jnp.zeros_like(wide)
    wide[0:16, :] = la_ref[...]
    tril = (iota((TOK, TOK), 0) >= iota((TOK, TOK), 1)).astype(F32)
    triu_bf = (iota((TOK, TOK), 0) <= iota((TOK, TOK), 1)).astype(F32).astype(BF16)
    hi, mid, lo = split3(wide[...])
    cum_t = dot(hi, triu_bf) + dot(mid, triu_bf) + dot(lo, triu_bf)
    cum = jnp.transpose(cum_t)
    last = cum[TOK - 1 : TOK, :]
    spread_map = (iota((128, CH), 1) // 64 == iota((128, CH), 0)).astype(F32).astype(BF16)

    def expand(v):
        hi, lo = split2(v)
        return dot(hi, spread_map) + dot(lo, spread_map)

    decays[me] = jnp.broadcast_to(jnp.exp(last), (8, 128))
    pl.semaphore_wait(pltpu.get_barrier_semaphore(), 15 + 7 + 1)

    def dec_copy(d, there):
        return remote(
            decays.at[me], decays.at[me], dec_send.at[d], dec_recv.at[d], {"seq": there}
        )

    def send_dec(d, carry):
        dec_copy(d, lax.rem(me + d, SEQ)).start()
        return carry

    lax.fori_loop(1, SEQ, send_dec, 0)

    weighted = (x_ref[...].astype(F32) * expand(jnp.exp(last - cum))).astype(BF16)
    b_t = jnp.transpose(b_ref[...].astype(F32)).astype(BF16)
    local[...] = dot(b_t, weighted).astype(BF16)

    def part(ref, p):
        return ref.at[
            pl.ds(pl.multiple_of((p // 2) * 16, 16), 16),
            pl.ds(pl.multiple_of((p % 2) * 512, 512), 512),
        ]

    def a_copy(d, there):
        return remote(part(local, there), taken.at[me], a_send.at[d], a_recv.at[d], {"seq": there})

    def send_a(d, carry):
        a_copy(d, lax.rem(me + d, SEQ)).start()
        return carry

    lax.fori_loop(1, SEQ, send_a, 0)
    taken[me] = part(local, me)[...]

    scores = lax.dot_general(
        c_ref[...], b_ref[...], (((1,), (1,)), ((), ())), preferred_element_type=F32
    )
    scores = scores * tril
    lane = iota((128, 128), 1)

    def heads(pairs):
        for q in pairs:
            cols = slice(128 * q, 128 * q + 128)
            xq = x_ref[:, cols]
            for r in range(2):
                rows = slice(128 * r, 128 * r + 128)
                width = 128 * (r + 1)
                out = []
                for h in (2 * q, 2 * q + 1):
                    decay = jnp.exp(
                        jnp.minimum(cum[rows, h : h + 1] - cum_t[h : h + 1, 0:width], 0.0)
                    )
                    mixing = (scores[rows, 0:width] * decay).astype(BF16)
                    out.append(dot(mixing, xq[0:width, :]))
                y_ref[rows, cols] = jnp.where(lane < 64, out[0], out[1])

    heads(range(0, 4))

    def wait_dec(d, carry):
        dec_copy(d, me).wait_recv()
        a_copy(d, me).wait_recv()
        return carry

    lax.fori_loop(1, SEQ, wait_dec, 0)
    half = lax.rem(me, 2)
    half_map = (
        ((iota((128, 512), 1) + half * 512) // 64 == iota((128, 512), 0)).astype(F32).astype(BF16)
    )
    hi, mid, lo = split3(decays[...].reshape(SEQ * 8, 128))
    factors = dot(hi, half_map) + dot(mid, half_map) + dot(lo, half_map)
    state = jnp.zeros((16, 512), F32)
    for s in range(SEQ):
        prefixes[s] = state.astype(BF16)
        state = factors[8 * s : 8 * s + 1, :] * state + taken[s].astype(F32)

    def p_copy(d, there):
        return remote(prefixes.at[there], part(entry, me), p_send.at[d], p_recv.at[d], {"seq": there})

    def send_p(d, carry):
        p_copy(d, lax.rem(me + d, SEQ)).start()
        return carry

    lax.fori_loop(1, SEQ, send_p, 0)
    part(entry, me)[...] = prefixes[me]

    heads(range(4, 8))

    first, second = choice_ref[0:1, :] == 0, choice_ref[1:2, :] == 0
    used = jnp.where(first, 1.0, 0.0) + jnp.where(second, 1.0, 0.0)
    gate = jnp.where(first, share_ref[0:1, :].astype(F32), 0.0) + jnp.where(
        second, share_ref[1:2, :].astype(F32), 0.0
    )
    used = jnp.broadcast_to(used, (128, TOK))
    place = dot(used.astype(BF16), triu_bf) - 1.0
    slot_map = jnp.where(place == iota((128, TOK), 0).astype(F32), used, 0.0)
    gmap_ref[...] = jnp.transpose(slot_map * gate).astype(BF16)
    slot_t = slot_map[0:CAP, :].astype(BF16)

    skip = jnp.concatenate([skip_ref[...], jnp.zeros((1, 112), F32)], axis=1)
    skip_wide = expand(jnp.broadcast_to(skip, (8, 128)))[0:1, :]
    decay_in = jnp.exp(cum)
    cum_wide = expand(decay_in)
    y_ref[...] += skip_wide * x_ref[...].astype(F32)

    def routed(v):
        hi, mid, lo = split3(v)
        return dot(slot_t, hi) + dot(slot_t, mid) + dot(slot_t, lo)

    slot_before = routed(y_ref[...])
    slot_cum = expand(routed(decay_in))
    slot_c = dot(slot_t, c_ref[...]).astype(BF16)

    def wait_p(d, carry):
        there = lax.rem(me - d + SEQ, SEQ)
        remote(
            prefixes.at[me], part(entry, there), p_send.at[d], p_recv.at[d], {"seq": there}
        ).wait_recv()
        return carry

    lax.fori_loop(1, SEQ, wait_p, 0)
    rows[me] = (slot_before + slot_cum * dot(slot_c, entry[...])).astype(BF16)

    def finish():
        outer = dot(c_ref[...], entry[...])
        mamba_ref[...] = (y_ref[...] + cum_wide * outer).astype(BF16)

    def drain():
        def wait_sends(d, carry):
            dec_copy(d, me).wait_send()
            a_copy(d, me).wait_send()
            p_copy(d, me).wait_send()
            return carry

        lax.fori_loop(1, SEQ, wait_sends, 0)

    return drain, finish


def near_first(i):
    odd = i % 2
    return odd * ((i + 1) // 2) + (1 - odd) * ((NZ - i // 2) % NZ)


def expert_part(
    finish, idle, rescale_ref, switch_ref, widen_ref, contract_ref,
    out_ref,
    rows, pg, pu, g1, u1, us, g2, u2, hidden, x_out, x_in, kept, z_out, z_in,
    ag_send, ag_recv, fw_send, fw_recv,
    g1_send, g1_recv, u1_send, u1_recv, g2_send, g2_recv, u2_send, u2_recv,
    hx_send, hx_recv, hy_send, hy_recv,
    xs_send, xs_recv, zs_send, zs_recv,
):
    me = lax.axis_index("seq")
    ch = lax.axis_index("chan")
    xh, z = me // NZ, me % NZ
    y, xl = ch // 2, ch % 2
    other = {"seq": (1 - xh) * NZ + z}
    beside = {"chan": y * 2 + 1 - xl}

    def at_z(there):
        return {"seq": xh * NZ + there % NZ}

    def at_y(there):
        return {"chan": (there % 4) * 2 + xl}

    def order(i):
        return (z - near_first(i) + NZ) % NZ

    def sixteen(start):
        return pl.ds(pl.multiple_of(start, 16), 16)

    fw = remote(rows.at[me], rows.at[me], fw_send, fw_recv, other)

    def ag_copy(way, k, half, block):
        row = half * NZ + block % NZ
        ref = rows.at[row]
        there = at_z(z + 1 if way == 0 else z + NZ - 1)
        return remote(ref, ref, ag_send.at[way, k, half], ag_recv.at[way, k, half], there)

    def ag_last(way, half, block):
        ref = rows.at[half * NZ + block % NZ, pl.ds(32 * way, 32)]
        there = at_z(z + 1 if way == 0 else z + NZ - 1)
        return remote(ref, ref, ag_send.at[way, 4, half], ag_recv.at[way, 4, half], there)

    def behind(way, k):
        return z - k + NZ if way == 0 else z + k

    fw.start()
    for way in range(2):
        ag_copy(way, 1, xh, z).start()
    finish()

    def gather(i):
        @pl.when(i == 0)
        def _():
            remote(rows.at[(1 - xh) * NZ + z], rows.at[(1 - xh) * NZ + z], fw_send, fw_recv, other).wait_recv()
            for way in range(2):
                ag_copy(way, 1, 1 - xh, z).start()
            idle()

        @pl.when((i % 2 == 1) & (i < NZ - 1))
        def _():
            k = (i + 1) // 2
            for j in range(2):
                half = xh + j - 2 * j * xh
                for way in range(2):
                    ag_copy(way, k, half, behind(way, k)).wait_recv()

                    @pl.when(k < 3)
                    def _():
                        ag_copy(way, k + 1, half, behind(way, k)).start()

                    @pl.when(k == 3)
                    def _():
                        ag_last(way, half, behind(way, k)).start()

        @pl.when(i == NZ - 1)
        def _():
            for way in range(2):
                for half in range(2):
                    ag_last(way, half, z + 4).wait_recv()

    def g1_copy(b):
        return remote(pg.at[b, 1 - xl], g1.at[b], g1_send.at[b], g1_recv.at[b], beside)

    def u1_copy(b, d, there, source):
        return remote(
            pu.at[b, :, sixteen(there * 16)], u1.at[b, source], u1_send.at[b, d], u1_recv.at[b, d], at_y(there)
        )

    def g2_copy(b, d, there, source):
        return remote(
            pg.at[b, xl, sixteen(there * 16)], g2.at[b, source], g2_send.at[b, d], g2_recv.at[b, d], at_y(there)
        )

    def u2_copy(b):
        return remote(us.at[b, 1 - xl], u2.at[b], u2_send.at[b], u2_recv.at[b], beside)

    lane = iota((128, 128), 1)

    def project(i):
        gather(i)
        b = order(i)
        v = jnp.concatenate([rows[b], rows[NZ + b]], axis=0).astype(F32)
        squares = jnp.sum(v * v, axis=1, keepdims=True)
        scaled = (v * rescale_ref[...]).astype(BF16)
        hi, mid, lo = split3(squares)
        extra = jnp.where(
            lane == 0,
            hi.astype(F32),
            jnp.where(lane == 1, mid.astype(F32), jnp.where(lane == 2, lo.astype(F32), 0.0)),
        ).astype(BF16)
        pg[b, :, :, HIDL:] = extra.reshape(2, 64, 128)
        pg[b, :, :, 0:HIDL] = dot(scaled, switch_ref[...]).astype(BF16).reshape(2, 64, HIDL)
        g1_copy(b).start()
        pu[b] = dot(scaled, widen_ref[...]).astype(BF16).reshape(2, 64, HIDL)
        for d in (1, 3, 2):
            u1_copy(b, d, (y + d) % 4, y).start()

    def fold(i):
        b = order(i)
        g1_copy(b).wait_recv()
        pg[b, xl] = (pg[b, xl].astype(F32) + g1[b].astype(F32)).astype(BF16)
        for d in (1, 3, 2):
            g2_copy(b, d, (y + d) % 4, y).start()
        total = pu[b, :, sixteen(y * 16), :].astype(F32)
        for d in (1, 3, 2):
            source = (y - d + 4) % 4
            u1_copy(b, d, y, source).wait_recv()
            total = total + u1[b, source].astype(F32)
        us[b] = total.astype(BF16)
        u2_copy(b).start()

    def hx_copy(b, owner):
        ref = hidden.at[b, owner, sixteen(y * 16)]
        return remote(ref, ref, hx_send.at[b], hx_recv.at[b], beside)

    def hy_copy(b, owner, d, source, there):
        ref = hidden.at[b, owner, sixteen(source * 16)]
        return remote(ref, ref, hy_send.at[b, owner, d], hy_recv.at[b, owner, d], at_y(there))

    def activate(i):
        b = order(i)
        gate = pg[b, xl, sixteen(y * 16), :].astype(F32)
        for d in (1, 3, 2):
            source = (y - d + 4) % 4
            g2_copy(b, d, y, source).wait_recv()
            gate = gate + g2[b, source].astype(F32)
        u2_copy(b).wait_recv()
        up = us[b, xl].astype(F32) + u2[b].astype(F32)
        squares = jnp.sum(gate[:, HIDL:], axis=1, keepdims=True)
        inv = lax.rsqrt(squares / WIDTH + EPS)
        gate = gate[:, 0:HIDL] * inv
        hidden[b, xl, sixteen(y * 16), :] = (gate / (1.0 + jnp.exp(-gate)) * (up * inv)).astype(BF16)
        hx_copy(b, xl).start()
        for d in (1, 3, 2):
            hy_copy(b, xl, d, y, y + d).start()

    def relay(i):
        b = order(i)
        hx_copy(b, 1 - xl).wait_recv()
        for d in (1, 3, 2):
            hy_copy(b, 1 - xl, d, y, y + d).start()

    def xs_copy(b):
        return remote(x_out.at[b], x_in.at[b], xs_send.at[b], xs_recv.at[b], other)

    def contract(i):
        b = order(i)
        for half in range(2):
            for d in (1, 3, 2):
                hy_copy(b, half, d, (y - d + 4) % 4, y).wait_recv()
        x_out[b] = dot(hidden[b, 1 - xh], contract_ref[...]).astype(BF16)
        xs_copy(b).start()
        kept[b] = dot(hidden[b, xh], contract_ref[...])

    def zs_copy(i, b, source):
        return remote(z_out.at[b], z_in.at[source], zs_send.at[i], zs_recv.at[i], at_z(b))

    def pass_on(i):
        b = order(i)
        xs_copy(b).wait_recv()
        z_out[b] = (kept[b] + x_in[b].astype(F32)).astype(BF16)

        @pl.when(i > 0)
        def _():
            zs_copy(i, b, z).start()

    stages = ((project, 0), (fold, 1), (activate, 2), (relay, 3), (contract, 4), (pass_on, 5))

    def step(i, carry):
        for stage, off in stages:

            @pl.when((i >= off) & (i < off + NZ))
            def _():
                stage(i - off)

        return carry

    lax.fori_loop(0, NZ + stages[-1][1], step, 0)
    out_ref[...] = kept[z] + x_in[z].astype(F32)

    def collect(i, carry):
        source = (z + near_first(i)) % NZ
        zs_copy(i, z, source).wait_recv()
        out_ref[...] += z_in[source].astype(F32)
        return carry

    lax.fori_loop(1, NZ, collect, 0)

    def drain():
        def wait_sends(b, carry):
            g1_copy(b).wait_send()
            u2_copy(b).wait_send()
            hx_copy(b, xl).wait_send()
            xs_copy(b).wait_send()
            for d in range(1, 4):
                u1_copy(b, d, y, y).wait_send()
                g2_copy(b, d, y, y).wait_send()
                for half in range(2):
                    hy_copy(b, half, d, y, y).wait_send()
            return carry

        lax.fori_loop(0, NZ, wait_sends, 0)

        def wait_z_sends(i, carry):
            zs_copy(i, z, z).wait_send()
            return carry

        lax.fori_loop(1, NZ, wait_z_sends, 0)
        fw.wait_send()
        for way in range(2):
            for half in range(2):
                ag_last(way, half, z).wait_send()
                for k in range(1, 4):
                    ag_copy(way, k, half, z).wait_send()

    return drain


def head_part(
    idle, mamba_ref, gmap_ref, expert_ref, pick_ref, closing_ref, lexicon_ref, div_ref,
    layer_ref, prob_ref,
    held, acc, ordered, squares, chan_stats, seq_stats,
    z_send, z_recv, r_send, r_recv, c_send, c_recv, s_send, s_recv,
):
    me = lax.axis_index("seq")
    ch = lax.axis_index("chan")
    xh, z = me // NZ, me % NZ
    y, xl = ch // 2, ch % 2
    x = xh * 2 + xl
    hi, lo = split2(expert_ref[...])
    gmap = gmap_ref[:, 0:CAP]
    layer = (mamba_ref[...].astype(F32) + dot(gmap, hi) + dot(gmap, lo)).astype(BF16)
    layer_ref[...] = layer
    offsets = jnp.concatenate(
        [pick_ref[...].astype(F32), jnp.full((1, 112), -1.0, F32)], axis=1
    )
    offsets = jnp.transpose(jnp.broadcast_to(offsets, (128, 128)))[0:16, 0:1]
    pick = (iota((16, TOK), 1).astype(F32) == offsets).astype(F32).astype(BF16)
    picked = dot(pick, layer).astype(BF16)
    held[0, y, x, 0:16, :] = picked[:, 0:512]
    held[1, y, x, 0:16, :] = picked[:, 512:1024]

    def at_x(there):
        there = there % 4
        return {"seq": (there // 2) * NZ + z, "chan": y * 2 + there % 2}

    def at_y(there):
        return {"chan": (there % 4) * 2 + xl}

    def z_copy(r):
        return remote(
            held.at[:, y, x, pl.ds(0, 16), :],
            held.at[:, y, x, pl.ds(16 * r, 16), :],
            z_send.at[r],
            z_recv.at[r],
            {"seq": xh * NZ + (z + near_first(r)) % NZ},
        )

    for r in range(1, NZ):
        z_copy(r).start()

    def piece(h, stage, e, g, kind):
        k, e = (e, 0) if stage == 0 else (stage - 1, e)
        yy, xx = (k, e) if h == 0 else (e, k)
        rows = (pl.ds(64 * g, 64), pl.ds(64 * g, 64), pl.ds(64 * g, 32), pl.ds(64 * g + 32, 32))[kind]
        return held.at[h, (y - yy + 4) % 4, (x - xx + 4) % 4, rows]

    def ring(h, stage, g, kind, source):
        ref = piece(h, stage, source, g, kind)
        move = 1 if kind % 2 == 0 else 3
        there = at_y(y + move) if (h == 0) == (stage == 0) else at_x(x + move)
        return remote(ref, ref, r_send.at[h, stage, g, kind], r_recv.at[h, stage, g, kind], there)

    def start(stage, g):
        for h in range(2):
            for kind in range(2):
                ring(h, stage, g, kind, 0).start()

    def arrive(stage, g):
        for kind in range(2):
            for h in range(2):
                ring(h, stage, g, kind, (1, 3)[kind]).wait_recv()
                ring(h, stage, g, kind + 2, (1, 3)[kind]).start()

    def arrive_far(stage, g):
        for h in range(2):
            for kind in (2, 3):
                ring(h, stage, g, kind, 2).wait_recv()

    def sent(stage):
        for g in range(2):
            for h in range(2):
                for kind in range(4):
                    ring(h, stage, g, kind, 0).wait_send()

    acc[...] = jnp.zeros_like(acc)
    squares[...] = jnp.zeros_like(squares)

    def use(stage, e):
        for h in range(2):
            k, ee = (e, 0) if stage == 0 else (stage - 1, e)
            yy, xx = (k, ee) if h == 0 else (ee, k)
            yy, xx = (y - yy + 4) % 4, (x - xx + 4) % 4
            upper, right = xx // 2, xx % 2
            first = pl.multiple_of((yy * 2 + right) * CH + h * 512, 512)
            v = held[h, yy, xx].astype(F32)
            squares[upper] += jnp.sum(v * v, axis=1, keepdims=True)
            scaled = (v * closing_ref[:, pl.ds(first, 512)]).astype(BF16)
            acc[upper] += dot(scaled, lexicon_ref[pl.ds(first, 512), :])

    for r in range(1, 4):
        z_copy(r).wait_recv()
    start(0, 0)
    start(1, 0)
    for r in range(4, NZ):
        z_copy(r).wait_recv()
    start(0, 1)
    start(1, 1)
    use(0, 0)
    for g in range(2):
        arrive(0, g)
        for k in (1, 3):
            start(1 + k, g)
        arrive(1, g)
    for g in range(2):
        arrive_far(0, g)
        start(3, g)
    idle()
    for e in (1, 3, 2):
        use(0, e)
    for e in (1, 3):
        use(1, e)
    for g in range(2):
        for k in (1, 3):
            arrive(1 + k, g)
    for g in range(2):
        arrive_far(1, g)
    use(1, 2)
    for k in (1, 3):
        for e in (1, 3):
            use(1 + k, e)
    for g in range(2):
        arrive(3, g)
    for k in (1, 3):
        for g in range(2):
            arrive_far(1 + k, g)
        use(1 + k, 2)
    for stage in (0, 1, 2, 4):
        sent(stage)
    for e in (1, 3):
        use(3, e)
    for g in range(2):
        arrive_far(3, g)
    use(3, 2)

    inv = lax.rsqrt(squares[...] / WIDTH + EPS)
    for r in range(NZ):
        rows = pl.ds(pl.multiple_of(((z - near_first(r) + NZ) % NZ) * 16, 16), 16)
        part = slice(16 * r, 16 * r + 16)
        ordered[:, rows, :] = acc[:, part, :] * inv[:, part, :]
    scores = ordered[...].reshape(TOK, TOK) / div_ref[0, 0]
    top = jnp.max(scores, axis=1, keepdims=True)
    mass = jnp.sum(jnp.exp(scores - top), axis=1, keepdims=True)
    tops = jnp.transpose(jnp.broadcast_to(top, (TOK, 128)))[0:8, :]
    masses = jnp.transpose(jnp.broadcast_to(mass, (TOK, 128)))[0:8, :]
    row = iota((8, 128), 0)
    chan_stats[ch] = jnp.where(
        row == 0,
        tops[:, 0:128],
        jnp.where(row == 1, tops[:, 128:256], jnp.where(row == 2, masses[:, 0:128], masses[:, 128:256])),
    )
    seq_stats[me] = jnp.zeros((8, 128), F32)

    def chan_copy(d, source, there):
        ref = chan_stats.at[source]
        return remote(ref, ref, c_send.at[d], c_recv.at[d], {"chan": there})

    def send_c(d, carry):
        chan_copy(d, ch, lax.rem(ch + d, CHAN)).start()
        return carry

    lax.fori_loop(1, CHAN, send_c, 0)

    def wait_c(d, carry):
        chan_copy(d, lax.rem(ch - d + CHAN, CHAN), ch).wait_recv()
        return carry

    lax.fori_loop(1, CHAN, wait_c, 0)

    def join(ref):
        tops = ref[:, 0:2, :]
        top = jnp.max(tops, axis=0)
        return top, jnp.sum(ref[:, 2:4, :] * jnp.exp(tops - top[None]), axis=0)

    seq_stats[me, 0:2, :], seq_stats[me, 2:4, :] = join(chan_stats)

    def seq_copy(d, source, there):
        ref = seq_stats.at[source]
        return remote(ref, ref, s_send.at[d], s_recv.at[d], {"seq": there})

    def send_s(d, carry):
        seq_copy(d, me, lax.rem(me + d, SEQ)).start()
        return carry

    lax.fori_loop(1, SEQ, send_s, 0)

    def wait_sends(d, carry):
        z_copy(d).wait_send()
        chan_copy(d, ch, ch).wait_send()
        return carry

    lax.fori_loop(1, NZ, wait_sends, 0)
    sent(3)

    def wait_s(d, carry):
        seq_copy(d, lax.rem(me - d + SEQ, SEQ), me).wait_recv()
        return carry

    lax.fori_loop(1, SEQ, wait_s, 0)
    top, mass = join(seq_stats)
    norm = top + jnp.log(mass)
    for half in range(2):
        rows = slice(128 * half, 128 * half + 128)
        column = jnp.transpose(jnp.broadcast_to(norm[half : half + 1, :], (128, 128)))[:, 0:1]
        prob_ref[rows, :] = scores[rows, :] - column

    def wait_s_sends(d, carry):
        seq_copy(d, me, me).wait_send()
        return carry

    lax.fori_loop(1, SEQ, wait_s_sends, 0)


def whole_kernel(
    x_ref, b_ref, c_ref, la_ref, skip_ref, choice_ref, share_ref,
    rescale_ref, switch_hbm, widen_hbm, contract_hbm,
    pick_ref, closing_ref, lexicon_hbm, div_ref,
    layer_ref, prob_ref,
    mamba, gmap, expert, switch, widen, contract, lexicon, rows, load_sem,
    *scratch,
):
    barrier = pltpu.get_barrier_semaphore()
    me = lax.axis_index("seq")
    ch = lax.axis_index("chan")
    greet("seq", SEQ, me)
    greet("chan", CHAN, ch)
    xh, z = me // NZ, me % NZ
    y, xl = ch // 2, ch % 2
    diagonal = {"seq": (1 - xh) * NZ + z, "chan": y * 2 + 1 - xl}
    pl.semaphore_signal(barrier, inc=1, device_id=diagonal, device_id_type=MESH)
    loads = [
        pltpu.make_async_copy(src, dst, load_sem.at[k])
        for k, (src, dst) in enumerate(
            ((switch_hbm, switch), (widen_hbm, widen), (contract_hbm, contract), (lexicon_hbm, lexicon))
        )
    ]
    for load in loads:
        load.start()
    first, finish = scan_part(
        x_ref, b_ref, c_ref, la_ref, skip_ref, choice_ref, share_ref,
        mamba, rows, gmap, *scratch[:13],
    )
    def idle():
        first()
        for load in loads:
            load.wait()

    drain = expert_part(finish, idle, rescale_ref, switch, widen, contract, expert, rows, *scratch[13 : 13 + 33])
    head_part(
        drain, mamba, gmap, expert, pick_ref, closing_ref, lexicon, div_ref, layer_ref, prob_ref, *scratch[46:]
    )


def whole_call(*args):
    vm = pl.BlockSpec(memory_space=pltpu.VMEM)
    hbm = pl.BlockSpec(memory_space=pl.ANY)
    dma = pltpu.SemaphoreType.DMA
    in_specs = [vm] * 8 + [hbm] * 3 + [vm] * 2 + [hbm, pl.BlockSpec(memory_space=pltpu.SMEM)]
    return pl.pallas_call(
        whole_kernel,
        out_shape=(
            jax.ShapeDtypeStruct((TOK, CH), BF16),
            jax.ShapeDtypeStruct((TOK, TOK), F32),
        ),
        in_specs=in_specs,
        out_specs=(vm, vm),
        scratch_shapes=[
            pltpu.VMEM((TOK, CH), BF16),
            pltpu.VMEM((TOK, 128), BF16),
            pltpu.VMEM((CAP, CH), F32),
            pltpu.VMEM((CH, HIDL), BF16),
            pltpu.VMEM((CH, HIDL), BF16),
            pltpu.VMEM((HIDL, CH), BF16),
            pltpu.VMEM((WIDTH, TOK), BF16),
            pltpu.VMEM((SEQ, CAP, CH), BF16),
            dma((4,)),
            pltpu.VMEM((128, TOK), F32),
            pltpu.VMEM((128, CH), BF16),
            pltpu.VMEM((SEQ, 16, 512), BF16),
            pltpu.VMEM((SEQ, 8, 128), F32),
            pltpu.VMEM((SEQ, 16, 512), BF16),
            pltpu.VMEM((128, CH), BF16),
            pltpu.VMEM((TOK, CH), F32),
            *[dma((SEQ,))] * 6,
            pltpu.VMEM((NZ, 2, 64, HIDL + 128), BF16),
            pltpu.VMEM((NZ, 2, 64, HIDL), BF16),
            pltpu.VMEM((NZ, 64, HIDL + 128), BF16),
            pltpu.VMEM((NZ, 4, 2, 16, HIDL), BF16),
            pltpu.VMEM((NZ, 2, 16, HIDL), BF16),
            pltpu.VMEM((NZ, 4, 16, HIDL + 128), BF16),
            pltpu.VMEM((NZ, 16, HIDL), BF16),
            pltpu.VMEM((NZ, 2, 64, HIDL), BF16),
            pltpu.VMEM((NZ, CAP, CH), BF16),
            pltpu.VMEM((NZ, CAP, CH), BF16),
            pltpu.VMEM((NZ, CAP, CH), F32),
            pltpu.VMEM((NZ, CAP, CH), BF16),
            pltpu.VMEM((NZ, CAP, CH), BF16),
            dma((2, 5, 2)), dma((2, 5, 2)), dma, dma,
            dma((NZ,)), dma((NZ,)), dma((NZ, 4)), dma((NZ, 4)),
            dma((NZ, 4)), dma((NZ, 4)), dma((NZ,)), dma((NZ,)),
            dma((NZ,)), dma((NZ,)), dma((NZ, 2, 4)), dma((NZ, 2, 4)),
            dma((NZ,)), dma((NZ,)), dma((NZ,)), dma((NZ,)),
            pltpu.VMEM((2, 4, 4, 128, 512), BF16),
            pltpu.VMEM((2, 128, TOK), F32),
            pltpu.VMEM((2, 128, TOK), F32),
            pltpu.VMEM((2, 128, 1), F32),
            pltpu.VMEM((CHAN, 8, 128), F32),
            pltpu.VMEM((SEQ, 8, 128), F32),
            dma((NZ,)), dma((NZ,)),
            dma((2, 5, 2, 4)), dma((2, 5, 2, 4)),
            dma((CHAN,)), dma((CHAN,)),
            dma((SEQ,)), dma((SEQ,)),
        ],
        compiler_params=pltpu.CompilerParams(
            collective_id=0, has_side_effects=True, vmem_limit_bytes=VMEM_LIMIT
        ),
        name="whole",
    )(*args)


def shards(
    recurrence_feed,
    memory_write_matrix,
    memory_read_matrix,
    log_shrink_table,
    skip_connection_scale,
    specialist_choices,
    specialist_mixing_shares,
    specialist_rescale_vector,
    specialist_switch_matrix,
    specialist_widen_matrix,
    specialist_contract_matrix,
    closing_rescale_vector,
    lexicon_matrix,
    softness_divisor,
    picked_entry_offsets,
):
    return whole_call(
        recurrence_feed,
        memory_write_matrix,
        memory_read_matrix,
        log_shrink_table.T,
        skip_connection_scale.reshape(1, -1),
        specialist_choices.T,
        specialist_mixing_shares.T,
        specialist_rescale_vector.reshape(1, -1),
        specialist_switch_matrix,
        specialist_widen_matrix,
        specialist_contract_matrix,
        picked_entry_offsets.reshape(1, -1),
        closing_rescale_vector.reshape(1, -1),
        lexicon_matrix,
        softness_divisor.reshape(1, 1),
    )


def solution(mesh):
    in_specs = (
        P(("dp", "seq"), "chan"),
        P(("dp", "seq"), None),
        P(("dp", "seq"), None),
        P(("dp", "seq"), "chan"),
        P("chan"),
        P(("dp", "seq"), None),
        P(("dp", "seq"), None),
        P("chan"),
        P("chan", "seq"),
        P("chan", "seq"),
        P("seq", "chan"),
        P(),
        P(None, ("seq", "chan")),
        P(),
        P(("dp", "seq")),
    )
    out_specs = (P(("dp", "seq"), "chan"), P("dp", ("seq", "chan")))
    return jax.shard_map(shards, mesh=mesh, in_specs=in_specs, out_specs=out_specs, check_vma=False)
```
